32 devices in a mesh: grp: 4 (over z), own: 8 (over y, x, core).
Axes of the slice: x: 2, y: 2, z: 4, core: 2. Of those that a mesh axis runs over, the one named last changes fastest.
Arguments:
- tokens: bfloat16 [16384, 768], P(('grp', 'own')), may hold values from -6 to 6
- doc_ids: int32 [16384], P(('grp', 'own')), may hold values from 0 to 4, as said below
- cotangent: bfloat16 [16384, 768], P(('grp', 'own')), may hold values from -6 to 6
- norm1_gain: bfloat16 [768], P('own'), may hold values from 0.5 to 1.5
- norm1_shift: bfloat16 [768], P('own'), may hold values from -1.75 to 1.75
- qkv_weight: bfloat16 [768, 2304], P('own'), may hold values from -0.21875 to 0.21875
- query_bias: bfloat16 [768], P('own'), may hold values from -3 to 3
- value_bias: bfloat16 [768], P('own'), may hold values from -3 to 3
- out_weight: bfloat16 [768, 768], P('own'), may hold values from -0.625 to 0.625
- out_bias: bfloat16 [768], P('own'), may hold values from -1.75 to 1.75
- norm2_gain: bfloat16 [768], P('own'), may hold values from 0.5 to 1.5
- norm2_shift: bfloat16 [768], P('own'), may hold values from -1.75 to 1.75
- fc_weight: bfloat16 [768, 3072], P('own'), may hold values from -0.21875 to 0.21875
- fc_bias: bfloat16 [3072], P('own'), may hold values from -3 to 3
- proj_weight: bfloat16 [3072, 768], P('own'), may hold values from -0.109375 to 0.109375
- proj_bias: bfloat16 [768], P('own'), may hold values from -1.75 to 1.75
Outputs:
- activations: bfloat16 [16384, 768], P(('grp', 'own'))
- tokens_grad: float32 [16384, 768], P(('grp', 'own'))
- norm1_gain_grad: float32 [768], P('own')
- norm1_shift_grad: float32 [768], P('own')
- qkv_weight_grad: float32 [768, 2304], P('own')
- query_bias_grad: float32 [768], P('own')
- value_bias_grad: float32 [768], P('own')
- out_weight_grad: float32 [768, 768], P('own')
- out_bias_grad: float32 [768], P('own')
- norm2_gain_grad: float32 [768], P('own')
- norm2_shift_grad: float32 [768], P('own')
- fc_weight_grad: float32 [768, 3072], P('own')
- fc_bias_grad: float32 [3072], P('own')
- proj_weight_grad: float32 [3072, 768], P('own')
- proj_bias_grad: float32 [768], P('own')
The draws below stay inside these ranges and needn't reach their ends.
Inputs may be any that keep to these rules, and one draw needn't show every extreme that they name: `doc_ids`: each row of 512 tokens numbers its documents 1, 2, ... in order from its first token, then may end with padding numbered 0.
All inputs are finite; a program needn't handle non-finite values.
Results may differ from the reference program's by a relative error of at most 0.017.
Values may be sent and summed in bfloat16 or wider, within the bound.
A program may use at most 192 MiB of HBM per device.

```python
import jax
import jax.numpy as jnp
from jax import lax

D = 768
FF = 3072
HEADS = 12
HEAD_DIM = 64
TOK_DEV = 512
USES = 2
TOKENS = 16384


def draw_doc_ids(key, part):
    key = jax.random.fold_in(key, 7)
    start_key, pad_key, row_key = jax.random.split(key, 3)
    rows = TOKENS // TOK_DEV
    column = lax.broadcasted_iota(jnp.int32, (rows, TOK_DEV), 1)
    row_index = lax.broadcasted_iota(jnp.int32, (rows, TOK_DEV), 0)
    chosen = jax.random.randint(row_key, (), 0, rows)
    eighth = TOK_DEV // 8
    starts = jax.random.randint(start_key, (rows, TOK_DEV), 0, TOK_DEV // 4) == 0
    forced = (row_index == chosen) & ((column == eighth) | (column == 2 * eighth) | (column == 3 * eighth))
    starts = starts | (column == 0) | forced
    numbers = jnp.minimum(jnp.cumsum(starts.astype(jnp.int32), axis=1), 4)
    padding = jax.random.randint(pad_key, (rows, 1), 0, eighth + 1)
    row_column = lax.broadcasted_iota(jnp.int32, (rows, 1), 0)
    padding = jnp.where(row_column == chosen, jnp.maximum(padding, 1), padding)
    numbers = jnp.where(column >= TOK_DEV - padding, 0, numbers)
    return numbers.reshape(TOKENS).astype(jnp.int32)


def levels(rng, extent, cuts, smallest, high):
    level, own = 1.0, jax.random.fold_in(rng, 6)
    for axis_at, shards_of in cuts:
        steps = jnp.exp(jax.random.uniform(jax.random.fold_in(own, axis_at), (shards_of,), jnp.float32, smallest / len(cuts), high / len(cuts)))
        level = level * jnp.repeat(steps, extent[axis_at] // shards_of).reshape([-1 if axis == axis_at else 1 for axis in range(len(extent))])
    return level


def gaussian(own_key, shape, deviation, bound, shards=(), held_as=jnp.bfloat16):
    array = deviation * jax.random.normal(own_key, shape, jnp.float32)
    if shards:
        array = array * levels(own_key, shape, shards, -0.22, 0.18)
    return jnp.clip(array, -bound, bound).astype(held_as)


def setup_inputs(seed: int = 0) -> dict:
    key_list = jax.random.split(jax.random.key(seed), 17)
    tokens = gaussian(key_list[0], (TOKENS, D), 1.0, 6.0, ((0, 32),))
    doc_ids = draw_doc_ids(jax.random.fold_in(key_list[16], 71), 0)
    cotangent = gaussian(key_list[2], (TOKENS, D), 1.0, 6.0, ((0, 32),))
    norm1_gain = jnp.clip(1.0 + 0.1 * jax.random.normal(key_list[3], (D,), jnp.float32), 0.5, 1.5).astype(jnp.bfloat16)
    norm1_shift = gaussian(key_list[4], (D,), 0.3, 1.75, ((0, 8),))
    qkv_weight = gaussian(key_list[5], (D, 3 * D), D ** -0.5, 0.21875, ((0, 8),))
    query_bias = gaussian(key_list[6], (D,), 0.5, 3.0, ((0, 8),))
    value_bias = gaussian(key_list[7], (D,), 0.5, 3.0, ((0, 8),))
    out_weight = gaussian(key_list[8], (D, D), (D // 8) ** -0.5, 0.625, ((0, 8),))
    out_bias = gaussian(key_list[9], (D,), 0.3, 1.75, ((0, 8),))
    norm2_gain = jnp.clip(1.0 + 0.1 * jax.random.normal(key_list[10], (D,), jnp.float32), 0.5, 1.5).astype(jnp.bfloat16)
    norm2_shift = gaussian(key_list[11], (D,), 0.3, 1.75, ((0, 8),))
    fc_weight = gaussian(key_list[12], (D, FF), D ** -0.5, 0.21875, ((0, 8),))
    fc_bias = gaussian(key_list[13], (FF,), 0.5, 3.0, ((0, 8),))
    proj_weight = gaussian(key_list[14], (FF, D), FF ** -0.5, 0.109375, ((0, 8),))
    proj_bias = gaussian(key_list[15], (D,), 0.3, 1.75, ((0, 8),))
    return dict(tokens=tokens, doc_ids=doc_ids, cotangent=cotangent, norm1_gain=norm1_gain, norm1_shift=norm1_shift, qkv_weight=qkv_weight, query_bias=query_bias, value_bias=value_bias, out_weight=out_weight, out_bias=out_bias, norm2_gain=norm2_gain, norm2_shift=norm2_shift, fc_weight=fc_weight, fc_bias=fc_bias, proj_weight=proj_weight, proj_bias=proj_bias)


@jax.custom_vjp
def low(v):
    return lax.optimization_barrier(v.astype(jnp.bfloat16)).astype(jnp.float32)

@jax.custom_vjp
def low_back(v):
    return v

def low_keep(v):
    return (low(v), None)

def low_pass(kept, grad):
    return (grad,)

def back_keep(v):
    return (v, None)

def back_low(kept, grad):
    return (low(grad),)
low.defvjp(low_keep, low_pass)
low_back.defvjp(back_keep, back_low)
EPSILON = 1e-05

def normalize(x, gain, shift):
    centre = x - lax.optimization_barrier(jnp.mean(x, axis=-1, keepdims=True))
    spread = lax.optimization_barrier(jnp.mean(centre * centre, axis=-1, keepdims=True))
    return centre * lax.rsqrt(spread + EPSILON) * gain + shift

def smooth(inner):
    return jax.nn.gelu(inner, approximate=True)

def visible(doc):
    count = doc.shape[0]
    row = lax.broadcasted_iota(jnp.int32, (count, count), 0)
    col = lax.broadcasted_iota(jnp.int32, (count, count), 1)
    same = doc[:, None] == doc[None, :]
    return same & (col <= row) & ((doc[None, :] != 0) | (row == col))

def attend(parts):
    query, key, value, doc = parts
    count = query.shape[0]
    q_heads = query.reshape(count, HEADS, HEAD_DIM)
    k_heads = key.reshape(count, HEADS, HEAD_DIM)
    v_heads = value.reshape(count, HEADS, HEAD_DIM)
    scores = low_back(jnp.einsum('thd,shd->hts', q_heads, k_heads, precision=lax.Precision.HIGHEST) * HEAD_DIM ** (-0.5))
    scores = jnp.where(visible(doc)[None], scores, -1e+30)
    probs = low(jax.nn.softmax(scores, axis=-1))
    mixed = jnp.einsum('hts,shd->thd', probs, v_heads, precision=lax.Precision.HIGHEST)
    return low(low_back(mixed.reshape(count, HEADS * HEAD_DIM)))

def layer(x, weights, doc_ids):
    gain_one, shift_one, w_qkv, bias_query, bias_value, w_out, bias_out, gain_two, shift_two, w_fc, bias_fc, w_proj, bias_proj = weights
    high = lax.Precision.HIGHEST
    rows = TOKENS // TOK_DEV
    h_one = low(normalize(x, gain_one, shift_one))
    qkv_bias = jnp.concatenate([bias_query, jnp.zeros((D,), bias_query.dtype), bias_value])
    packed = low(low_back(jnp.dot(h_one, w_qkv, precision=high) + qkv_bias))
    query = packed[:, :D].reshape(rows, TOK_DEV, D)
    key = packed[:, D:2 * D].reshape(rows, TOK_DEV, D)
    value = packed[:, 2 * D:].reshape(rows, TOK_DEV, D)
    mixed = lax.map(jax.checkpoint(attend), (query, key, value, doc_ids.reshape(rows, TOK_DEV)))
    mixed = mixed.reshape(TOKENS, D)
    middle = x + low_back(jnp.dot(mixed, w_out, precision=high) + bias_out)
    h_two = low(normalize(middle, gain_two, shift_two))
    inner = low_back(jnp.dot(h_two, w_fc, precision=high) + bias_fc)
    active = low(smooth(inner))
    return middle + low_back(jnp.dot(active, w_proj, precision=high) + bias_proj)

def reference(tokens, doc_ids, cotangent, norm1_gain, norm1_shift, qkv_weight, query_bias, value_bias, out_weight, out_bias, norm2_gain, norm2_shift, fc_weight, fc_bias, proj_weight, proj_bias):
    params = (norm1_gain, norm1_shift, qkv_weight, query_bias, value_bias, out_weight, out_bias, norm2_gain, norm2_shift, fc_weight, fc_bias, proj_weight, proj_bias)
    floats = tuple((item.astype(jnp.float32) for item in params))

    def forward(x, *weights):
        for use in range(USES):
            x = layer(x, weights, doc_ids)
        return x
    result, pull = jax.vjp(forward, tokens.astype(jnp.float32), *floats)
    grads = pull(cotangent.astype(jnp.float32))
    return (result.astype(jnp.bfloat16), grads[0], grads[1], grads[2], grads[3], grads[4], grads[5], grads[6], grads[7], grads[8], grads[9], grads[10], grads[11], grads[12], grads[13])
```

```python
import functools

import jax
import jax.numpy as jnp
from jax import lax
from jax.experimental import pallas as pl
from jax.experimental.pallas import tpu as pltpu
from jax.sharding import PartitionSpec as P

HEADS = 12
HEAD_DIM = 64
USES = 2
EPSILON = 1e-05
SCALE = HEAD_DIM ** (-0.5)
TANH_SCALE = 0.7978845608028654
TANH_CUBIC = 0.044715
MESH = pl.DeviceIdType.MESH
f32 = jnp.float32
bf16 = jnp.bfloat16

GAIN1, SHIFT1, BIAS_Q, BIAS_V, BIAS_OUT, GAIN2, SHIFT2, BIAS_PROJ, BIAS_FC = range(9)


def dot(a, b, ca=1, cb=0):
    return lax.dot_general(a, b, (((ca,), (cb,)), ((), ())), preferred_element_type=f32)


def loop(count, body):
    def step(i, carry):
        body(i)
        return carry

    lax.fori_loop(0, count, step, 0)


def span(begin, end, body):
    def step(i, carry):
        body(i)
        return carry

    lax.fori_loop(begin, end, step, 0)


def part(i, size):
    return pl.ds(pl.multiple_of(i * size, size), size)


def centred(x):
    centre = x - jnp.mean(x, axis=-1, keepdims=True)
    spread = jnp.mean(centre * centre, axis=-1, keepdims=True)
    return centre, lax.rsqrt(spread + EPSILON)


def norm_forward(x, gain, shift, h):
    rows = 128

    def step(i):
        centre, r = centred(x[part(i, rows), :].astype(f32))
        h[part(i, rows), :] = (centre * r * gain + shift).astype(bf16)

    loop(x.shape[0] // rows, step)


def norm_backward(x, dh, gain, grad, out, sums, gain_row, shift_row, low=None):
    rows = 128
    sums[gain_row : gain_row + 1, :] = jnp.zeros_like(gain)
    sums[shift_row : shift_row + 1, :] = jnp.zeros_like(gain)

    def step(i):
        centre, r = centred(x[part(i, rows), :].astype(f32))
        n = centre * r
        d = dh[part(i, rows), :]
        sums[gain_row : gain_row + 1, :] += jnp.sum(d * n, axis=0, keepdims=True)
        sums[shift_row : shift_row + 1, :] += jnp.sum(d, axis=0, keepdims=True)
        e = d * gain
        inner = e - jnp.mean(e, axis=-1, keepdims=True) - n * jnp.mean(e * n, axis=-1, keepdims=True)
        result = grad[part(i, rows), :].astype(f32) + r * inner
        out[part(i, rows), :] = result
        if low is not None:
            low[part(i, rows), :] = result.astype(bf16)

    loop(x.shape[0] // rows, step)


def column_sum(x):
    return jnp.sum(x.astype(f32), axis=0, keepdims=True)


def make_mask(doc, mask):
    count = doc.shape[1]
    half = count // 2
    ids = doc[0:1, :].astype(f32)
    keys = jnp.broadcast_to(ids, (128, count)).T[:, :1]
    for k0, q0, place in ((0, 0, 0), (half, half, count)):
        width = count - q0
        row = lax.broadcasted_iota(jnp.int32, (half, width), 0) + k0
        col = lax.broadcasted_iota(jnp.int32, (half, width), 1) + q0
        key = keys[k0 : k0 + half]
        same = (key == ids[:, q0:]) & (row <= col) & ((key != 0.0) | (row == col))
        mask[:, place : place + width] = jnp.where(same, 0.0, -1e30)


def head_lanes(h, x):
    lane = lax.broadcasted_iota(jnp.int32, (1, 2 * HEAD_DIM), 1)
    keep = (lane < HEAD_DIM) if h == 0 else (lane >= HEAD_DIM)
    return jnp.where(keep, x, jnp.zeros_like(x))


def attention_forward(qkv, mask, probs, o, begin=0, end=6):
    count, width = o.shape
    half = count // 2
    pair = 2 * HEAD_DIM

    def step(i):
        col = part(i, pair)
        q = qkv[:, col]
        k = qkv[:, pl.ds(pl.multiple_of(width + i * pair, pair), pair)]
        v = qkv[:, pl.ds(pl.multiple_of(2 * width + i * pair, pair), pair)]
        vt = v.T
        outs = []
        for h in range(2):
            kh = head_lanes(h, k)
            s0 = dot(kh[:half], q, 1, 1) + mask[:, :count]
            s1 = dot(kh[half:], q[half:], 1, 1) + mask[:, count:]
            m0 = jnp.max(s0, axis=0, keepdims=True)
            m1 = jnp.max(s1, axis=0, keepdims=True)
            top = jnp.concatenate([m0[:, :half], jnp.maximum(m0[:, half:], m1)], axis=1)
            e0 = jnp.exp(s0 - top)
            e1 = jnp.exp(s1 - top[:, half:])
            l0 = jnp.sum(e0, axis=0, keepdims=True)
            l1 = jnp.sum(e1, axis=0, keepdims=True)
            r = 1.0 / jnp.concatenate([l0[:, :half], l0[:, half:] + l1], axis=1)
            p0 = (e0 * r).astype(bf16)
            p1 = (e1 * r[:, half:]).astype(bf16)
            probs[2 * i + h, :, :count] = p0
            probs[2 * i + h, :, count:] = p1
            vh = vt[h * HEAD_DIM : (h + 1) * HEAD_DIM]
            first = dot(vh[:, :half], p0)
            second = dot(vh[:, half:], p1)
            outs.append(jnp.concatenate([first[:, :half], first[:, half:] + second], axis=1))
        o[:, col] = jnp.concatenate(outs, axis=0).astype(bf16).T

    span(begin, end, step)


def attention_backward(qkv, probs, do, dz, sums):
    count, width = do.shape
    half = count // 2
    pair = 2 * HEAD_DIM

    def step(i):
        cq = part(i, pair)
        ck = pl.ds(pl.multiple_of(width + i * pair, pair), pair)
        cv = pl.ds(pl.multiple_of(2 * width + i * pair, pair), pair)
        q, k, v, d = qkv[:, cq], qkv[:, ck], qkv[:, cv], do[:, cq]
        dq = dk = dv = None
        for h in range(2):
            dh, kh, qh = head_lanes(h, d), head_lanes(h, k), head_lanes(h, q)
            p0 = probs[2 * i + h, :, :count]
            p1 = probs[2 * i + h, :, count:]
            d0 = dot(v[:half], dh, 1, 1)
            d1 = dot(v[half:], dh[half:], 1, 1)
            w0 = p0.astype(f32)
            w1 = p1.astype(f32)
            t0 = jnp.sum(d0 * w0, axis=0, keepdims=True)
            t1 = jnp.sum(d1 * w1, axis=0, keepdims=True)
            t = jnp.concatenate([t0[:, :half], t0[:, half:] + t1], axis=1)
            s0 = (w0 * (d0 - t)).astype(bf16)
            s1 = (w1 * (d1 - t[:, half:])).astype(bf16)
            v_term = jnp.concatenate([dot(p0, dh), dot(p1, dh[half:])], axis=0)
            k_term = jnp.concatenate([dot(s0, qh), dot(s1, qh[half:])], axis=0)
            qa = dot(s0, kh[:half], 0, 0)
            qb = dot(s1, kh[half:], 0, 0)
            q_term = jnp.concatenate([qa[:half], qa[half:] + qb], axis=0)
            dq = q_term if dq is None else dq + q_term
            dk = k_term if dk is None else dk + k_term
            dv = v_term if dv is None else dv + v_term
        dq = (dq * SCALE).astype(bf16)
        dv = dv.astype(bf16)
        dz[:, cq] = dq
        dz[:, ck] = dk.astype(bf16)
        dz[:, cv] = dv
        sums[BIAS_Q : BIAS_Q + 1, cq] = column_sum(dq)
        sums[BIAS_V : BIAS_V + 1, cq] = column_sum(dv)

    loop(width // pair, step)


def small(block, row):
    return block[row : row + 1, :]


def hidden_forward(h2, wfc, block, f, slope, begin, end):
    width = h2.shape[1]

    def hidden(i):
        col = part(i, width)
        u = dot(h2[...], wfc[:, col]) + block[pl.ds(BIAS_FC + i, 1), :]
        square = u * u
        t = jnp.tanh(u * (TANH_SCALE + (TANH_SCALE * TANH_CUBIC) * square))
        rise = 0.5 + 0.5 * t
        f[:, col] = (u * rise).astype(bf16)
        inner = TANH_SCALE + (3.0 * TANH_SCALE * TANH_CUBIC) * square
        slope[:, col] = (rise + (0.5 * u) * (1.0 - t * t) * inner).astype(bf16)

    span(begin, end, hidden)


def forward_layer(x, block, weights, mask, kept, result, ready):
    wqkv, wout, wfc, wproj = weights
    h1, qkv, probs, o, x1, h2, slope, f = kept
    width = x.shape[1]
    ready("small")
    norm_forward(x, small(block, GAIN1), small(block, SHIFT1), h1)
    ready("qkv")
    h = h1[...]
    qkv[:, :width] = (dot(h, wqkv[:, :width]) + small(block, BIAS_Q)).astype(bf16) * SCALE
    qkv[:, width : 2 * width] = dot(h, wqkv[:, width : 2 * width]).astype(bf16)
    qkv[:, 2 * width :] = (dot(h, wqkv[:, 2 * width :]) + small(block, BIAS_V)).astype(bf16)
    attention_forward(qkv, mask, probs, o)
    ready("out")
    x1[...] = x[...].astype(f32) + (dot(o[...], wout[...]) + small(block, BIAS_OUT))
    norm_forward(x1, small(block, GAIN2), small(block, SHIFT2), h2)
    ready("fc")

    hidden_forward(h2, wfc, block, f, slope, 0, wfc.shape[1] // width)
    ready("proj")
    result[...] = x1[...] + (dot(f[...], wproj[...]) + small(block, BIAS_PROJ))


def backward_hidden(gm, wproj, slope, du, sums):
    width = gm.shape[1]

    def hidden(i):
        col = part(i, width)
        d = (dot(gm[...], wproj[col, :], 1, 1) * slope[:, col].astype(f32)).astype(bf16)
        du[:, col] = d
        sums[pl.ds(BIAS_FC + i, 1), :] = column_sum(d)

    loop(wproj.shape[0] // width, hidden)


def backward_layer(x, grad, gm, block, weights, kept, scratch, result, sums, done):
    wqkv, wout, wfc, wproj = weights
    qkv, probs, x1, slope = kept
    dh, do, da = scratch
    sums[BIAS_PROJ : BIAS_PROJ + 1, :] = column_sum(gm[...])
    backward_hidden(gm, wproj, slope, slope, sums)
    done("du")
    dh[...] = dot(slope[...], wfc[...], 1, 1)
    norm_backward(x1, dh, small(block, GAIN2), grad, result, sums, GAIN2, SHIFT2, da)
    done("da")
    sums[BIAS_OUT : BIAS_OUT + 1, :] = column_sum(da[...])
    do[...] = dot(da[...], wout[...], 1, 1).astype(bf16)
    attention_backward(qkv, probs, do, qkv, sums)
    done("dz")
    dh[...] = dot(qkv[...], wqkv[...], 1, 1)
    norm_backward(x, dh, small(block, GAIN1), result, result, sums, GAIN1, SHIFT1)


def coords():
    own = lax.axis_index("own")
    return lax.axis_index("grp"), own // 2, lax.rem(own, 2)


class Unit:
    def __init__(self, shard, full, row, rows, col, cols):
        self.shard, self.full = shard, full
        self.row, self.rows, self.col, self.cols = row, rows, col, cols

    def mine(self, half=None):
        rows = self.rows if half is None else self.rows // 2
        start = self.row + (0 if half is None else half * rows)
        return self.shard.at[pl.ds(start, rows), pl.ds(self.col, self.cols)]

    def block(self, owner, half=None):
        rows = self.rows if half is None else self.rows // 2
        start = owner * self.shard.shape[0] + self.row + (0 if half is None else half * rows)
        return self.full.at[pl.ds(pl.multiple_of(start, 16), rows), pl.ds(self.col, self.cols)]


PIECES = [(1, 0), (1, 1), (2, 0), (2, 1), (3, 0), (3, 1)]


class Gather:
    def __init__(self, units, link_send, link_recv, core_send, core_recv, own_sem):
        self.units = units
        self.link_send, self.link_recv = link_send, link_recv
        self.core_send, self.core_recv, self.own_sem = core_send, core_recv, own_sem
        self.grp, self.chip, self.core = coords()
        self.odd = lax.rem(self.grp, 2)
        self.sent = []

    def owner(self, offset):
        return jnp.bitwise_xor(self.chip, offset) * 2 + self.core

    def device(self, chip_offset, along_z=False):
        own = jnp.bitwise_xor(self.chip, chip_offset) * 2 + self.core
        grp = self.grp + 1 - 2 * self.odd if along_z else self.grp
        return (grp, own)

    def link(self, k, src, dst, piece, out, device):
        return pltpu.make_async_remote_copy(
            src_ref=src,
            dst_ref=dst,
            send_sem=self.link_send.at[k, out],
            recv_sem=self.link_recv.at[k, piece],
            device_id=device,
            device_id_type=MESH,
        )

    def across(self, k, src, dst, slot):
        return pltpu.make_async_remote_copy(
            src_ref=src,
            dst_ref=dst,
            send_sem=self.core_send.at[k, slot],
            recv_sem=self.core_recv.at[k, slot],
            device_id=(self.grp, self.chip * 2 + 1 - self.core),
            device_id_type=MESH,
        )

    def own(self, k):
        unit = self.units[k]
        return pltpu.make_async_copy(unit.mine(), unit.block(self.owner(0)), self.own_sem.at[k])

    def first(self, k, offset, half, out):
        unit = self.units[k]
        piece = PIECES.index((offset, half))
        return self.link(
            k, unit.mine(half), unit.block(self.owner(0), half), piece, out, self.device(offset)
        )

    def relay(self, k, offset, half, way, out):
        unit = self.units[k]
        piece = unit.block(self.owner(offset), half)
        return self.link(k, piece, piece, PIECES.index((3, half)), out, self.device(way))

    def pair(self, k, offset, half, out):
        unit = self.units[k]
        piece = unit.block(self.owner(offset), half)
        return self.link(k, piece, piece, PIECES.index((offset, half)), out, self.device(0, True))

    def hand(self, k, offset, half):
        unit = self.units[k]
        piece = unit.block(self.owner(offset), half)
        return self.across(k, piece, piece, PIECES.index((offset, half)))

    def arrived(self, k, offset, half):
        unit = self.units[k]
        piece = unit.block(self.owner(offset), half)
        self.link(k, piece, piece, PIECES.index((offset, half)), 0, self.device(1)).wait_recv()

    def plan(self, k):
        even = [
            self.first(k, 1, 0, 0),
            self.first(k, 2, 1, 1),
            self.first(k, 1, 1, 2),
            self.first(k, 2, 0, 3),
            self.pair(k, 1, 0, 4),
            self.pair(k, 2, 1, 5),
        ]
        odd = [
            self.first(k, 1, 1, 0),
            self.first(k, 2, 0, 1),
            self.relay(k, 2, 0, 1, 2),
            self.relay(k, 1, 1, 2, 3),
            self.pair(k, 3, 0, 4),
            self.pair(k, 3, 1, 5),
        ]
        return even, odd

    def start(self, k):
        even, odd = self.plan(k)

        @pl.when(self.odd == 0)
        def _():
            for copy in even[:4]:
                copy.start()

        @pl.when(self.odd == 1)
        def _():
            for copy in odd[:2]:
                copy.start()

        unit = self.units[k]
        self.across(k, unit.mine(), unit.block(self.owner(0)), len(PIECES)).start()
        self.own(k).start()

    def serve_first(self, k):
        even, odd = self.plan(k)

        @pl.when(self.odd == 0)
        def _():
            for at, (offset, half) in enumerate(((1, 0), (2, 1), (1, 1), (2, 0))):
                self.arrived(k, offset, half)
                if at < 2:
                    even[4 + at].start()
                self.hand(k, offset, half).start()

        @pl.when(self.odd == 1)
        def _():
            for at, (offset, half) in enumerate(((2, 0), (1, 1))):
                self.arrived(k, offset, half)
                odd[2 + at].start()
                self.hand(k, offset, half).start()

    def serve_second(self, k):
        even, odd = self.plan(k)

        @pl.when(self.odd == 0)
        def _():
            for half in range(2):
                self.arrived(k, 3, half)
                self.hand(k, 3, half).start()

        @pl.when(self.odd == 1)
        def _():
            for half in range(2):
                self.arrived(k, 3, half)
                odd[4 + half].start()
                self.hand(k, 3, half).start()
            for offset, half in ((1, 0), (2, 1)):
                self.arrived(k, offset, half)
                self.hand(k, offset, half).start()

    def finish(self, k):
        unit = self.units[k]
        other = 1 - 2 * self.core
        self.own(k).wait()
        whole = unit.block(self.owner(0) + other)
        self.across(k, whole, whole, len(PIECES)).wait_recv()
        for slot, (offset, half) in enumerate(PIECES):
            piece = unit.block(self.owner(offset) + other, half)
            self.across(k, piece, piece, slot).wait_recv()

    def drain(self, k):
        even, odd = self.plan(k)

        @pl.when(self.odd == 0)
        def _():
            for copy in even:
                copy.wait_send()

        @pl.when(self.odd == 1)
        def _():
            for copy in odd:
                copy.wait_send()

        unit = self.units[k]
        self.across(k, unit.mine(), unit.block(self.owner(0)), len(PIECES)).wait_send()
        for offset, half in PIECES:
            self.hand(k, offset, half).wait_send()


def store(copies, sem, src, dst):
    copy = pltpu.make_async_copy(src, dst, sem.at[len(copies)])
    copy.start()
    copies.append(copy)


def first_kernel(
    tokens, doc, packed, sqkv, sout, sfc, sproj,
    x2_out, block_out, mask_out, wqkv_out, wout_out, wfc_out, wproj_out,
    h1_out, qkv_out, probs_out, o_out, x1_out, h2_out, slope_out, f_out,
    wqkv, wout, wfc, wproj, block, mask, h1, qkv, probs, o, x1, h2, slope, f, x2, many,
    link_send, link_recv, core_send, core_recv, own_sem, small_send, small_recv, out_sem,
):
    grp, chip, core = coords()
    me = chip * 2 + core
    width = tokens.shape[1]
    barrier = pltpu.get_barrier_semaphore()
    peers = [(grp, jnp.bitwise_xor(me, j)) for j in range(1, 8)]
    peers.append((grp + 1 - 2 * lax.rem(grp, 2), me))
    for peer in peers:
        pl.semaphore_signal(barrier, inc=1, device_id=peer, device_id_type=MESH)
    pl.semaphore_wait(barrier, len(peers))

    units = [Unit(sqkv, wqkv, 0, sqkv.shape[0], i * width, width) for i in range(3)]
    units += [Unit(sout, wout, 0, sout.shape[0], 0, width)]
    units += [Unit(sfc, wfc, 0, sfc.shape[0], i * width, width) for i in range(sfc.shape[1] // width)]
    thirds = sproj.shape[0] // 3
    units += [Unit(sproj, wproj, i * thirds, thirds, 0, width) for i in range(3)]
    gather = Gather(units, link_send, link_recv, core_send, core_recv, own_sem)
    count = len(units)

    def small_copy(j, slot):
        return pltpu.make_async_remote_copy(
            src_ref=packed,
            dst_ref=many.at[slot],
            send_sem=small_send.at[j - 1],
            recv_sem=small_recv.at[j - 1],
            device_id=(grp, jnp.bitwise_xor(me, j)),
            device_id_type=MESH,
        )

    for j in range(1, 8):
        small_copy(j, j).start()
    gather.start(0)
    gather.start(1)
    copies = []

    def slot(s):
        if s < count:
            gather.serve_first(s)
        if s + 2 < count:
            gather.start(s + 2)
        if 0 <= s - 1 < count:
            gather.serve_second(s - 1)
        if 0 <= s - 2 < count:
            gather.finish(s - 2)

    make_mask(doc, mask)
    store(copies, out_sem, mask, mask_out)
    total = packed[...].astype(f32)
    for j in range(1, 8):
        small_copy(j, j).wait_recv()
        total = total + many[j].astype(f32)
    block[...] = total
    store(copies, out_sem, block, block_out)
    norm_forward(tokens, small(block, GAIN1), small(block, SHIFT1), h1)
    store(copies, out_sem, h1, h1_out)
    for s in range(3):
        slot(s)
    h = h1[...]
    qkv[:, :width] = (dot(h, wqkv[:, :width]) + small(block, BIAS_Q)).astype(bf16) * SCALE
    slot(3)
    qkv[:, width : 2 * width] = dot(h1[...], wqkv[:, width : 2 * width]).astype(bf16)
    slot(4)
    store(copies, out_sem, wqkv, wqkv_out)
    qkv[:, 2 * width :] = (dot(h1[...], wqkv[:, 2 * width :]) + small(block, BIAS_V)).astype(bf16)
    store(copies, out_sem, qkv, qkv_out)
    attention_forward(qkv, mask, probs, o, 0, 2)
    slot(5)
    store(copies, out_sem, wout, wout_out)
    attention_forward(qkv, mask, probs, o, 2, 4)
    slot(6)
    attention_forward(qkv, mask, probs, o, 4, 6)
    store(copies, out_sem, probs, probs_out)
    store(copies, out_sem, o, o_out)
    x1[...] = tokens[...].astype(f32) + (dot(o[...], wout[...]) + small(block, BIAS_OUT))
    norm_forward(x1, small(block, GAIN2), small(block, SHIFT2), h2)
    store(copies, out_sem, x1, x1_out)
    store(copies, out_sem, h2, h2_out)
    slot(7)
    hidden_forward(h2, wfc, block, f, slope, 0, 2)
    slot(8)
    hidden_forward(h2, wfc, block, f, slope, 2, 3)
    slot(9)
    store(copies, out_sem, wfc, wfc_out)
    hidden_forward(h2, wfc, block, f, slope, 3, 4)
    store(copies, out_sem, f, f_out)
    store(copies, out_sem, slope, slope_out)

    def project(i):
        rows = [pl.ds(owner * sproj.shape[0] + i * thirds, thirds) for owner in range(8)]
        left = jnp.concatenate([f[:, at] for at in rows], axis=1)
        right = jnp.concatenate([wproj[at, :] for at in rows], axis=0)
        return dot(left, right)

    slot(10)
    x2[...] = x1[...] + (project(0) + small(block, BIAS_PROJ))
    slot(11)
    x2[...] += project(1)
    slot(12)
    store(copies, out_sem, wproj, wproj_out)
    x2[...] += project(2)
    store(copies, out_sem, x2, x2_out)
    for k in range(count):
        gather.drain(k)
    for j in range(1, 8):
        small_copy(j, j).wait_send()
    for copy in copies:
        copy.wait()


def fetch(copies, src, dst, sem):
    copy = pltpu.make_async_copy(src, dst, sem)
    copy.start()
    copies.append(copy)
    return copy


def second_kernel(
    x_in, cot_in, block, mask_in, wqkv_in, wout_in, wfc_in, wproj_in,
    act_out, grad_out, sums, h1_out, dz_out, o_out, da_out, h2_out, du_out, f_out,
    x, cot, mask, wqkv, wout, wfc, wproj, h1, qkv, probs, o, x1, h2, slope, f, x2, dh, do, da, act, in_sem, out_sem,
):
    loads = []
    for src, dst in (
        (x_in, x), (mask_in, mask), (wqkv_in, wqkv), (wout_in, wout), (wfc_in, wfc), (wproj_in, wproj), (cot_in, cot)
    ):
        fetch(loads, src, dst, in_sem.at[len(loads)])
    x_here, mask_here, qkv_here, out_here, fc_here, proj_here, cot_here = loads
    waits = {"small": x_here, "qkv": qkv_here, "out": out_here, "fc": fc_here, "proj": proj_here}
    copies = []
    mask_here.wait()
    forward_layer(
        x, block, (wqkv, wout, wfc, wproj), mask, (h1, qkv, probs, o, x1, h2, slope, f), x2,
        lambda name: waits[name].wait(),
    )
    for src, dst in ((h1, h1_out), (o, o_out), (h2, h2_out), (f, f_out)):
        store(copies, out_sem, src, dst)
    act[...] = x2[...].astype(bf16)
    store(copies, out_sem, act, act_out)
    cot_here.wait()
    sums[...] = jnp.zeros_like(sums)
    backward_layer(
        x, cot, cot, block, (wqkv, wout, wfc, wproj), (qkv, probs, x1, slope), (dh, do, da), x2, sums,
        lambda name: store(copies, out_sem, *{"du": (slope, du_out), "da": (da, da_out), "dz": (qkv, dz_out)}[name]),
    )
    store(copies, out_sem, x2, grad_out)
    for copy in copies:
        copy.wait()


def third_kernel(
    x_in, grad_in, block, wqkv_in, wout_in, wfc_in, wproj_in, qkv_in, probs_in, x1_in, slope_in,
    grad_out, sums, gm_out, dz_out, da_out, du_out,
    x, grad, wqkv, wout, wfc, wproj, qkv, probs, x1, slope, dh, do, da, gm, in_sem, out_sem,
):
    loads = []
    for src, dst in (
        (grad_in, grad), (wproj_in, wproj), (slope_in, slope), (wfc_in, wfc), (x1_in, x1), (wout_in, wout),
        (qkv_in, qkv), (probs_in, probs), (wqkv_in, wqkv), (x_in, x),
    ):
        fetch(loads, src, dst, in_sem.at[len(loads)])
    copies = []
    for copy in loads:
        copy.wait()
    sums[...] = jnp.zeros_like(sums)
    gm[...] = grad[...].astype(bf16)
    store(copies, out_sem, gm, gm_out)
    backward_layer(
        x, grad, gm, block, (wqkv, wout, wfc, wproj), (qkv, probs, x1, slope), (dh, do, da), grad, sums,
        lambda name: store(copies, out_sem, *{"du": (slope, du_out), "da": (da, da_out), "dz": (qkv, dz_out)}[name]),
    )
    store(copies, out_sem, grad, grad_out)
    for copy in copies:
        copy.wait()


VMEM_BYTES = 62 * 2**20


def spec(shape, dtype):
    return jax.ShapeDtypeStruct(shape, dtype)


def kernels_body(*args):
    tokens, doc, cotangent = args[:3]
    gain1, shift1, sqkv, bq, bv, sout, bo, gain2, shift2, sfc, bfc, sproj, bp = args[3:]
    count, width = tokens.shape
    ff = sfc.shape[1]
    owners = lax.axis_size("own")
    me = lax.axis_index("own")
    rows = [gain1, shift1, bq, bv, bo, gain2, shift2, bp]
    stacked = jnp.tile(jnp.stack(rows), (1, owners))
    mine = lax.broadcasted_iota(jnp.int32, stacked.shape, 1) // gain1.shape[0] == me
    stacked = jnp.where(mine, stacked, jnp.zeros_like(stacked))
    tiled = jnp.tile(bfc, owners)
    mine = lax.broadcasted_iota(jnp.int32, tiled.shape, 0) // bfc.shape[0] == me
    tiled = jnp.where(mine, tiled, jnp.zeros_like(tiled)).reshape(ff // width, width)
    packed = jnp.concatenate([stacked, tiled, jnp.zeros((16 - 8 - ff // width, width), bf16)])

    hbm = pl.BlockSpec(memory_space=pl.ANY)
    vmem = pl.BlockSpec(memory_space=pltpu.VMEM)
    V = pltpu.VMEM
    half = count // 2
    x_s = ((count, width), f32)
    low_s = ((count, width), bf16)
    qkv_s = ((count, 3 * width), bf16)
    ff_s = ((count, ff), bf16)
    probs_s = ((HEADS, half, count + half), bf16)
    mask_s = ((half, count + half), f32)
    block_s = ((16, width), f32)
    w_s = [((width, 3 * width), bf16), ((width, width), bf16), ((width, ff), bf16), ((ff, width), bf16)]
    units = 3 + 1 + ff // width + 3
    dma = pltpu.SemaphoreType.DMA

    def call(kernel, inputs, outs, scratch, in_specs, out_specs, **params):
        return pl.pallas_call(
            kernel,
            out_shape=[spec(*s) for s in outs],
            in_specs=in_specs,
            out_specs=out_specs,
            scratch_shapes=scratch,
            compiler_params=pltpu.CompilerParams(vmem_limit_bytes=VMEM_BYTES, **params),
        )(*inputs)

    outs = [x_s, block_s, mask_s, *w_s, low_s, qkv_s, probs_s, low_s, x_s, low_s, ff_s, ff_s]
    (x2, block, mask, wqkv, wout, wfc, wproj, h1a, qkva, probsa, oa, x1a, h2a, slopea, fa) = call(
        first_kernel,
        (tokens, doc.reshape(1, count), packed, sqkv, sout, sfc, sproj),
        outs,
        [V(*s) for s in w_s]
        + [V(*s) for s in (block_s, mask_s, low_s, qkv_s, probs_s, low_s, x_s, low_s, ff_s, ff_s, x_s)]
        + [V((8, 16, width), bf16)]
        + [dma((units, 6)), dma((units, 6)), dma((units, 7)), dma((units, 7)), dma((units,)), dma((7,)), dma((7,))]
        + [dma((len(outs),))],
        [vmem] * 3 + [hbm] * 4,
        [hbm] * len(outs),
        collective_id=0,
        has_side_effects=True,
    )
    outs = [low_s, x_s, block_s, low_s, qkv_s, low_s, low_s, low_s, ff_s, ff_s]
    act, grad, sumsb, h1b, dzb, ob, dab, h2b, dub, fb = call(
        second_kernel,
        (x2, cotangent, block, mask, wqkv, wout, wfc, wproj),
        outs,
        [V(*s) for s in (x_s, low_s, mask_s, *w_s, low_s, qkv_s, probs_s, low_s, x_s, low_s, ff_s, ff_s, x_s, x_s)]
        + [V(*s) for s in (low_s, low_s, low_s)]
        + [dma((7,)), dma((9,))],
        [hbm, hbm, vmem, hbm, hbm, hbm, hbm, hbm],
        [hbm, hbm, vmem] + [hbm] * 7,
    )
    outs = [x_s, block_s, low_s, qkv_s, low_s, ff_s]
    tokens_grad, sumsa, gma, dza, daa, dua = call(
        third_kernel,
        (tokens, grad, block, wqkv, wout, wfc, wproj, qkva, probsa, x1a, slopea),
        outs,
        [V(*s) for s in (low_s, x_s, *w_s, qkv_s, probs_s, x_s, ff_s, x_s, low_s, low_s, low_s)]
        + [dma((10,)), dma((5,))],
        [hbm, hbm, vmem] + [hbm] * 8,
        [hbm, vmem] + [hbm] * 4,
    )

    def term(xa, ya, xb, yb):
        return jnp.einsum("td,te->de", xa, ya, preferred_element_type=f32) + jnp.einsum(
            "td,te->de", xb, yb, preferred_element_type=f32
        )

    full = [
        term(h1a, dza, h1b, dzb),
        term(oa, daa, ob, dab),
        term(h2a, dua, h2b, dub),
        term(fa, gma, fb, cotangent),
    ]
    final = [
        lax.psum(lax.psum_scatter(w.astype(bf16), "own", scatter_dimension=0, tiled=True), "grp").astype(f32)
        for w in full
    ]
    sums = lax.psum(sumsa + sumsb, ("grp", "own"))

    def own(row):
        return lax.dynamic_slice(sums, (row, me * gain1.shape[0]), (1, gain1.shape[0]))[0]

    bfc_grad = lax.dynamic_slice(
        sums[BIAS_FC : BIAS_FC + ff // width].reshape(ff), (me * bfc.shape[0],), (bfc.shape[0],)
    )
    return (
        act, tokens_grad, own(GAIN1), own(SHIFT1), final[0], own(BIAS_Q), own(BIAS_V), final[1], own(BIAS_OUT),
        own(GAIN2), own(SHIFT2), final[2], bfc_grad, final[3], own(BIAS_PROJ),
    )


def as_sent(shard):
    return jax.tree.map(lambda a: a.astype(jnp.bfloat16) if a.dtype == jnp.float32 else a, shard)


def normalize(x, gain, shift):
    centre = x - jnp.mean(x, axis=-1, keepdims=True)
    spread = jnp.mean(centre * centre, axis=-1, keepdims=True)
    return centre * lax.rsqrt(spread + EPSILON) * gain + shift


def smooth(inner):
    return jax.nn.gelu(inner, approximate=True)


def visible(doc):
    count = doc.shape[0]
    row = lax.broadcasted_iota(jnp.int32, (count, count), 0)
    col = lax.broadcasted_iota(jnp.int32, (count, count), 1)
    same = doc[:, None] == doc[None, :]
    return same & (col <= row) & ((doc[None, :] != 0) | (row == col))


def plain_forward(x, weights, mask):
    (
        gain_one,
        shift_one,
        w_qkv,
        bias_query,
        bias_value,
        w_out,
        bias_out,
        gain_two,
        shift_two,
        w_fc,
        bias_fc,
        w_proj,
        bias_proj,
    ) = weights
    width = w_qkv.shape[0]
    count = x.shape[0]
    scale = HEAD_DIM ** (-0.5)
    f32 = jnp.float32
    h_one = normalize(x, gain_one.astype(f32), shift_one.astype(f32)).astype(jnp.bfloat16)
    qkv_bias = jnp.concatenate(
        [bias_query.astype(f32), jnp.zeros((width,), f32), bias_value.astype(f32)]
    )
    packed = (jnp.dot(h_one, w_qkv, preferred_element_type=f32) + qkv_bias).astype(jnp.bfloat16)
    query = packed[:, :width].reshape(count, HEADS, HEAD_DIM)
    key = packed[:, width : 2 * width].reshape(count, HEADS, HEAD_DIM)
    value = packed[:, 2 * width :].reshape(count, HEADS, HEAD_DIM)
    scores = jnp.einsum("thd,shd->hts", query, key, preferred_element_type=f32) * scale
    scores = jnp.where(mask[None], scores, -1e30)
    probs = jax.nn.softmax(scores, axis=-1)
    probs_low = probs.astype(jnp.bfloat16)
    mixed = jnp.einsum("hts,shd->thd", probs_low, value, preferred_element_type=f32)
    mixed = mixed.reshape(count, width).astype(jnp.bfloat16)
    middle = x + (jnp.dot(mixed, w_out, preferred_element_type=f32) + bias_out.astype(f32))
    h_two = normalize(middle, gain_two.astype(f32), shift_two.astype(f32)).astype(jnp.bfloat16)
    inner = jnp.dot(h_two, w_fc, preferred_element_type=f32) + bias_fc.astype(f32)
    active = smooth(inner).astype(jnp.bfloat16)
    result = middle + (jnp.dot(active, w_proj, preferred_element_type=f32) + bias_proj.astype(f32))
    kept = (h_one, query, key, value, probs, probs_low, mixed, middle, h_two, inner, active)
    return (result, kept)


def plain_backward(x, weights, mask, grad):
    (
        gain_one,
        shift_one,
        w_qkv,
        bias_query,
        bias_value,
        w_out,
        bias_out,
        gain_two,
        shift_two,
        w_fc,
        bias_fc,
        w_proj,
        bias_proj,
    ) = weights
    result, kept = plain_forward(x, weights, mask)
    h_one, query, key, value, probs, probs_low, mixed, middle, h_two, inner, active = kept
    width = w_qkv.shape[0]
    count = x.shape[0]
    scale = HEAD_DIM ** (-0.5)
    f32 = jnp.float32
    grad_branch = grad.astype(jnp.bfloat16)
    g_wproj = jnp.einsum("tf,td->fd", active, grad_branch, preferred_element_type=f32)
    g_bproj = jnp.sum(grad_branch.astype(f32), axis=0)
    d_active = jnp.einsum("td,fd->tf", grad_branch, w_proj, preferred_element_type=f32)
    unused, pull_smooth = jax.vjp(smooth, inner)
    d_inner = pull_smooth(d_active)[0].astype(jnp.bfloat16)
    g_wfc = jnp.einsum("td,tf->df", h_two, d_inner, preferred_element_type=f32)
    g_bfc = jnp.sum(d_inner.astype(f32), axis=0)
    d_htwo = jnp.einsum("tf,df->td", d_inner, w_fc, preferred_element_type=f32)
    unused, pull_two = jax.vjp(normalize, middle, gain_two.astype(f32), shift_two.astype(f32))
    d_mid, g_gain2, g_shift2 = pull_two(d_htwo)
    d_middle = grad + d_mid
    d_attn = d_middle.astype(jnp.bfloat16)
    g_wout = jnp.einsum("td,te->de", mixed, d_attn, preferred_element_type=f32)
    g_bout = jnp.sum(d_attn.astype(f32), axis=0)
    d_mixed = jnp.einsum("te,de->td", d_attn, w_out, preferred_element_type=f32).astype(
        jnp.bfloat16
    )
    d_mixed = d_mixed.reshape(count, HEADS, HEAD_DIM)
    d_probs = jnp.einsum("thd,shd->hts", d_mixed, value, preferred_element_type=f32)
    d_value = jnp.einsum("hts,thd->shd", probs_low, d_mixed, preferred_element_type=f32)
    d_scores = probs * (d_probs - jnp.sum(d_probs * probs, axis=-1, keepdims=True))
    d_scores = d_scores.astype(jnp.bfloat16)
    d_query = jnp.einsum("hts,shd->thd", d_scores, key, preferred_element_type=f32) * scale
    d_key = jnp.einsum("hts,thd->shd", d_scores, query, preferred_element_type=f32) * scale
    d_packed = jnp.concatenate(
        [d_query.reshape(count, width), d_key.reshape(count, width), d_value.reshape(count, width)],
        axis=1,
    ).astype(jnp.bfloat16)
    g_wqkv = jnp.einsum("td,te->de", h_one, d_packed, preferred_element_type=f32)
    column_sums = jnp.sum(d_packed.astype(f32), axis=0)
    g_bquery = column_sums[:width]
    g_bvalue = column_sums[2 * width :]
    d_hone = jnp.einsum("te,de->td", d_packed, w_qkv, preferred_element_type=f32)
    unused, pull_one = jax.vjp(normalize, x, gain_one.astype(f32), shift_one.astype(f32))
    d_input, g_gain1, g_shift1 = pull_one(d_hone)
    terms = (
        g_gain1,
        g_shift1,
        g_wqkv,
        g_bquery,
        g_bvalue,
        g_wout,
        g_bout,
        g_gain2,
        g_shift2,
        g_wfc,
        g_bfc,
        g_wproj,
        g_bproj,
    )
    return (d_middle + d_input, terms)


def plain_body(
    tokens,
    doc_ids,
    cotangent,
    norm1_gain,
    norm1_shift,
    qkv_weight,
    query_bias,
    value_bias,
    out_weight,
    out_bias,
    norm2_gain,
    norm2_shift,
    fc_weight,
    fc_bias,
    proj_weight,
    proj_bias,
):
    shards = (
        norm1_gain,
        norm1_shift,
        qkv_weight,
        query_bias,
        value_bias,
        out_weight,
        out_bias,
        norm2_gain,
        norm2_shift,
        fc_weight,
        fc_bias,
        proj_weight,
        proj_bias,
    )
    mask = visible(doc_ids)

    def fetch():
        return (
            lax.all_gather(shards[0], "own", axis=0, tiled=True),
            lax.all_gather(shards[1], "own", axis=0, tiled=True),
            lax.all_gather(shards[2], "own", axis=0, tiled=True),
            lax.all_gather(shards[3], "own", axis=0, tiled=True),
            lax.all_gather(shards[4], "own", axis=0, tiled=True),
            lax.all_gather(shards[5], "own", axis=0, tiled=True),
            lax.all_gather(shards[6], "own", axis=0, tiled=True),
            lax.all_gather(shards[7], "own", axis=0, tiled=True),
            lax.all_gather(shards[8], "own", axis=0, tiled=True),
            lax.all_gather(shards[9], "own", axis=0, tiled=True),
            lax.all_gather(shards[10], "own", axis=0, tiled=True),
            lax.all_gather(shards[11], "own", axis=0, tiled=True),
            lax.all_gather(shards[12], "own", axis=0, tiled=True),
        )

    current = tokens.astype(jnp.float32)
    saved = []
    for use in range(USES):
        saved.append(current)
        current, kept = plain_forward(current, fetch(), mask)
    grad = cotangent.astype(jnp.float32)
    summed = None
    for use in reversed(range(USES)):
        grad, terms = plain_backward(saved[use], fetch(), mask, grad)
        if summed is None:
            summed = terms
        else:
            summed = tuple((first + second for first, second in zip(summed, terms)))
    owned = (
        lax.psum_scatter(summed[0], "own", scatter_dimension=0, tiled=True),
        lax.psum_scatter(summed[1], "own", scatter_dimension=0, tiled=True),
        lax.psum_scatter(summed[2], "own", scatter_dimension=0, tiled=True),
        lax.psum_scatter(summed[3], "own", scatter_dimension=0, tiled=True),
        lax.psum_scatter(summed[4], "own", scatter_dimension=0, tiled=True),
        lax.psum_scatter(summed[5], "own", scatter_dimension=0, tiled=True),
        lax.psum_scatter(summed[6], "own", scatter_dimension=0, tiled=True),
        lax.psum_scatter(summed[7], "own", scatter_dimension=0, tiled=True),
        lax.psum_scatter(summed[8], "own", scatter_dimension=0, tiled=True),
        lax.psum_scatter(summed[9], "own", scatter_dimension=0, tiled=True),
        lax.psum_scatter(summed[10], "own", scatter_dimension=0, tiled=True),
        lax.psum_scatter(summed[11], "own", scatter_dimension=0, tiled=True),
        lax.psum_scatter(summed[12], "own", scatter_dimension=0, tiled=True),
    )
    final = jax.tree.map(lambda part: part.astype(jnp.float32), lax.psum(as_sent(owned), "grp"))
    return (current.astype(jnp.bfloat16), grad) + tuple(final)


def solution(mesh):
    return jax.shard_map(
        kernels_body if tuple(mesh.axis_sizes) == (4, 8) else plain_body,
        mesh=mesh,
        in_specs=(
            P(("grp", "own"), None),
            P(("grp", "own")),
            P(("grp", "own"), None),
            P("own"),
            P("own"),
            P("own", None),
            P("own"),
            P("own"),
            P("own", None),
            P("own"),
            P("own"),
            P("own"),
            P("own", None),
            P("own"),
            P("own", None),
            P("own"),
        ),
        out_specs=(
            P(("grp", "own"), None),
            P(("grp", "own"), None),
            P("own"),
            P("own"),
            P("own", None),
            P("own"),
            P("own"),
            P("own", None),
            P("own"),
            P("own"),
            P("own"),
            P("own", None),
            P("own"),
            P("own", None),
            P("own"),
        ),
        check_vma=False,
    )
```

```python
import functools

import jax
import jax.numpy as jnp
from jax import lax
from jax.experimental import pallas as pl
from jax.experimental.pallas import tpu as pltpu
from jax.sharding import PartitionSpec as P

HEADS = 12
HEAD_DIM = 64
USES = 2
EPSILON = 1e-05
SCALE = HEAD_DIM ** (-0.5)
TANH_SCALE = 0.7978845608028654
TANH_CUBIC = 0.044715
MESH = pl.DeviceIdType.MESH
f32 = jnp.float32
bf16 = jnp.bfloat16

GAIN1, SHIFT1, BIAS_Q, BIAS_V, BIAS_OUT, GAIN2, SHIFT2, BIAS_PROJ, BIAS_FC = range(9)


def dot(a, b, ca=1, cb=0):
    return lax.dot_general(a, b, (((ca,), (cb,)), ((), ())), preferred_element_type=f32)


def loop(count, body):
    def step(i, carry):
        body(i)
        return carry

    lax.fori_loop(0, count, step, 0)


def span(begin, end, body):
    def step(i, carry):
        body(i)
        return carry

    lax.fori_loop(begin, end, step, 0)


def part(i, size):
    return pl.ds(pl.multiple_of(i * size, size), size)


def centred(x):
    centre = x - jnp.mean(x, axis=-1, keepdims=True)
    spread = jnp.mean(centre * centre, axis=-1, keepdims=True)
    return centre, lax.rsqrt(spread + EPSILON)


def norm_forward(x, gain, shift, h):
    rows = 128

    def step(i):
        centre, r = centred(x[part(i, rows), :].astype(f32))
        h[part(i, rows), :] = (centre * r * gain + shift).astype(bf16)

    loop(x.shape[0] // rows, step)


def norm_backward(x, dh, gain, grad, out, sums, gain_row, shift_row, low=None):
    rows = 128

    def step(i):
        centre, r = centred(x[part(i, rows), :].astype(f32))
        n = centre * r
        d = dh[part(i, rows), :]
        sums[gain_row : gain_row + 1, :] += jnp.sum(d * n, axis=0, keepdims=True)
        sums[shift_row : shift_row + 1, :] += jnp.sum(d, axis=0, keepdims=True)
        e = d * gain
        inner = e - jnp.mean(e, axis=-1, keepdims=True) - n * jnp.mean(e * n, axis=-1, keepdims=True)
        result = grad[part(i, rows), :].astype(f32) + r * inner
        out[part(i, rows), :] = result
        if low is not None:
            low[part(i, rows), :] = result.astype(bf16)

    loop(x.shape[0] // rows, step)


def column_sum(x):
    return jnp.sum(x.astype(f32), axis=0, keepdims=True)


def make_mask(doc, mask):
    count = doc.shape[1]
    half = count // 2
    ids = doc[0:1, :].astype(f32)
    keys = jnp.broadcast_to(ids, (128, count)).T[:, :1]
    for k0, q0, place in ((0, 0, 0), (half, half, count)):
        width = count - q0
        row = lax.broadcasted_iota(jnp.int32, (half, width), 0) + k0
        col = lax.broadcasted_iota(jnp.int32, (half, width), 1) + q0
        key = keys[k0 : k0 + half]
        same = (key == ids[:, q0:]) & (row <= col) & ((key != 0.0) | (row == col))
        mask[:, place : place + width] = jnp.where(same, 0.0, -1e30)


def head_lanes(h, x):
    lane = lax.broadcasted_iota(jnp.int32, (1, 2 * HEAD_DIM), 1)
    keep = (lane < HEAD_DIM) if h == 0 else (lane >= HEAD_DIM)
    return jnp.where(keep, x, jnp.zeros_like(x))


def head_place(i, h, half, width):
    row = pl.ds(pl.multiple_of((i // 2) * half, half), half)
    col = (lax.rem(i, 2) * 2 + h) * width
    return row, col


def attention_forward(qkv, mask, probs, o, begin=0, end=6):
    count, width = o.shape
    half = count // 2
    pair = 2 * HEAD_DIM

    def step(i):
        col = part(i, pair)
        q = qkv[:, col]
        k = qkv[:, pl.ds(pl.multiple_of(width + i * pair, pair), pair)]
        v = qkv[:, pl.ds(pl.multiple_of(2 * width + i * pair, pair), pair)]
        vt = v.T
        outs = []
        for h in range(2):
            kh = head_lanes(h, k)
            s0 = dot(kh[:half], q, 1, 1) + mask[:, :count]
            s1 = dot(kh[half:], q[half:], 1, 1) + mask[:, count:]
            m0 = jnp.max(s0, axis=0, keepdims=True)
            m1 = jnp.max(s1, axis=0, keepdims=True)
            top = jnp.concatenate([m0[:, :half], jnp.maximum(m0[:, half:], m1)], axis=1)
            e0 = jnp.exp(s0 - top)
            e1 = jnp.exp(s1 - top[:, half:])
            l0 = jnp.sum(e0, axis=0, keepdims=True)
            l1 = jnp.sum(e1, axis=0, keepdims=True)
            r = 1.0 / jnp.concatenate([l0[:, :half], l0[:, half:] + l1], axis=1)
            p0 = (e0 * r).astype(bf16)
            p1 = (e1 * r[:, half:]).astype(bf16)
            row, at = head_place(i, h, half, count + half)
            probs[row, pl.ds(pl.multiple_of(at, 128), count)] = p0
            probs[row, pl.ds(pl.multiple_of(at + count, 128), half)] = p1
            vh = vt[h * HEAD_DIM : (h + 1) * HEAD_DIM]
            first = dot(vh[:, :half], p0)
            second = dot(vh[:, half:], p1)
            outs.append(jnp.concatenate([first[:, :half], first[:, half:] + second], axis=1))
        o[:, col] = jnp.concatenate(outs, axis=0).astype(bf16).T

    span(begin, end, step)


def attention_backward(qkv, probs, do, dz, sums, begin=0, end=6):
    count, width = do.shape
    half = count // 2
    pair = 2 * HEAD_DIM

    def step(i):
        cq = part(i, pair)
        ck = pl.ds(pl.multiple_of(width + i * pair, pair), pair)
        cv = pl.ds(pl.multiple_of(2 * width + i * pair, pair), pair)
        q, k, v, d = qkv[:, cq], qkv[:, ck], qkv[:, cv], do[:, cq]
        dq = dk = dv = None
        for h in range(2):
            dh, kh, qh = head_lanes(h, d), head_lanes(h, k), head_lanes(h, q)
            row, at = head_place(i, h, half, count + half)
            p0 = probs[row, pl.ds(pl.multiple_of(at, 128), count)]
            p1 = probs[row, pl.ds(pl.multiple_of(at + count, 128), half)]
            d0 = dot(v[:half], dh, 1, 1)
            d1 = dot(v[half:], dh[half:], 1, 1)
            w0 = p0.astype(f32)
            w1 = p1.astype(f32)
            t0 = jnp.sum(d0 * w0, axis=0, keepdims=True)
            t1 = jnp.sum(d1 * w1, axis=0, keepdims=True)
            t = jnp.concatenate([t0[:, :half], t0[:, half:] + t1], axis=1)
            s0 = (w0 * (d0 - t)).astype(bf16)
            s1 = (w1 * (d1 - t[:, half:])).astype(bf16)
            v_term = jnp.concatenate([dot(p0, dh), dot(p1, dh[half:])], axis=0)
            k_term = jnp.concatenate([dot(s0, qh), dot(s1, qh[half:])], axis=0)
            qa = dot(s0, kh[:half], 0, 0)
            qb = dot(s1, kh[half:], 0, 0)
            q_term = jnp.concatenate([qa[:half], qa[half:] + qb], axis=0)
            dq = q_term if dq is None else dq + q_term
            dk = k_term if dk is None else dk + k_term
            dv = v_term if dv is None else dv + v_term
        dq = (dq * SCALE).astype(bf16)
        dv = dv.astype(bf16)
        dz[:, cq] = dq
        dz[:, ck] = dk.astype(bf16)
        dz[:, cv] = dv
        sums[BIAS_Q : BIAS_Q + 1, cq] += column_sum(dq)
        sums[BIAS_V : BIAS_V + 1, cq] += column_sum(dv)

    span(begin, end, step)


def small(block, row):
    return block[row : row + 1, :]


def hidden_forward(h2, wfc, block, f, slope, begin, end):
    width = h2.shape[1]

    def hidden(i):
        col = part(i, width)
        u = dot(h2[...], wfc[:, col]) + block[pl.ds(BIAS_FC + i, 1), :]
        square = u * u
        t = jnp.tanh(u * (TANH_SCALE + (TANH_SCALE * TANH_CUBIC) * square))
        rise = 0.5 + 0.5 * t
        f[:, col] = (u * rise).astype(bf16)
        inner = TANH_SCALE + (3.0 * TANH_SCALE * TANH_CUBIC) * square
        slope[:, col] = (rise + (0.5 * u) * (1.0 - t * t) * inner).astype(bf16)

    span(begin, end, hidden)


def forward_layer(x, block, weights, mask, kept, result, ready):
    wqkv, wout, wfc, wproj = weights
    h1, qkv, probs, o, x1, h2, slope, f = kept
    width = x.shape[1]
    ready("small")
    norm_forward(x, small(block, GAIN1), small(block, SHIFT1), h1)
    ready("qkv")
    h = h1[...]
    qkv[:, :width] = (dot(h, wqkv[:, :width]) + small(block, BIAS_Q)).astype(bf16) * SCALE
    qkv[:, width : 2 * width] = dot(h, wqkv[:, width : 2 * width]).astype(bf16)
    qkv[:, 2 * width :] = (dot(h, wqkv[:, 2 * width :]) + small(block, BIAS_V)).astype(bf16)
    attention_forward(qkv, mask, probs, o)
    ready("out")
    x1[...] = x[...].astype(f32) + (dot(o[...], wout[...]) + small(block, BIAS_OUT))
    norm_forward(x1, small(block, GAIN2), small(block, SHIFT2), h2)
    ready("fc")

    hidden_forward(h2, wfc, block, f, slope, 0, wfc.shape[1] // width)
    ready("proj")
    result[...] = x1[...] + (dot(f[...], wproj[...]) + small(block, BIAS_PROJ))


def backward_hidden(gm, wproj, slope, du, sums):
    width = gm.shape[1]

    def hidden(i):
        col = part(i, width)
        d = (dot(gm[...], wproj[col, :], 1, 1) * slope[:, col].astype(f32)).astype(bf16)
        du[:, col] = d
        sums[pl.ds(BIAS_FC + i, 1), :] = column_sum(d)

    loop(wproj.shape[0] // width, hidden)


def backward_layer(x, grad, gm, block, weights, kept, scratch, result, sums, done):
    wqkv, wout, wfc, wproj = weights
    qkv, probs, x1, slope = kept
    dh, do, da = scratch
    sums[BIAS_PROJ : BIAS_PROJ + 1, :] = column_sum(gm[...])
    backward_hidden(gm, wproj, slope, slope, sums)
    done("du")
    dh[...] = dot(slope[...], wfc[...], 1, 1)
    norm_backward(x1, dh, small(block, GAIN2), grad, result, sums, GAIN2, SHIFT2, da)
    done("da")
    sums[BIAS_OUT : BIAS_OUT + 1, :] = column_sum(da[...])
    do[...] = dot(da[...], wout[...], 1, 1).astype(bf16)
    attention_backward(qkv, probs, do, qkv, sums)
    done("dz")
    dh[...] = dot(qkv[...], wqkv[...], 1, 1)
    norm_backward(x, dh, small(block, GAIN1), result, result, sums, GAIN1, SHIFT1)


def coords():
    own = lax.axis_index("own")
    return lax.axis_index("grp"), own // 2, lax.rem(own, 2)


class Unit:
    def __init__(self, shard, full, row, rows, col, cols):
        self.shard, self.full = shard, full
        self.row, self.rows, self.col, self.cols = row, rows, col, cols

    def mine(self, half=None):
        rows = self.rows if half is None else self.rows // 2
        start = self.row + (0 if half is None else half * rows)
        return self.shard.at[pl.ds(start, rows), pl.ds(self.col, self.cols)]

    def block(self, owner, half=None):
        rows = self.rows if half is None else self.rows // 2
        start = owner * self.shard.shape[0] + self.row + (0 if half is None else half * rows)
        return self.full.at[pl.ds(pl.multiple_of(start, 16), rows), pl.ds(self.col, self.cols)]


PIECES = [(1, 0), (1, 1), (2, 0), (2, 1), (3, 0), (3, 1)]


class Gather:
    def __init__(self, units, link_send, link_recv, core_send, core_recv, own_sem):
        self.units = units
        self.link_send, self.link_recv = link_send, link_recv
        self.core_send, self.core_recv, self.own_sem = core_send, core_recv, own_sem
        self.grp, self.chip, self.core = coords()
        self.odd = lax.rem(self.grp, 2)
        self.sent = []

    def owner(self, offset):
        return jnp.bitwise_xor(self.chip, offset) * 2 + self.core

    def device(self, chip_offset, along_z=False):
        own = jnp.bitwise_xor(self.chip, chip_offset) * 2 + self.core
        grp = self.grp + 1 - 2 * self.odd if along_z else self.grp
        return (grp, own)

    def link(self, k, src, dst, piece, out, device):
        return pltpu.make_async_remote_copy(
            src_ref=src,
            dst_ref=dst,
            send_sem=self.link_send.at[k, out],
            recv_sem=self.link_recv.at[k, piece],
            device_id=device,
            device_id_type=MESH,
        )

    def across(self, k, src, dst, slot):
        return pltpu.make_async_remote_copy(
            src_ref=src,
            dst_ref=dst,
            send_sem=self.core_send.at[k, slot],
            recv_sem=self.core_recv.at[k, slot],
            device_id=(self.grp, self.chip * 2 + 1 - self.core),
            device_id_type=MESH,
        )

    def own(self, k):
        unit = self.units[k]
        return pltpu.make_async_copy(unit.mine(), unit.block(self.owner(0)), self.own_sem.at[k])

    def first(self, k, offset, half, out):
        unit = self.units[k]
        piece = PIECES.index((offset, half))
        return self.link(
            k, unit.mine(half), unit.block(self.owner(0), half), piece, out, self.device(offset)
        )

    def relay(self, k, offset, half, way, out):
        unit = self.units[k]
        piece = unit.block(self.owner(offset), half)
        return self.link(k, piece, piece, PIECES.index((3, half)), out, self.device(way))

    def pair(self, k, offset, half, out):
        unit = self.units[k]
        piece = unit.block(self.owner(offset), half)
        return self.link(k, piece, piece, PIECES.index((offset, half)), out, self.device(0, True))

    def hand(self, k, offset, half):
        unit = self.units[k]
        piece = unit.block(self.owner(offset), half)
        return self.across(k, piece, piece, PIECES.index((offset, half)))

    def arrived(self, k, offset, half):
        unit = self.units[k]
        piece = unit.block(self.owner(offset), half)
        self.link(k, piece, piece, PIECES.index((offset, half)), 0, self.device(1)).wait_recv()

    def even(self, k, out):
        if out < 4:
            return self.first(k, *((1, 0), (2, 1), (1, 1), (2, 0))[out], out)
        return self.pair(k, *((1, 0), (2, 1))[out - 4], out)

    def uneven(self, k, out):
        if out < 2:
            return self.first(k, *((1, 1), (2, 0))[out], out)
        if out < 4:
            return self.relay(k, *((2, 0, 1), (1, 1, 2))[out - 2], out)
        return self.pair(k, 3, out - 4, out)

    def start(self, k):
        @pl.when(self.odd == 0)
        def _():
            for out in range(4):
                self.even(k, out).start()

        @pl.when(self.odd == 1)
        def _():
            for out in range(2):
                self.uneven(k, out).start()

        unit = self.units[k]
        self.across(k, unit.mine(), unit.block(self.owner(0)), len(PIECES)).start()
        self.own(k).start()

    def serve_first(self, k):
        @pl.when(self.odd == 0)
        def _():
            for at, (offset, half) in enumerate(((1, 0), (2, 1), (1, 1), (2, 0))):
                self.arrived(k, offset, half)
                if at < 2:
                    self.even(k, 4 + at).start()
                self.hand(k, offset, half).start()

        @pl.when(self.odd == 1)
        def _():
            for at, (offset, half) in enumerate(((2, 0), (1, 1))):
                self.arrived(k, offset, half)
                self.uneven(k, 2 + at).start()
                self.hand(k, offset, half).start()

    def serve_second(self, k):
        @pl.when(self.odd == 0)
        def _():
            for half in range(2):
                self.arrived(k, 3, half)
                self.hand(k, 3, half).start()

        @pl.when(self.odd == 1)
        def _():
            for half in range(2):
                self.arrived(k, 3, half)
                self.uneven(k, 4 + half).start()
                self.hand(k, 3, half).start()
            for offset, half in ((1, 0), (2, 1)):
                self.arrived(k, offset, half)
                self.hand(k, offset, half).start()

    def finish(self, k):
        unit = self.units[k]
        other = 1 - 2 * self.core
        self.own(k).wait()
        whole = unit.block(self.owner(0) + other)
        self.across(k, whole, whole, len(PIECES)).wait_recv()
        for slot, (offset, half) in enumerate(PIECES):
            piece = unit.block(self.owner(offset) + other, half)
            self.across(k, piece, piece, slot).wait_recv()

    def drain(self, k):
        @pl.when(self.odd == 0)
        def _():
            for out in range(6):
                self.even(k, out).wait_send()

        @pl.when(self.odd == 1)
        def _():
            for out in range(6):
                self.uneven(k, out).wait_send()

        unit = self.units[k]
        self.across(k, unit.mine(), unit.block(self.owner(0)), len(PIECES)).wait_send()
        for offset, half in PIECES:
            self.hand(k, offset, half).wait_send()


def store(copies, sem, src, dst):
    copy = pltpu.make_async_copy(src, dst, sem.at[len(copies)])
    copy.start()
    copies.append(copy)


def first_kernel(
    tokens, doc, packed, sqkv, sout, sfc, sproj,
    x2_out, block_out, mask_out, wqkv_out, wout_out, wfc_out, wproj_out,
    h1_out, qkv_out, probs_out, o_out, x1_out, h2_out, slope_out, f_out,
    wqkv, wout, wfc, wproj, block, mask, h1, qkv, probs, o, x1, h2, slope, f, x2, many,
    link_send, link_recv, core_send, core_recv, own_sem, small_send, small_recv, out_sem,
):
    grp, chip, core = coords()
    me = chip * 2 + core
    width = tokens.shape[1]
    barrier = pltpu.get_barrier_semaphore()
    peers = [(grp, jnp.bitwise_xor(me, j)) for j in range(1, 8)]
    peers.append((grp + 1 - 2 * lax.rem(grp, 2), me))
    for peer in peers:
        pl.semaphore_signal(barrier, inc=1, device_id=peer, device_id_type=MESH)
    pl.semaphore_wait(barrier, len(peers))

    units = [Unit(sqkv, wqkv, 0, sqkv.shape[0], i * width, width) for i in range(3)]
    units += [Unit(sout, wout, 0, sout.shape[0], 0, width)]
    units += [Unit(sfc, wfc, 0, sfc.shape[0], i * width, width) for i in range(sfc.shape[1] // width)]
    thirds = sproj.shape[0] // 3
    units += [Unit(sproj, wproj, i * thirds, thirds, 0, width) for i in range(3)]
    gather = Gather(units, link_send, link_recv, core_send, core_recv, own_sem)
    count = len(units)

    def small_copy(j, slot):
        return pltpu.make_async_remote_copy(
            src_ref=packed,
            dst_ref=many.at[slot],
            send_sem=small_send.at[j - 1],
            recv_sem=small_recv.at[j - 1],
            device_id=(grp, jnp.bitwise_xor(me, j)),
            device_id_type=MESH,
        )

    for j in range(1, 8):
        small_copy(j, j).start()
    gather.start(0)
    gather.start(1)
    copies = []

    def slot(s):
        if s < count:
            gather.serve_first(s)
        if s + 2 < count:
            gather.start(s + 2)
        if 0 <= s - 1 < count:
            gather.serve_second(s - 1)
        if 0 <= s - 2 < count:
            gather.finish(s - 2)

    make_mask(doc, mask)
    store(copies, out_sem, mask, mask_out)
    total = packed[...].astype(f32)
    for j in range(1, 8):
        small_copy(j, j).wait_recv()
        total = total + many[j].astype(f32)
    block[...] = total
    store(copies, out_sem, block, block_out)
    norm_forward(tokens, small(block, GAIN1), small(block, SHIFT1), h1)
    store(copies, out_sem, h1, h1_out)
    for s in range(3):
        slot(s)
    h = h1[...]
    qkv[:, :width] = (dot(h, wqkv[:, :width]) + small(block, BIAS_Q)).astype(bf16) * SCALE
    slot(3)
    qkv[:, width : 2 * width] = dot(h1[...], wqkv[:, width : 2 * width]).astype(bf16)
    slot(4)
    store(copies, out_sem, wqkv, wqkv_out)
    qkv[:, 2 * width :] = (dot(h1[...], wqkv[:, 2 * width :]) + small(block, BIAS_V)).astype(bf16)
    store(copies, out_sem, qkv, qkv_out)
    attention_forward(qkv, mask, probs, o, 0, 2)
    slot(5)
    store(copies, out_sem, wout, wout_out)
    attention_forward(qkv, mask, probs, o, 2, 4)
    slot(6)
    attention_forward(qkv, mask, probs, o, 4, 6)
    store(copies, out_sem, probs, probs_out)
    store(copies, out_sem, o, o_out)
    x1[...] = tokens[...].astype(f32) + (dot(o[...], wout[...]) + small(block, BIAS_OUT))
    norm_forward(x1, small(block, GAIN2), small(block, SHIFT2), h2)
    store(copies, out_sem, x1, x1_out)
    store(copies, out_sem, h2, h2_out)
    slot(7)
    hidden_forward(h2, wfc, block, f, slope, 0, 2)
    slot(8)
    hidden_forward(h2, wfc, block, f, slope, 2, 3)
    slot(9)
    store(copies, out_sem, wfc, wfc_out)
    hidden_forward(h2, wfc, block, f, slope, 3, 4)
    store(copies, out_sem, f, f_out)
    store(copies, out_sem, slope, slope_out)

    def project(i):
        rows = [pl.ds(owner * sproj.shape[0] + i * thirds, thirds) for owner in range(8)]
        left = jnp.concatenate([f[:, at] for at in rows], axis=1)
        right = jnp.concatenate([wproj[at, :] for at in rows], axis=0)
        return dot(left, right)

    slot(10)
    x2[...] = x1[...] + (project(0) + small(block, BIAS_PROJ))
    slot(11)
    x2[...] += project(1)
    slot(12)
    store(copies, out_sem, wproj, wproj_out)
    x2[...] += project(2)
    store(copies, out_sem, x2, x2_out)
    for k in range(count):
        gather.drain(k)
    for j in range(1, 8):
        small_copy(j, j).wait_send()
    for copy in copies:
        copy.wait()


def third_kernel(
    x_in, cot_in, grad_in, block, wqkv_in, wout_in, wfc_in, wproj_in,
    h1a_in, qkv_in, probs_in, oa_in, x1_in, h2a_in, slope_in, fa_in,
    sumsb, h1b_in, dzb_in, ob_in, dab_in, h2b_in, dub_in, fb_in,
    grad_out, sums_out, gqkv_out, gout_out, gfc_out, gproj_out,
    x, cot, grad, tiles, h1a, qkv, oa, x1, h2a, slope, shared, h1b, dzb, ob, dab, h2b, dub,
    gm, dh, do, da, sums,
    buf_p, buf_o, recv_p, recv_o, hop1_p, hop1_o, hop2_p, hop2_o, zin_p, zin_o, zmid_p, zmid_o, tot_p, tot_o,
    small_in, small_tot,
    in_sem, tile_sem, out_sem, send, recv, small_send, small_recv,
):
    grp, chip, core = coords()
    yy, xx = chip // 2, lax.rem(chip, 2)
    me = chip * 2 + core
    width = x.shape[1]
    loads = {}

    def load(name, src, dst):
        copy = pltpu.make_async_copy(src, dst, in_sem.at[len(loads)])
        copy.start()
        loads[name] = copy

    count = x.shape[0]
    fb, fa = shared.at[pl.ds(0, count), :], shared.at[pl.ds(count, count), :]
    probs = shared.at[pl.ds(0, probs_in.shape[0]), :]
    load("grad", grad_in, grad)
    load("fb", fb_in, fb)
    load("cot", cot_in, cot)
    load("fa", fa_in, fa)

    ff_tiles = wfc_in.shape[1] // width
    sources = [wproj_in.at[pl.ds(i * width, width), :] for i in range(ff_tiles)]
    sources += [wfc_in.at[:, pl.ds(i * width, width)] for i in range(ff_tiles)]
    sources += [wout_in] + [wqkv_in.at[:, pl.ds(i * width, width)] for i in range(3)]
    ring = tiles.shape[0]

    def tile_copy(t):
        return pltpu.make_async_copy(sources[t], tiles.at[t % ring], tile_sem.at[t % ring])

    def tile(t):
        tile_copy(t).wait()
        return tiles[t % ring]

    def next_tile(t):
        if t + ring < len(sources):
            tile_copy(t + ring).start()

    core_peer = (grp, jnp.bitwise_xor(me, 1))
    x_peer = (grp, jnp.bitwise_xor(me, 2))
    y_peer = (grp, jnp.bitwise_xor(me, 4))
    low = grp == 1
    middle = (grp == 1) | (grp == 2)
    end = jnp.logical_not(middle)
    inward = (jnp.where(grp == 0, 1, 2), me)
    outward = (jnp.where(low, 0, 3), me)
    across = (jnp.where(low, 2, 1), me)

    barrier = pltpu.get_barrier_semaphore()
    for peer in (core_peer, x_peer, y_peer):
        pl.semaphore_signal(barrier, inc=1, device_id=peer, device_id_type=MESH)

    @pl.when(end)
    def _():
        pl.semaphore_signal(barrier, inc=1, device_id=inward, device_id_type=MESH)
        pl.semaphore_wait(barrier, 4)

    @pl.when(middle)
    def _():
        pl.semaphore_signal(barrier, inc=1, device_id=outward, device_id_type=MESH)
        pl.semaphore_signal(barrier, inc=1, device_id=across, device_id_type=MESH)
        pl.semaphore_wait(barrier, 5)

    def remote(src, dst, i, stage, peer):
        return pltpu.make_async_remote_copy(
            src_ref=src, dst_ref=dst, send_sem=send.at[i, stage], recv_sem=recv.at[i, stage],
            device_id=peer, device_id_type=MESH,
        )

    thirds = 3
    chunks = thirds + ff_tiles + 1 + 3
    copies = []

    class Chunk:
        def __init__(self, i):
            self.i = i
            if i < thirds:
                at, sets = i, (buf_p, recv_p, hop1_p, hop2_p, zin_p, zmid_p, tot_p)
            else:
                at, sets = i - thirds, (buf_o, recv_o, hop1_o, hop2_o, zin_o, zmid_o, tot_o)
            self.slot = at % sets[0].shape[0]
            self.again = at >= sets[0].shape[0]
            self.buf = sets[0].at[self.slot]
            self.recv, self.hop1, self.hop2, self.zin, self.zmid, self.tot = (s.at[at] for s in sets[1:])
            self.rows = sets[1].shape[3]
            half = self.rows // 2
            self.top, self.bottom = pl.ds(0, half), pl.ds(half, half)

        def to_core(self):
            return remote(self.buf.at[1 - core], self.recv, self.i, 0, core_peer)

        def first(self):
            return (
                remote(self.recv.at[:, 1 - xx, self.top, :], self.hop1.at[0], self.i, 1, x_peer),
                remote(self.recv.at[1 - yy, :, self.bottom, :], self.hop1.at[1], self.i, 2, y_peer),
            )

        def second(self):
            return (
                remote(self.recv.at[1 - yy, xx, self.top, :], self.hop2.at[0], self.i, 3, y_peer),
                remote(self.recv.at[yy, 1 - xx, self.bottom, :], self.hop2.at[1], self.i, 4, x_peer),
            )

        def to_middle(self):
            return remote(self.recv.at[yy, xx], self.zin, self.i, 5, inward)

        def between(self):
            return remote(self.recv.at[yy, xx], self.zmid, self.i, 6, across)

        def to_end(self):
            return remote(self.tot, self.tot, self.i, 7, outward)

        def begin(self):
            if self.again:
                Chunk(self.i - len_ring(self.i)).to_core().wait_send()

        def stage_b(self):
            self.to_core().wait_recv()
            self.recv[...] = self.recv[...] + self.buf[core]
            for copy in self.first():
                copy.start()

        def stage_c(self):
            for copy in self.first():
                copy.wait_recv()
            self.recv[:, xx, self.top, :] = self.recv[:, xx, self.top, :] + self.hop1[0]
            self.recv[yy, :, self.bottom, :] = self.recv[yy, :, self.bottom, :] + self.hop1[1]
            for copy in self.second():
                copy.start()

        def stage_d(self):
            for copy in self.second():
                copy.wait_recv()
            self.recv[yy, xx, self.top, :] = self.recv[yy, xx, self.top, :] + self.hop2[0]
            self.recv[yy, xx, self.bottom, :] = self.recv[yy, xx, self.bottom, :] + self.hop2[1]

            @pl.when(end)
            def _():
                self.to_middle().start()

        def stage_e(self):
            @pl.when(middle)
            def _():
                self.to_middle().wait_recv()
                self.recv[yy, xx] = self.recv[yy, xx] + self.zin[...]
                self.between().start()

        def stage_f(self):
            @pl.when(middle)
            def _():
                self.between().wait_recv()
                self.tot[...] = self.recv[yy, xx] + self.zmid[...]
                self.to_end().start()

        def stage_g(self):
            @pl.when(end)
            def _():
                self.to_end().wait_recv()

            i = self.i
            if i < thirds:
                place = gproj_out.at[pl.ds(i * self.rows, self.rows), :]
            elif i < thirds + ff_tiles:
                place = gfc_out.at[:, pl.ds((i - thirds) * width, width)]
            elif i == thirds + ff_tiles:
                place = gout_out
            else:
                place = gqkv_out.at[:, pl.ds((i - thirds - ff_tiles - 1) * width, width)]
            store(copies, out_sem, self.tot, place)

        def finish(self):
            last = chunks - buf_o.shape[0] if self.i >= thirds else thirds - buf_p.shape[0]
            if self.i >= last:
                self.to_core().wait_send()
            for copy in self.first() + self.second():
                copy.wait_send()

            @pl.when(end)
            def _():
                self.to_middle().wait_send()

            @pl.when(middle)
            def _():
                self.between().wait_send()
                self.to_end().wait_send()

    def len_ring(i):
        return buf_p.shape[0] if i < thirds else buf_o.shape[0]

    def put(chunk, value):
        rows = chunk.rows
        for owner in range(8):
            chunk.buf[owner % 2, owner // 4, (owner // 2) % 2] = value[owner * rows : (owner + 1) * rows].astype(bf16)

    def made(i):
        Chunk(i).to_core().start()

    def proj_chunk(i):
        chunk = Chunk(i)
        chunk.begin()
        rows = chunk.rows
        for owner in range(8):
            col = pl.ds((owner * thirds + i) * rows, rows)
            value = dot(fb[:, col], cot[...], 0, 0) + dot(fa[:, col], gm[...], 0, 0)
            chunk.buf[owner % 2, owner // 4, (owner // 2) % 2] = value.astype(bf16)
        made(i)

    def other_chunk(i, xa, ya, xb, yb, col):
        chunk = Chunk(i)
        chunk.begin()
        cols = pl.ds(col * width, width)
        value = dot(xa[...], ya[:, cols], 0, 0) + dot(xb[...], yb[:, cols], 0, 0)
        put(chunk, value)
        made(i)

    def b(i):
        Chunk(i).stage_b()

    def period(k):
        for lag, name in ((0, "stage_c"), (1, "stage_d"), (2, "stage_e"), (3, "stage_f"), (5, "stage_g")):
            if 0 <= k - lag < chunks:
                getattr(Chunk(k - lag), name)()

    for t in range(ring):
        tile_copy(t).start()
    load("slope", slope_in, slope)
    load("x1", x1_in, x1)
    load("h2a", h2a_in, h2a)
    load("h2b", h2b_in, h2b)
    load("dub", dub_in, dub)
    load("qkv", qkv_in, qkv)
    load("oa", oa_in, oa)
    load("ob", ob_in, ob)
    load("dab", dab_in, dab)
    load("h1a", h1a_in, h1a)
    load("h1b", h1b_in, h1b)
    load("dzb", dzb_in, dzb)
    load("x", x_in, x)

    sums[...] = sumsb[...]
    loads["grad"].wait()
    gm[...] = grad[...].astype(bf16)
    loads["fb"].wait()
    loads["cot"].wait()
    loads["fa"].wait()
    proj_chunk(0)
    proj_chunk(1)
    b(0)
    sums[BIAS_PROJ : BIAS_PROJ + 1, :] += column_sum(gm[...])
    proj_chunk(2)
    load("probs", probs_in, probs)
    b(1)
    loads["slope"].wait()

    def hidden(t):
        cols = pl.ds(t * width, width)
        d = (dot(gm[...], tile(t), 1, 1) * slope[:, cols].astype(f32)).astype(bf16)
        slope[:, cols] = d
        sums[BIAS_FC + t : BIAS_FC + t + 1, :] += column_sum(d)
        next_tile(t)

    hidden(0)
    hidden(1)
    period(0)
    b(2)
    hidden(2)
    hidden(3)
    total = dot(slope[:, :width], tile(4), 1, 1)
    next_tile(4)
    for t in range(1, ff_tiles):
        total = total + dot(slope[:, t * width : (t + 1) * width], tile(ff_tiles + t), 1, 1)
        next_tile(ff_tiles + t)
    dh[...] = total
    period(1)
    for name in ("h2a", "h2b", "dub", "x1"):
        loads[name].wait()
    other_chunk(3, h2a, slope, h2b, dub, 0)
    norm_backward(x1, dh, small(block, GAIN2), grad, grad, sums, GAIN2, SHIFT2, da)
    do[...] = dot(da[...], tile(2 * ff_tiles), 1, 1).astype(bf16)
    sums[BIAS_OUT : BIAS_OUT + 1, :] += column_sum(da[...])
    b(3)
    period(2)
    other_chunk(4, h2a, slope, h2b, dub, 1)
    loads["qkv"].wait()
    loads["probs"].wait()
    attention_backward(qkv, probs, do, qkv, sums, 0, 2)
    b(4)
    period(3)
    other_chunk(5, h2a, slope, h2b, dub, 2)
    attention_backward(qkv, probs, do, qkv, sums, 2, 4)
    b(5)
    period(4)
    other_chunk(6, h2a, slope, h2b, dub, 3)
    attention_backward(qkv, probs, do, qkv, sums, 4, 6)
    b(6)
    period(5)
    for name in ("oa", "ob", "dab"):
        loads[name].wait()
    other_chunk(7, oa, da, ob, dab, 0)
    total = dot(qkv[:, :width], tile(2 * ff_tiles + 1), 1, 1)
    for t in range(1, 3):
        total = total + dot(qkv[:, t * width : (t + 1) * width], tile(2 * ff_tiles + 1 + t), 1, 1)
    dh[...] = total
    b(7)
    period(6)
    for name in ("h1a", "h1b", "dzb"):
        loads[name].wait()
    other_chunk(8, h1a, qkv, h1b, dzb, 0)
    loads["x"].wait()
    norm_backward(x, dh, small(block, GAIN1), grad, grad, sums, GAIN1, SHIFT1)
    store(copies, out_sem, grad, grad_out)
    b(8)
    period(7)
    other_chunk(9, h1a, qkv, h1b, dzb, 1)

    def small_copy(step, src, peer):
        return pltpu.make_async_remote_copy(
            src_ref=src, dst_ref=small_in.at[step], send_sem=small_send.at[step], recv_sem=small_recv.at[step],
            device_id=peer, device_id_type=MESH,
        )

    own_peers = (core_peer, x_peer, y_peer)

    def small_next(step):
        small_copy(step, small_tot.at[step], own_peers[step]).wait_recv()
        small_tot[step + 1] = small_tot[step] + small_in[step]
        if step + 1 < 3:
            small_copy(step + 1, small_tot.at[step + 1], own_peers[step + 1]).start()
        else:

            @pl.when(end)
            def _():
                small_copy(3, small_tot.at[3], inward).start()

    def small_middle():
        @pl.when(middle)
        def _():
            small_copy(3, small_tot.at[3], inward).wait_recv()
            small_tot[4] = small_tot[3] + small_in[3]
            small_copy(4, small_tot.at[4], across).start()

    def small_last():
        @pl.when(middle)
        def _():
            small_copy(4, small_tot.at[4], across).wait_recv()
            small_tot[5] = small_tot[4] + small_in[4]
            small_copy(5, small_tot.at[5], outward).start()
            sums_out[...] = small_tot[5]

    small_tot[0] = sums[...]
    small_copy(0, small_tot.at[0], own_peers[0]).start()
    b(9)
    period(8)
    small_next(0)
    other_chunk(10, h1a, qkv, h1b, dzb, 2)
    b(10)
    period(9)
    small_next(1)
    period(10)
    small_next(2)
    period(11)
    small_middle()
    period(12)
    small_last()
    period(13)
    period(14)
    period(15)

    @pl.when(end)
    def _():
        small_copy(5, small_tot.at[5], outward).wait_recv()
        sums_out[...] = small_in[5]

    for i in range(chunks):
        Chunk(i).finish()
    for step in range(3):
        small_copy(step, small_tot.at[step], own_peers[step]).wait_send()

    @pl.when(end)
    def _():
        small_copy(3, small_tot.at[3], inward).wait_send()

    @pl.when(middle)
    def _():
        small_copy(4, small_tot.at[4], across).wait_send()
        small_copy(5, small_tot.at[5], outward).wait_send()

    for copy in copies:
        copy.wait()


def fetch(copies, src, dst, sem):
    copy = pltpu.make_async_copy(src, dst, sem)
    copy.start()
    copies.append(copy)
    return copy


def second_kernel(
    x_in, cot_in, block, mask_in, wqkv_in, wout_in, wfc_in, wproj_in,
    act_out, grad_out, sums, h1_out, dz_out, o_out, da_out, h2_out, du_out, f_out,
    x, cot, mask, wqkv, wout, wfc, wproj, h1, qkv, probs, o, x1, h2, slope, f, x2, dh, do, da, act, in_sem, out_sem,
):
    loads = []
    for src, dst in (
        (x_in, x), (mask_in, mask), (wqkv_in, wqkv), (wout_in, wout), (wfc_in, wfc), (wproj_in, wproj), (cot_in, cot)
    ):
        fetch(loads, src, dst, in_sem.at[len(loads)])
    x_here, mask_here, qkv_here, out_here, fc_here, proj_here, cot_here = loads
    waits = {"small": x_here, "qkv": qkv_here, "out": out_here, "fc": fc_here, "proj": proj_here}
    copies = []
    mask_here.wait()
    forward_layer(
        x, block, (wqkv, wout, wfc, wproj), mask, (h1, qkv, probs, o, x1, h2, slope, f), x2,
        lambda name: waits[name].wait(),
    )
    for src, dst in ((h1, h1_out), (o, o_out), (h2, h2_out), (f, f_out)):
        store(copies, out_sem, src, dst)
    act[...] = x2[...].astype(bf16)
    store(copies, out_sem, act, act_out)
    cot_here.wait()
    sums[...] = jnp.zeros_like(sums)
    backward_layer(
        x, cot, cot, block, (wqkv, wout, wfc, wproj), (qkv, probs, x1, slope), (dh, do, da), x2, sums,
        lambda name: store(copies, out_sem, *{"du": (slope, du_out), "da": (da, da_out), "dz": (qkv, dz_out)}[name]),
    )
    store(copies, out_sem, x2, grad_out)
    for copy in copies:
        copy.wait()


VMEM_BYTES = 62 * 2**20


def spec(shape, dtype):
    return jax.ShapeDtypeStruct(shape, dtype)


def kernels_body(*args):
    tokens, doc, cotangent = args[:3]
    gain1, shift1, sqkv, bq, bv, sout, bo, gain2, shift2, sfc, bfc, sproj, bp = args[3:]
    count, width = tokens.shape
    ff = sfc.shape[1]
    owners = lax.axis_size("own")
    me = lax.axis_index("own")
    rows = [gain1, shift1, bq, bv, bo, gain2, shift2, bp]
    stacked = jnp.tile(jnp.stack(rows), (1, owners))
    mine = lax.broadcasted_iota(jnp.int32, stacked.shape, 1) // gain1.shape[0] == me
    stacked = jnp.where(mine, stacked, jnp.zeros_like(stacked))
    tiled = jnp.tile(bfc, owners)
    mine = lax.broadcasted_iota(jnp.int32, tiled.shape, 0) // bfc.shape[0] == me
    tiled = jnp.where(mine, tiled, jnp.zeros_like(tiled)).reshape(ff // width, width)
    packed = jnp.concatenate([stacked, tiled, jnp.zeros((16 - 8 - ff // width, width), bf16)])

    hbm = pl.BlockSpec(memory_space=pl.ANY)
    vmem = pl.BlockSpec(memory_space=pltpu.VMEM)
    V = pltpu.VMEM
    half = count // 2
    x_s = ((count, width), f32)
    low_s = ((count, width), bf16)
    qkv_s = ((count, 3 * width), bf16)
    ff_s = ((count, ff), bf16)
    probs_s = ((HEADS // 4 * half, 4 * (count + half)), bf16)
    mask_s = ((half, count + half), f32)
    block_s = ((16, width), f32)
    w_s = [((width, 3 * width), bf16), ((width, width), bf16), ((width, ff), bf16), ((ff, width), bf16)]
    units = 3 + 1 + ff // width + 3
    dma = pltpu.SemaphoreType.DMA

    def call(kernel, inputs, outs, scratch, in_specs, out_specs, **params):
        return pl.pallas_call(
            kernel,
            out_shape=[spec(*s) for s in outs],
            in_specs=in_specs,
            out_specs=out_specs,
            scratch_shapes=scratch,
            compiler_params=pltpu.CompilerParams(vmem_limit_bytes=VMEM_BYTES, **params),
        )(*inputs)

    outs = [x_s, block_s, mask_s, *w_s, low_s, qkv_s, probs_s, low_s, x_s, low_s, ff_s, ff_s]
    (x2, block, mask, wqkv, wout, wfc, wproj, h1a, qkva, probsa, oa, x1a, h2a, slopea, fa) = call(
        first_kernel,
        (tokens, doc.reshape(1, count), packed, sqkv, sout, sfc, sproj),
        outs,
        [V(*s) for s in w_s]
        + [V(*s) for s in (block_s, mask_s, low_s, qkv_s, probs_s, low_s, x_s, low_s, ff_s, ff_s, x_s)]
        + [V((8, 16, width), bf16)]
        + [dma((units, 6)), dma((units, 6)), dma((units, 7)), dma((units, 7)), dma((units,)), dma((7,)), dma((7,))]
        + [dma((len(outs),))],
        [vmem] * 3 + [hbm] * 4,
        [hbm] * len(outs),
        collective_id=0,
        has_side_effects=True,
    )
    outs = [low_s, x_s, block_s, low_s, qkv_s, low_s, low_s, low_s, ff_s, ff_s]
    act, grad, sumsb, h1b, dzb, ob, dab, h2b, dub, fb = call(
        second_kernel,
        (x2, cotangent, block, mask, wqkv, wout, wfc, wproj),
        outs,
        [V(*s) for s in (x_s, low_s, mask_s, *w_s, low_s, qkv_s, probs_s, low_s, x_s, low_s, ff_s, ff_s, x_s, x_s)]
        + [V(*s) for s in (low_s, low_s, low_s)]
        + [dma((7,)), dma((9,))],
        [hbm, hbm, vmem, hbm, hbm, hbm, hbm, hbm],
        [hbm, hbm, vmem] + [hbm] * 7,
    )
    shard = sqkv.shape[0]
    third = sproj.shape[0] // 3
    tiles = 1 + 3 + ff // width

    half_rows = [((3, 2, 2, third // 2, width), bf16), ((tiles, 2, 2, shard // 2, width), bf16)]
    half_rows2 = [((3, 2, third // 2, width), bf16), ((tiles, 2, shard // 2, width), bf16)]
    blocks = [((3, third, width), bf16), ((tiles, shard, width), bf16)]
    outs = [x_s, block_s, *[(s.shape, bf16) for s in (sqkv, sout, sfc, sproj)]]
    scratch = [low_s, low_s, x_s, ((4, width, width), bf16), low_s, qkv_s, low_s, x_s, low_s, ff_s]
    scratch += [((2 * count, ff), bf16)]
    scratch += [low_s, qkv_s, low_s, low_s, low_s, ff_s, low_s, x_s, low_s, low_s, block_s]
    scratch += [((2, 2, 2, 2, third, width), bf16), ((2, 2, 2, 2, shard, width), bf16)]
    scratch += [((3, 2, 2, third, width), bf16), ((tiles, 2, 2, shard, width), bf16)]
    scratch += half_rows + half_rows2 + blocks * 3
    scratch += [((6, 16, width), f32), ((6, 16, width), f32)]
    tokens_grad, sums, *grads = call(
        third_kernel,
        (
            tokens, cotangent, grad, block, wqkv, wout, wfc, wproj, h1a, qkva, probsa, oa, x1a, h2a, slopea, fa,
            sumsb, h1b, dzb, ob, dab, h2b, dub, fb,
        ),
        outs,
        [V(*s) for s in scratch]
        + [dma((18,)), dma((4,)), dma((12,)), dma((tiles + 3, 8)), dma((tiles + 3, 8)), dma((6,)), dma((6,))],
        [hbm, hbm, hbm, vmem] + [hbm] * 12 + [vmem] + [hbm] * 7,
        [hbm, vmem] + [hbm] * 4,
        collective_id=1,
        has_side_effects=True,
    )
    final = [g.astype(f32) for g in grads]

    def own(row):
        return lax.dynamic_slice(sums, (row, me * gain1.shape[0]), (1, gain1.shape[0]))[0]

    bfc_grad = lax.dynamic_slice(
        sums[BIAS_FC : BIAS_FC + ff // width].reshape(ff), (me * bfc.shape[0],), (bfc.shape[0],)
    )
    return (
        act, tokens_grad, own(GAIN1), own(SHIFT1), final[0], own(BIAS_Q), own(BIAS_V), final[1], own(BIAS_OUT),
        own(GAIN2), own(SHIFT2), final[2], bfc_grad, final[3], own(BIAS_PROJ),
    )


def as_sent(shard):
    return jax.tree.map(lambda a: a.astype(jnp.bfloat16) if a.dtype == jnp.float32 else a, shard)


def normalize(x, gain, shift):
    centre = x - jnp.mean(x, axis=-1, keepdims=True)
    spread = jnp.mean(centre * centre, axis=-1, keepdims=True)
    return centre * lax.rsqrt(spread + EPSILON) * gain + shift


def smooth(inner):
    return jax.nn.gelu(inner, approximate=True)


def visible(doc):
    count = doc.shape[0]
    row = lax.broadcasted_iota(jnp.int32, (count, count), 0)
    col = lax.broadcasted_iota(jnp.int32, (count, count), 1)
    same = doc[:, None] == doc[None, :]
    return same & (col <= row) & ((doc[None, :] != 0) | (row == col))


def plain_forward(x, weights, mask):
    (
        gain_one,
        shift_one,
        w_qkv,
        bias_query,
        bias_value,
        w_out,
        bias_out,
        gain_two,
        shift_two,
        w_fc,
        bias_fc,
        w_proj,
        bias_proj,
    ) = weights
    width = w_qkv.shape[0]
    count = x.shape[0]
    scale = HEAD_DIM ** (-0.5)
    f32 = jnp.float32
    h_one = normalize(x, gain_one.astype(f32), shift_one.astype(f32)).astype(jnp.bfloat16)
    qkv_bias = jnp.concatenate(
        [bias_query.astype(f32), jnp.zeros((width,), f32), bias_value.astype(f32)]
    )
    packed = (jnp.dot(h_one, w_qkv, preferred_element_type=f32) + qkv_bias).astype(jnp.bfloat16)
    query = packed[:, :width].reshape(count, HEADS, HEAD_DIM)
    key = packed[:, width : 2 * width].reshape(count, HEADS, HEAD_DIM)
    value = packed[:, 2 * width :].reshape(count, HEADS, HEAD_DIM)
    scores = jnp.einsum("thd,shd->hts", query, key, preferred_element_type=f32) * scale
    scores = jnp.where(mask[None], scores, -1e30)
    probs = jax.nn.softmax(scores, axis=-1)
    probs_low = probs.astype(jnp.bfloat16)
    mixed = jnp.einsum("hts,shd->thd", probs_low, value, preferred_element_type=f32)
    mixed = mixed.reshape(count, width).astype(jnp.bfloat16)
    middle = x + (jnp.dot(mixed, w_out, preferred_element_type=f32) + bias_out.astype(f32))
    h_two = normalize(middle, gain_two.astype(f32), shift_two.astype(f32)).astype(jnp.bfloat16)
    inner = jnp.dot(h_two, w_fc, preferred_element_type=f32) + bias_fc.astype(f32)
    active = smooth(inner).astype(jnp.bfloat16)
    result = middle + (jnp.dot(active, w_proj, preferred_element_type=f32) + bias_proj.astype(f32))
    kept = (h_one, query, key, value, probs, probs_low, mixed, middle, h_two, inner, active)
    return (result, kept)


def plain_backward(x, weights, mask, grad):
    (
        gain_one,
        shift_one,
        w_qkv,
        bias_query,
        bias_value,
        w_out,
        bias_out,
        gain_two,
        shift_two,
        w_fc,
        bias_fc,
        w_proj,
        bias_proj,
    ) = weights
    result, kept = plain_forward(x, weights, mask)
    h_one, query, key, value, probs, probs_low, mixed, middle, h_two, inner, active = kept
    width = w_qkv.shape[0]
    count = x.shape[0]
    scale = HEAD_DIM ** (-0.5)
    f32 = jnp.float32
    grad_branch = grad.astype(jnp.bfloat16)
    g_wproj = jnp.einsum("tf,td->fd", active, grad_branch, preferred_element_type=f32)
    g_bproj = jnp.sum(grad_branch.astype(f32), axis=0)
    d_active = jnp.einsum("td,fd->tf", grad_branch, w_proj, preferred_element_type=f32)
    unused, pull_smooth = jax.vjp(smooth, inner)
    d_inner = pull_smooth(d_active)[0].astype(jnp.bfloat16)
    g_wfc = jnp.einsum("td,tf->df", h_two, d_inner, preferred_element_type=f32)
    g_bfc = jnp.sum(d_inner.astype(f32), axis=0)
    d_htwo = jnp.einsum("tf,df->td", d_inner, w_fc, preferred_element_type=f32)
    unused, pull_two = jax.vjp(normalize, middle, gain_two.astype(f32), shift_two.astype(f32))
    d_mid, g_gain2, g_shift2 = pull_two(d_htwo)
    d_middle = grad + d_mid
    d_attn = d_middle.astype(jnp.bfloat16)
    g_wout = jnp.einsum("td,te->de", mixed, d_attn, preferred_element_type=f32)
    g_bout = jnp.sum(d_attn.astype(f32), axis=0)
    d_mixed = jnp.einsum("te,de->td", d_attn, w_out, preferred_element_type=f32).astype(
        jnp.bfloat16
    )
    d_mixed = d_mixed.reshape(count, HEADS, HEAD_DIM)
    d_probs = jnp.einsum("thd,shd->hts", d_mixed, value, preferred_element_type=f32)
    d_value = jnp.einsum("hts,thd->shd", probs_low, d_mixed, preferred_element_type=f32)
    d_scores = probs * (d_probs - jnp.sum(d_probs * probs, axis=-1, keepdims=True))
    d_scores = d_scores.astype(jnp.bfloat16)
    d_query = jnp.einsum("hts,shd->thd", d_scores, key, preferred_element_type=f32) * scale
    d_key = jnp.einsum("hts,thd->shd", d_scores, query, preferred_element_type=f32) * scale
    d_packed = jnp.concatenate(
        [d_query.reshape(count, width), d_key.reshape(count, width), d_value.reshape(count, width)],
        axis=1,
    ).astype(jnp.bfloat16)
    g_wqkv = jnp.einsum("td,te->de", h_one, d_packed, preferred_element_type=f32)
    column_sums = jnp.sum(d_packed.astype(f32), axis=0)
    g_bquery = column_sums[:width]
    g_bvalue = column_sums[2 * width :]
    d_hone = jnp.einsum("te,de->td", d_packed, w_qkv, preferred_element_type=f32)
    unused, pull_one = jax.vjp(normalize, x, gain_one.astype(f32), shift_one.astype(f32))
    d_input, g_gain1, g_shift1 = pull_one(d_hone)
    terms = (
        g_gain1,
        g_shift1,
        g_wqkv,
        g_bquery,
        g_bvalue,
        g_wout,
        g_bout,
        g_gain2,
        g_shift2,
        g_wfc,
        g_bfc,
        g_wproj,
        g_bproj,
    )
    return (d_middle + d_input, terms)


def plain_body(
    tokens,
    doc_ids,
    cotangent,
    norm1_gain,
    norm1_shift,
    qkv_weight,
    query_bias,
    value_bias,
    out_weight,
    out_bias,
    norm2_gain,
    norm2_shift,
    fc_weight,
    fc_bias,
    proj_weight,
    proj_bias,
):
    shards = (
        norm1_gain,
        norm1_shift,
        qkv_weight,
        query_bias,
        value_bias,
        out_weight,
        out_bias,
        norm2_gain,
        norm2_shift,
        fc_weight,
        fc_bias,
        proj_weight,
        proj_bias,
    )
    mask = visible(doc_ids)

    def fetch():
        return (
            lax.all_gather(shards[0], "own", axis=0, tiled=True),
            lax.all_gather(shards[1], "own", axis=0, tiled=True),
            lax.all_gather(shards[2], "own", axis=0, tiled=True),
            lax.all_gather(shards[3], "own", axis=0, tiled=True),
            lax.all_gather(shards[4], "own", axis=0, tiled=True),
            lax.all_gather(shards[5], "own", axis=0, tiled=True),
            lax.all_gather(shards[6], "own", axis=0, tiled=True),
            lax.all_gather(shards[7], "own", axis=0, tiled=True),
            lax.all_gather(shards[8], "own", axis=0, tiled=True),
            lax.all_gather(shards[9], "own", axis=0, tiled=True),
            lax.all_gather(shards[10], "own", axis=0, tiled=True),
            lax.all_gather(shards[11], "own", axis=0, tiled=True),
            lax.all_gather(shards[12], "own", axis=0, tiled=True),
        )

    current = tokens.astype(jnp.float32)
    saved = []
    for use in range(USES):
        saved.append(current)
        current, kept = plain_forward(current, fetch(), mask)
    grad = cotangent.astype(jnp.float32)
    summed = None
    for use in reversed(range(USES)):
        grad, terms = plain_backward(saved[use], fetch(), mask, grad)
        if summed is None:
            summed = terms
        else:
            summed = tuple((first + second for first, second in zip(summed, terms)))
    owned = (
        lax.psum_scatter(summed[0], "own", scatter_dimension=0, tiled=True),
        lax.psum_scatter(summed[1], "own", scatter_dimension=0, tiled=True),
        lax.psum_scatter(summed[2], "own", scatter_dimension=0, tiled=True),
        lax.psum_scatter(summed[3], "own", scatter_dimension=0, tiled=True),
        lax.psum_scatter(summed[4], "own", scatter_dimension=0, tiled=True),
        lax.psum_scatter(summed[5], "own", scatter_dimension=0, tiled=True),
        lax.psum_scatter(summed[6], "own", scatter_dimension=0, tiled=True),
        lax.psum_scatter(summed[7], "own", scatter_dimension=0, tiled=True),
        lax.psum_scatter(summed[8], "own", scatter_dimension=0, tiled=True),
        lax.psum_scatter(summed[9], "own", scatter_dimension=0, tiled=True),
        lax.psum_scatter(summed[10], "own", scatter_dimension=0, tiled=True),
        lax.psum_scatter(summed[11], "own", scatter_dimension=0, tiled=True),
        lax.psum_scatter(summed[12], "own", scatter_dimension=0, tiled=True),
    )
    final = jax.tree.map(lambda part: part.astype(jnp.float32), lax.psum(as_sent(owned), "grp"))
    return (current.astype(jnp.bfloat16), grad) + tuple(final)


def solution(mesh):
    return jax.shard_map(
        kernels_body if tuple(mesh.axis_sizes) == (4, 8) else plain_body,
        mesh=mesh,
        in_specs=(
            P(("grp", "own"), None),
            P(("grp", "own")),
            P(("grp", "own"), None),
            P("own"),
            P("own"),
            P("own", None),
            P("own"),
            P("own"),
            P("own", None),
            P("own"),
            P("own"),
            P("own"),
            P("own", None),
            P("own"),
            P("own", None),
            P("own"),
        ),
        out_specs=(
            P(("grp", "own"), None),
            P(("grp", "own"), None),
            P("own"),
            P("own"),
            P("own", None),
            P("own"),
            P("own"),
            P("own", None),
            P("own"),
            P("own"),
            P("own"),
            P("own", None),
            P("own"),
            P("own", None),
            P("own"),
        ),
        check_vma=False,
    )
```

```python
import functools

import jax
import jax.numpy as jnp
from jax import lax
from jax.experimental import pallas as pl
from jax.experimental.pallas import tpu as pltpu
from jax.sharding import PartitionSpec as P

HEADS = 12
HEAD_DIM = 64
USES = 2
EPSILON = 1e-05
SCALE = HEAD_DIM ** (-0.5)
TANH_SCALE = 0.7978845608028654
TANH_CUBIC = 0.044715
MESH = pl.DeviceIdType.MESH
f32 = jnp.float32
bf16 = jnp.bfloat16

GAIN1, SHIFT1, BIAS_Q, BIAS_V, BIAS_OUT, GAIN2, SHIFT2, BIAS_PROJ, BIAS_FC = range(9)


def dot(a, b, ca=1, cb=0):
    return lax.dot_general(a, b, (((ca,), (cb,)), ((), ())), preferred_element_type=f32)


def loop(count, body):
    def step(i, carry):
        body(i)
        return carry

    lax.fori_loop(0, count, step, 0)


def span(begin, end, body):
    def step(i, carry):
        body(i)
        return carry

    lax.fori_loop(begin, end, step, 0)


def part(i, size):
    return pl.ds(pl.multiple_of(i * size, size), size)


def centred(x):
    centre = x - jnp.mean(x, axis=-1, keepdims=True)
    spread = jnp.mean(centre * centre, axis=-1, keepdims=True)
    return centre, lax.rsqrt(spread + EPSILON)


def norm_forward(x, gain, shift, h):
    rows = 128

    def step(i):
        centre, r = centred(x[part(i, rows), :].astype(f32))
        h[part(i, rows), :] = (centre * r * gain + shift).astype(bf16)

    loop(x.shape[0] // rows, step)


def norm_backward(x, dh, gain, grad, out, sums, gain_row, shift_row, low=None):
    rows = 128

    def step(i):
        centre, r = centred(x[part(i, rows), :].astype(f32))
        n = centre * r
        d = dh[part(i, rows), :]
        sums[gain_row : gain_row + 1, :] += jnp.sum(d * n, axis=0, keepdims=True)
        sums[shift_row : shift_row + 1, :] += jnp.sum(d, axis=0, keepdims=True)
        e = d * gain
        inner = e - jnp.mean(e, axis=-1, keepdims=True) - n * jnp.mean(e * n, axis=-1, keepdims=True)
        result = grad[part(i, rows), :].astype(f32) + r * inner
        out[part(i, rows), :] = result
        if low is not None:
            low[part(i, rows), :] = result.astype(bf16)

    loop(x.shape[0] // rows, step)


def column_sum(x):
    return jnp.sum(x.astype(f32), axis=0, keepdims=True)


def make_mask(doc, mask):
    count = doc.shape[1]
    half = count // 2
    ids = doc[0:1, :].astype(f32)
    keys = jnp.broadcast_to(ids, (128, count)).T[:, :1]
    for k0, q0, place in ((0, 0, 0), (half, half, count)):
        width = count - q0
        row = lax.broadcasted_iota(jnp.int32, (half, width), 0) + k0
        col = lax.broadcasted_iota(jnp.int32, (half, width), 1) + q0
        key = keys[k0 : k0 + half]
        same = (key == ids[:, q0:]) & (row <= col) & ((key != 0.0) | (row == col))
        mask[:, place : place + width] = jnp.where(same, 0.0, -1e30)


def head_lanes(h, x):
    lane = lax.broadcasted_iota(jnp.int32, (1, 2 * HEAD_DIM), 1)
    keep = (lane < HEAD_DIM) if h == 0 else (lane >= HEAD_DIM)
    return jnp.where(keep, x, jnp.zeros_like(x))


def attention_forward(qkv, mask, probs, o, begin=0, end=6, shift=0):
    count, width = o.shape
    half = count // 2
    pair = 2 * HEAD_DIM

    def step(i):
        col = part(i, pair)
        q = qkv[:, col]
        k = qkv[:, pl.ds(pl.multiple_of(width + i * pair, pair), pair)]
        v = qkv[:, pl.ds(pl.multiple_of(2 * width + i * pair, pair), pair)]
        vt = v.T
        outs = []
        for h in range(2):
            kh = head_lanes(h, k)
            s0 = dot(kh[:half], q, 1, 1) + mask[:, :count]
            s1 = dot(kh[half:], q[half:], 1, 1) + mask[:, count:]
            m0 = jnp.max(s0, axis=0, keepdims=True)
            m1 = jnp.max(s1, axis=0, keepdims=True)
            top = jnp.concatenate([m0[:, :half], jnp.maximum(m0[:, half:], m1)], axis=1)
            e0 = jnp.exp(s0 - top)
            e1 = jnp.exp(s1 - top[:, half:])
            l0 = jnp.sum(e0, axis=0, keepdims=True)
            l1 = jnp.sum(e1, axis=0, keepdims=True)
            r = 1.0 / jnp.concatenate([l0[:, :half], l0[:, half:] + l1], axis=1)
            p0 = (e0 * r).astype(bf16)
            p1 = (e1 * r[:, half:]).astype(bf16)
            row = pl.ds(h * half, half)
            probs[i - shift, row, :count] = p0
            probs[i - shift, row, count:] = p1
            vh = vt[h * HEAD_DIM : (h + 1) * HEAD_DIM]
            first = dot(vh[:, :half], p0)
            second = dot(vh[:, half:], p1)
            outs.append(jnp.concatenate([first[:, :half], first[:, half:] + second], axis=1))
        o[:, col] = jnp.concatenate(outs, axis=0).astype(bf16).T

    span(begin, end, step)


def attention_backward(qkv, probs, do, dz, sums, begin=0, end=6, shift=0):
    count, width = do.shape
    half = count // 2
    pair = 2 * HEAD_DIM

    def step(i):
        cq = part(i, pair)
        ck = pl.ds(pl.multiple_of(width + i * pair, pair), pair)
        cv = pl.ds(pl.multiple_of(2 * width + i * pair, pair), pair)
        q, k, v, d = qkv[:, cq], qkv[:, ck], qkv[:, cv], do[:, cq]
        dq = dk = dv = None
        for h in range(2):
            dh, kh, qh = head_lanes(h, d), head_lanes(h, k), head_lanes(h, q)
            row = pl.ds(h * half, half)
            p0 = probs[i - shift, row, :count]
            p1 = probs[i - shift, row, count:]
            d0 = dot(v[:half], dh, 1, 1)
            d1 = dot(v[half:], dh[half:], 1, 1)
            w0 = p0.astype(f32)
            w1 = p1.astype(f32)
            t0 = jnp.sum(d0 * w0, axis=0, keepdims=True)
            t1 = jnp.sum(d1 * w1, axis=0, keepdims=True)
            t = jnp.concatenate([t0[:, :half], t0[:, half:] + t1], axis=1)
            s0 = (w0 * (d0 - t)).astype(bf16)
            s1 = (w1 * (d1 - t[:, half:])).astype(bf16)
            v_term = jnp.concatenate([dot(p0, dh), dot(p1, dh[half:])], axis=0)
            k_term = jnp.concatenate([dot(s0, qh), dot(s1, qh[half:])], axis=0)
            qa = dot(s0, kh[:half], 0, 0)
            qb = dot(s1, kh[half:], 0, 0)
            q_term = jnp.concatenate([qa[:half], qa[half:] + qb], axis=0)
            dq = q_term if dq is None else dq + q_term
            dk = k_term if dk is None else dk + k_term
            dv = v_term if dv is None else dv + v_term
        dq = (dq * SCALE).astype(bf16)
        dv = dv.astype(bf16)
        dz[:, cq] = dq
        dz[:, ck] = dk.astype(bf16)
        dz[:, cv] = dv
        sums[BIAS_Q : BIAS_Q + 1, cq] += column_sum(dq)
        sums[BIAS_V : BIAS_V + 1, cq] += column_sum(dv)

    span(begin, end, step)


def small(block, row):
    return block[row : row + 1, :]


def hidden_tile(h2, weight, bias, f, slope, i):
    count, width = h2.shape
    rows = 128
    third = f.shape[2] // 8
    for first in range(0, count, rows):
        these = pl.ds(first, rows)
        u = dot(h2[these, :], weight) + bias
        square = u * u
        t = jnp.tanh(u * (TANH_SCALE + (TANH_SCALE * TANH_CUBIC) * square))
        rise = 0.5 + 0.5 * t
        active = (u * rise).astype(bf16)
        for place in range(width // third):
            owner = i * (width // third // 3) + place // 3
            f[place % 3, these, part(owner, third)] = active[:, place * third : (place + 1) * third]
        inner = TANH_SCALE + (3.0 * TANH_SCALE * TANH_CUBIC) * square
        slope[these, part(i, width)] = (rise + (0.5 * u) * (1.0 - t * t) * inner).astype(bf16)


def hidden_forward(h2, wfc, block, f, slope, begin, end):
    width = h2.shape[1]

    def hidden(i):
        hidden_tile(h2, wfc[:, part(i, width)], block[pl.ds(BIAS_FC + i, 1), :], f, slope, i)

    span(begin, end, hidden)


def project(f, wproj, i):
    third = f.shape[2] // 8
    rows = [wproj[pl.ds((owner * 3 + i) * third, third), :] for owner in range(8)]
    return dot(f[i], jnp.concatenate(rows, axis=0))


def coords():
    own = lax.axis_index("own")
    return lax.axis_index("grp"), own // 2, lax.rem(own, 2)


class Unit:
    def __init__(self, shard, full, row, rows, col, cols, shared=True):
        self.shard, self.full, self.shared = shard, full, shared
        self.row, self.rows, self.col, self.cols = row, rows, col, cols

    def mine(self, half=None):
        rows = self.rows if half is None else self.rows // 2
        start = self.row + (0 if half is None else half * rows)
        return self.shard.at[pl.ds(start, rows), pl.ds(self.col, self.cols)]

    def block(self, owner, half=None):
        rows = self.rows if half is None else self.rows // 2
        start = owner * self.shard.shape[0] + self.row + (0 if half is None else half * rows)
        return self.full.at[pl.ds(pl.multiple_of(start, 16), rows), pl.ds(self.col, self.cols)]


PIECES = [(1, 0), (1, 1), (2, 0), (2, 1), (3, 0), (3, 1)]


class Gather:
    def __init__(self, units, link_send, link_recv, core_send, core_recv, own_sem):
        self.units = units
        self.link_send, self.link_recv = link_send, link_recv
        self.core_send, self.core_recv, self.own_sem = core_send, core_recv, own_sem
        self.grp, self.chip, self.core = coords()
        self.odd = lax.rem(self.grp, 2)
        self.sent = []

    def owner(self, offset):
        return jnp.bitwise_xor(self.chip, offset) * 2 + self.core

    def device(self, chip_offset, along_z=False):
        own = jnp.bitwise_xor(self.chip, chip_offset) * 2 + self.core
        grp = self.grp + 1 - 2 * self.odd if along_z else self.grp
        return (grp, own)

    def link(self, k, src, dst, piece, out, device):
        return pltpu.make_async_remote_copy(
            src_ref=src,
            dst_ref=dst,
            send_sem=self.link_send.at[k, out],
            recv_sem=self.link_recv.at[k, piece],
            device_id=device,
            device_id_type=MESH,
        )

    def across(self, k, src, dst, slot):
        return pltpu.make_async_remote_copy(
            src_ref=src,
            dst_ref=dst,
            send_sem=self.core_send.at[k, slot],
            recv_sem=self.core_recv.at[k, slot],
            device_id=(self.grp, self.chip * 2 + 1 - self.core),
            device_id_type=MESH,
        )

    def own(self, k):
        unit = self.units[k]
        return pltpu.make_async_copy(unit.mine(), unit.block(self.owner(0)), self.own_sem.at[k])

    def first(self, k, offset, half, out):
        unit = self.units[k]
        piece = PIECES.index((offset, half))
        return self.link(
            k, unit.mine(half), unit.block(self.owner(0), half), piece, out, self.device(offset)
        )

    def relay(self, k, offset, half, way, out):
        unit = self.units[k]
        piece = unit.block(self.owner(offset), half)
        return self.link(k, piece, piece, PIECES.index((3, half)), out, self.device(way))

    def pair(self, k, offset, half, out):
        unit = self.units[k]
        piece = unit.block(self.owner(offset), half)
        return self.link(k, piece, piece, PIECES.index((offset, half)), out, self.device(0, True))

    def hand(self, k, offset, half):
        unit = self.units[k]
        piece = unit.block(self.owner(offset), half)
        return self.across(k, piece, piece, PIECES.index((offset, half)))

    def arrived(self, k, offset, half):
        unit = self.units[k]
        piece = unit.block(self.owner(offset), half)
        self.link(k, piece, piece, PIECES.index((offset, half)), 0, self.device(1)).wait_recv()

    def sends(self, k, odd):
        own = [(1, 0), (2, 1), (1, 1), (2, 0)]
        if not self.units[k].shared:
            own = [(2, 0), (1, 1), (1, 0), (2, 1)]
        elif odd:
            own = [(1, 1), (2, 0)]
        calls = [functools.partial(self.first, k, *what) for what in own]
        if odd or not self.units[k].shared:
            calls += [functools.partial(self.relay, k, *what) for what in ((2, 0, 1), (1, 1, 2))]
        if self.units[k].shared:
            pairs = ((3, 0), (3, 1)) if odd else ((1, 0), (2, 1))
            calls += [functools.partial(self.pair, k, *what) for what in pairs]
        return len(own), [functools.partial(call, out) for out, call in enumerate(calls)]

    def each_kind(self, k, body):
        if not self.units[k].shared:
            body(True)
            return

        @pl.when(self.odd == 0)
        def _():
            body(False)

        @pl.when(self.odd == 1)
        def _():
            body(True)

    def start(self, k):
        def body(odd):
            own, calls = self.sends(k, odd)
            for call in calls[:own]:
                call().start()

        self.each_kind(k, body)
        unit = self.units[k]
        self.across(k, unit.mine(), unit.block(self.owner(0)), len(PIECES)).start()
        self.own(k).start()

    def serve(self, k, odd, pieces, then):
        for piece in pieces:
            self.arrived(k, *piece)
            if piece in then:
                then[piece]().start()
            self.hand(k, *piece).start()

    def serve_first(self, k):
        def body(odd):
            own, calls = self.sends(k, odd)
            if odd:
                then = {(2, 0): calls[own], (1, 1): calls[own + 1]}
                self.serve(k, odd, ((2, 0), (1, 1)), then)
            else:
                then = {(1, 0): calls[own], (2, 1): calls[own + 1]}
                self.serve(k, odd, ((1, 0), (2, 1), (1, 1), (2, 0)), then)

        self.each_kind(k, body)

    def serve_second(self, k):
        def body(odd):
            own, calls = self.sends(k, odd)
            if not self.units[k].shared:
                self.serve(k, odd, ((1, 0), (2, 1), (3, 0), (3, 1)), {})
            elif odd:
                then = {(3, 0): calls[own + 2], (3, 1): calls[own + 3]}
                self.serve(k, odd, ((3, 0), (3, 1), (1, 0), (2, 1)), then)
            else:
                self.serve(k, odd, ((3, 0), (3, 1)), {})

        self.each_kind(k, body)

    def finish(self, k):
        unit = self.units[k]
        other = 1 - 2 * self.core
        self.own(k).wait()
        whole = unit.block(self.owner(0) + other)
        self.across(k, whole, whole, len(PIECES)).wait_recv()
        for slot, (offset, half) in enumerate(PIECES):
            piece = unit.block(self.owner(offset) + other, half)
            self.across(k, piece, piece, slot).wait_recv()

    def drain(self, k):
        def body(odd):
            own, calls = self.sends(k, odd)
            for call in calls:
                call().wait_send()

        self.each_kind(k, body)
        unit = self.units[k]
        self.across(k, unit.mine(), unit.block(self.owner(0)), len(PIECES)).wait_send()
        for offset, half in PIECES:
            self.hand(k, offset, half).wait_send()


def store(copies, sem, src, dst):
    copy = pltpu.make_async_copy(src, dst, sem.at[len(copies)])
    copy.start()
    copies.append(copy)


def first_kernel(
    tokens, doc, packed, sqkv, sout, sfc, sproj,
    x2_out, block_out, mask_out, w_out,
    h1_out, qkv_out, probs_out, o_out, x1_out, h2_out, slope_out, f_out,
    wqkv, wout, wfc, wproj, block, mask, h1, qkv, probs, o, x1, h2, slope, f, x2, many,
    link_send, link_recv, core_send, core_recv, own_sem, small_send, small_recv, out_sem,
):
    grp, chip, core = coords()
    me = chip * 2 + core
    width = tokens.shape[1]
    barrier = pltpu.get_barrier_semaphore()
    peers = [(grp, jnp.bitwise_xor(me, j)) for j in range(1, 8)]
    peers.append((grp + 1 - 2 * lax.rem(grp, 2), me))
    for peer in peers:
        pl.semaphore_signal(barrier, inc=1, device_id=peer, device_id_type=MESH)
    pl.semaphore_wait(barrier, len(peers))

    units = [Unit(sqkv, wqkv, 0, sqkv.shape[0], i * width, width) for i in range(3)]
    units += [Unit(sout, wout, 0, sout.shape[0], 0, width)]
    units += [Unit(sfc, wfc, 0, sfc.shape[0], i * width, width) for i in range(sfc.shape[1] // width)]
    thirds = sproj.shape[0] // 3
    units += [Unit(sproj, wproj, i * thirds, thirds, 0, width, i == 0) for i in range(3)]
    gather = Gather(units, link_send, link_recv, core_send, core_recv, own_sem)
    count = len(units)

    def small_copy(j, slot):
        return pltpu.make_async_remote_copy(
            src_ref=packed,
            dst_ref=many.at[slot],
            send_sem=small_send.at[j - 1],
            recv_sem=small_recv.at[j - 1],
            device_id=(grp, jnp.bitwise_xor(me, j)),
            device_id_type=MESH,
        )

    for j in range(1, 8):
        small_copy(j, j).start()
    gather.start(0)
    gather.start(1)
    copies = []

    def slot(s):
        if s < count:
            gather.serve_first(s)
        if s + 2 < count:
            gather.start(s + 2)
        if 0 <= s - 2 < count:
            gather.serve_second(s - 2)
        if 0 <= s - 3 < count:
            gather.finish(s - 3)

    make_mask(doc, mask)
    store(copies, out_sem, mask, mask_out)
    slot(0)
    total = packed[...].astype(f32)
    for j in range(1, 8):
        small_copy(j, j).wait_recv()
        total = total + many[j].astype(f32)
    block[...] = total
    store(copies, out_sem, block, block_out)
    slot(1)
    norm_forward(tokens, small(block, GAIN1), small(block, SHIFT1), h1)
    store(copies, out_sem, h1, h1_out)
    slot(2)
    slot(3)
    qkv[:, :width] = (dot(h1[...], wqkv[:, :width]) + small(block, BIAS_Q)).astype(bf16) * SCALE
    slot(4)
    qkv[:, width : 2 * width] = dot(h1[...], wqkv[:, width : 2 * width]).astype(bf16)
    slot(5)
    for i in range(3):
        store(copies, out_sem, wqkv.at[:, pl.ds(i * width, width)], w_out.at[i])
    qkv[:, 2 * width :] = (dot(h1[...], wqkv[:, 2 * width :]) + small(block, BIAS_V)).astype(bf16)
    store(copies, out_sem, qkv, qkv_out)
    attention_forward(qkv, mask, probs, o, 0, 1)
    slot(6)
    store(copies, out_sem, wout, w_out.at[3])
    attention_forward(qkv, mask, probs, o, 1, 3)
    slot(7)
    attention_forward(qkv, mask, probs, o, 3, 5)
    slot(8)
    attention_forward(qkv, mask, probs, o, 5, 6)
    store(copies, out_sem, probs, probs_out)
    store(copies, out_sem, o, o_out)
    x1[...] = tokens[...].astype(f32) + (dot(o[...], wout[...]) + small(block, BIAS_OUT))
    norm_forward(x1, small(block, GAIN2), small(block, SHIFT2), h2)
    store(copies, out_sem, x1, x1_out)
    store(copies, out_sem, h2, h2_out)
    slot(9)
    hidden_forward(h2, wfc, block, f, slope, 0, 2)
    slot(10)
    fc_tiles = wfc.shape[1] // width
    for i in range(fc_tiles):
        store(copies, out_sem, wfc.at[:, pl.ds(i * width, width)], w_out.at[4 + i])
    hidden_forward(h2, wfc, block, f, slope, 2, 4)
    store(copies, out_sem, f, f_out)
    store(copies, out_sem, slope, slope_out)

    slot(11)
    x2[...] = x1[...] + (project(f, wproj, 0) + small(block, BIAS_PROJ))
    slot(12)
    x2[...] += project(f, wproj, 1)
    slot(13)
    for i in range(fc_tiles):
        store(copies, out_sem, wproj.at[pl.ds(i * width, width), :], w_out.at[4 + fc_tiles + i])
    x2[...] += project(f, wproj, 2)
    store(copies, out_sem, x2, x2_out)
    for k in range(count):
        gather.drain(k)
    for j in range(1, 8):
        small_copy(j, j).wait_send()
    for copy in copies:
        copy.wait()


def second_kernel(
    x2_in, tokens_in, cot_in, mask_in, block, w_in, w_parts_in, w_thirds_in,
    h1a_in, qkv_in, probs_in, oa_in, x1_in, h2a_in, slope_in, fa_in,
    act_out, grad_out, sums_out, gqkv_out, gout_out, gfc_out, gproj_out,
    x, tokens, cot, grad, x1, dh, tiles, h1a, qkv, oa, h2a, slope, h1b, dzb, ob, h2b, dub, shared, more_probs,
    gm, da, dab, sums,
    buf_p, buf_o, recv_p, recv_o, hop1_p, hop1_o, hop2_p, hop2_o, zmid_p, zmid_o, tot_p, tot_o,
    small_in, small_tot,
    in_sem, tile_sem, out_sem, send, recv, small_send, small_recv,
):
    grp, chip, core = coords()
    yy, xx = chip // 2, lax.rem(chip, 2)
    me = chip * 2 + core
    width = x.shape[1]
    loads = {}

    def load(name, src, dst):
        copy = pltpu.make_async_copy(src, dst, in_sem.at[len(loads)])
        copy.start()
        loads[name] = copy

    fb, fa = shared.at[pl.ds(0, 3)], shared.at[pl.ds(3, 3)]
    probs = shared.at[:, :, pl.ds(0, probs_in.shape[2])]
    some_probs = shared.at[pl.ds(3, 3), :, pl.ds(0, probs_in.shape[2])]
    half = x.shape[0] // 2
    mask = dh.at[pl.ds(0, half), :]
    load("x", x2_in, x)

    ff_tiles = w_in.shape[0] - 8
    ring = tiles.shape[0]
    fc_at, proj_at = 4, 4 + ff_tiles
    order = [proj_at + t for t in range(ff_tiles)] + [fc_at + t for t in range(ff_tiles)] + [3, 0, 1, 2]

    def tile_copy(t):
        return pltpu.make_async_copy(w_in.at[order[t]], tiles.at[t % ring], tile_sem.at[t % ring])

    def tile(t):
        tile_copy(t).wait()
        return tiles[t % ring]

    def next_tile(t):
        if t + ring < len(order):
            tile_copy(t + ring).start()

    def square(value):
        return value.reshape(width, width)

    def resident(t):
        if t < 2:
            return square(buf_o[t])
        if t < 4:
            return jnp.concatenate(
                [buf_p[t - 2, 0].reshape(-1, width), buf_p[t - 2, 1, 0].reshape(-1, width)], axis=0
            )
        return square(recv_o[2 * (t - 4) : 2 * (t - 4) + 2])

    for t in range(2):
        load(f"w{t}", w_parts_in.at[t], buf_o.at[t])
    load("w2", w_thirds_in.at[2, pl.ds(0, 2)], buf_p.at[0, 0])
    load("w2b", w_thirds_in.at[2, 2], buf_p.at[0, 1, 0])
    load("mask", mask_in, mask)
    load("w3", w_thirds_in.at[3, pl.ds(0, 2)], buf_p.at[1, 0])
    load("w3b", w_thirds_in.at[3, 2], buf_p.at[1, 1, 0])
    for t in range(ff_tiles):
        load(f"w{fc_at + t}", w_parts_in.at[fc_at + t], recv_o.at[pl.ds(2 * t, 2)])
    for t in range(ring):
        tile_copy(t).start()
    core_peer = (grp, jnp.bitwise_xor(me, 1))
    x_peer = (grp, jnp.bitwise_xor(me, 2))
    y_peer = (grp, jnp.bitwise_xor(me, 4))
    low = grp == 1
    middle = (grp == 1) | (grp == 2)
    end = jnp.logical_not(middle)
    inward = (jnp.where(grp == 0, 1, 2), me)
    outward = (jnp.where(low, 0, 3), me)
    across = (jnp.where(low, 2, 1), me)

    barrier = pltpu.get_barrier_semaphore()

    def greet():
        for peer in (core_peer, x_peer, y_peer):
            pl.semaphore_signal(barrier, inc=1, device_id=peer, device_id_type=MESH)

        @pl.when(end)
        def _():
            pl.semaphore_signal(barrier, inc=1, device_id=inward, device_id_type=MESH)

        @pl.when(middle)
        def _():
            pl.semaphore_signal(barrier, inc=1, device_id=outward, device_id_type=MESH)
            pl.semaphore_signal(barrier, inc=1, device_id=across, device_id_type=MESH)

    def remote(src, dst, i, stage, peer):
        return pltpu.make_async_remote_copy(
            src_ref=src, dst_ref=dst, send_sem=send.at[i, stage], recv_sem=recv.at[i, stage],
            device_id=peer, device_id_type=MESH,
        )

    third_width = width // 3
    specs = [(True, 0, 0, width // 2), (True, 0, width // 2, width // 2), (True, 1, 0, width), (True, 2, 0, width)]
    projs = len(specs)
    specs += [(False, j, 0, width) for j in range(ff_tiles + 3)]
    specs += [(False, ff_tiles + 3, 0, 2 * third_width), (False, ff_tiles + 3, 2 * third_width, third_width)]
    chunks = len(specs)
    copies = []

    buffers = (
        (buf_p, buf_o), (recv_p, recv_o), (hop1_p, hop1_o), (hop2_p, hop2_o), (zmid_p, zmid_o),
        (tot_p, tot_o),
    )

    class Chunk:
        def __init__(self, i):
            self.i = i
            self.proj, self.at, col, self.width = specs[i]
            cols = pl.ds(col, self.width)
            sets = [pair[0 if self.proj else 1] for pair in buffers]
            ring = sets[0].shape[0]
            order = i if self.proj else i - projs
            self.previous = i - ring if order >= ring else None
            self.last = i + ring >= (projs if self.proj else chunks)
            self.rows = sets[1].shape[3]
            self.buf = sets[0].at[order % ring, :, :, :, :, cols]
            self.recv = sets[1].at[self.at, :, :, :, cols]
            self.hop1 = sets[2].at[self.at, :, :, :, cols]
            self.hop2, self.zmid, self.tot = (
                s.at[self.at, :, :, cols] if len(s.shape) == 4 else s.at[self.at, :, cols] for s in sets[3:]
            )
            half = self.rows // 2
            self.top, self.bottom = pl.ds(0, half), pl.ds(half, half)
            self.cols = cols

        def to_core(self):
            return remote(self.buf.at[1 - core], self.recv, self.i, 0, core_peer)

        def first(self):
            return (
                remote(self.recv.at[:, 1 - xx, self.top, :], self.hop1.at[0], self.i, 1, x_peer),
                remote(self.recv.at[1 - yy, :, self.bottom, :], self.hop1.at[1], self.i, 2, y_peer),
            )

        def second(self):
            return (
                remote(self.recv.at[1 - yy, xx, self.top, :], self.hop2.at[0], self.i, 3, y_peer),
                remote(self.recv.at[yy, 1 - xx, self.bottom, :], self.hop2.at[1], self.i, 4, x_peer),
            )

        def to_middle(self):
            return remote(self.recv.at[yy, xx], self.tot, self.i, 5, inward)

        def between(self):
            return remote(self.recv.at[yy, xx], self.zmid, self.i, 6, across)

        def to_end(self):
            return remote(self.tot, self.tot, self.i, 7, outward)

        def begin(self):
            if self.previous is not None:
                Chunk(self.previous).to_core().wait_send()

        def stage_b(self):
            self.to_core().wait_recv()
            self.recv[...] = self.recv[...] + self.buf[core]
            for copy in self.first():
                copy.start()

        def stage_c(self):
            for copy in self.first():
                copy.wait_recv()
            self.recv[:, xx, self.top, :] = self.recv[:, xx, self.top, :] + self.hop1[0]
            self.recv[yy, :, self.bottom, :] = self.recv[yy, :, self.bottom, :] + self.hop1[1]
            for copy in self.second():
                copy.start()

        def stage_d(self):
            for copy in self.second():
                copy.wait_recv()
            self.recv[yy, xx, self.top, :] = self.recv[yy, xx, self.top, :] + self.hop2[0]
            self.recv[yy, xx, self.bottom, :] = self.recv[yy, xx, self.bottom, :] + self.hop2[1]

            @pl.when(end)
            def _():
                self.to_middle().start()

        def stage_e(self):
            @pl.when(middle)
            def _():
                self.to_middle().wait_recv()
                self.recv[yy, xx] = self.recv[yy, xx] + self.tot[...]
                self.between().start()

        def stage_f(self):
            @pl.when(middle)
            def _():
                self.between().wait_recv()
                self.tot[...] = self.recv[yy, xx] + self.zmid[...]
                self.to_end().start()

        def stage_g(self):
            @pl.when(end)
            def _():
                self.to_end().wait_recv()

            if self.proj:
                place = gproj_out.at[pl.ds(self.at * self.rows, self.rows), self.cols]
            elif self.at < ff_tiles:
                place = gfc_out.at[:, pl.ds(self.at * width, width)]
            elif self.at == ff_tiles:
                place = gout_out
            else:
                place = gqkv_out.at[:, pl.ds((self.at - ff_tiles - 1) * width + specs[self.i][2], self.width)]
            store(copies, out_sem, self.tot, place)

        def finish(self):
            if self.last:
                self.to_core().wait_send()
            for copy in self.first() + self.second():
                copy.wait_send()

            @pl.when(end)
            def _():
                self.to_middle().wait_send()

            @pl.when(middle)
            def _():
                self.between().wait_send()
                self.to_end().wait_send()

    def made(i):
        Chunk(i).to_core().start()

    def proj_chunk(i):
        chunk = Chunk(i)
        chunk.begin()
        rows = chunk.rows
        yb, ya = cot[:, chunk.cols], gm[:, chunk.cols]
        for owner in range(8):
            col = pl.ds(owner * rows, rows)
            value = dot(fb[chunk.at, :, col], yb, 0, 0) + dot(fa[chunk.at, :, col], ya, 0, 0)
            chunk.buf[owner % 2, owner // 4, (owner // 2) % 2] = value.astype(bf16)
        made(i)

    def other_chunk(i, xa, ya, xb, yb, col):
        chunk = Chunk(i)
        chunk.begin()
        cols = pl.ds(col, chunk.width)
        rows = chunk.rows
        for first in (0, 4):
            these = pl.ds(first * rows, 4 * rows)
            value = dot(xa[:, these], ya[:, cols], 0, 0) + dot(xb[:, these], yb[:, cols], 0, 0)
            for at in range(4):
                owner = first + at
                piece = value[at * rows : (at + 1) * rows].astype(bf16)
                chunk.buf[owner % 2, owner // 4, (owner // 2) % 2] = piece
        made(i)

    def b(i):
        Chunk(i).stage_b()

    def period(k):
        if k < chunks:
            Chunk(k).stage_c()
        if 2 <= k + 2 < chunks:
            b(k + 2)
        for lag, name in ((1, "stage_d"), (2, "stage_e"), (3, "stage_f"), (5, "stage_g")):
            if 0 <= k - lag < chunks:
                getattr(Chunk(k - lag), name)()

    sums[...] = jnp.zeros_like(sums)
    loads["x"].wait()
    norm_forward(x, small(block, GAIN1), small(block, SHIFT1), h1b)
    for name in ("w0", "w1", "w2", "w2b"):
        loads[name].wait()
    for t, (bias, scale) in enumerate(((small(block, BIAS_Q), SCALE), (None, None), (small(block, BIAS_V), None))):
        z = dot(h1b[...], resident(t))
        z = z if bias is None else z + bias
        z = z.astype(bf16)
        dzb[:, t * width : (t + 1) * width] = z if scale is None else z * scale
    loads["mask"].wait()
    attention_forward(dzb, mask, some_probs, ob, 0, 3)
    load("cot", cot_in, cot)
    for name, src, dst in (
        ("h2a", h2a_in, h2a), ("slope", slope_in, slope), ("qkv", qkv_in, qkv), ("oa", oa_in, oa), ("h1a", h1a_in, h1a),
        ("tokens", tokens_in, tokens),
    ):
        load(name, src, dst)
    attention_forward(dzb, mask, more_probs, ob, 3, 6, 3)
    loads["w3"].wait()
    loads["w3b"].wait()
    for first in range(0, x.shape[0], 128):
        these = pl.ds(first, 128)
        x1[these, :] = x[these, :] + (dot(ob[these, :], resident(3)) + small(block, BIAS_OUT))
    norm_forward(x1, small(block, GAIN2), small(block, SHIFT2), h2b)
    for t in range(ff_tiles):
        loads[f"w{fc_at + t}"].wait()
    for t in range(ff_tiles):
        hidden_tile(h2b, resident(fc_at + t), block[BIAS_FC + t : BIAS_FC + t + 1, :], fb, dub, t)
    third = fb.shape[2] // 8

    def hidden_rows(t):
        owners = width // (3 * third)
        pieces = [
            fb[j, :, pl.ds((t * owners + owner) * third, third)] for owner in range(owners) for j in range(3)
        ]
        return jnp.concatenate(pieces, axis=1)

    for t in range(ff_tiles):
        tile_copy(t).wait()
    dh[...] = dot(hidden_rows(0), tiles[0])
    for t in range(1, ff_tiles):
        dh[...] += dot(hidden_rows(t), tiles[t])
    for first in range(0, x.shape[0], 128):
        these = pl.ds(first, 128)
        gm[these, :] = (x1[these, :] + (dh[these, :] + small(block, BIAS_PROJ))).astype(bf16)
    store(copies, out_sem, gm, act_out)

    def hidden_backward(g, held, t):
        cols = pl.ds(t * width, width)
        d = (dot(g[...], tiles[t], 1, 1) * held[:, cols].astype(f32)).astype(bf16)
        held[:, cols] = d
        sums[BIAS_FC + t : BIAS_FC + t + 1, :] += column_sum(d)

    def input_gradient(held, weights):
        dh[...] = dot(held[:, :width], weights[0](), 1, 1)
        for t in range(1, len(weights)):
            dh[...] += dot(held[:, t * width : (t + 1) * width], weights[t](), 1, 1)

    def residents(first, number):
        return [functools.partial(resident, first + t) for t in range(number)]

    def streamed(first, number):
        return [functools.partial(tile, first + t) for t in range(number)]

    loads["cot"].wait()
    sums[BIAS_PROJ : BIAS_PROJ + 1, :] += column_sum(cot[...])
    for t in range(ff_tiles):
        hidden_backward(cot, dub, t)
    input_gradient(dub, residents(fc_at, ff_tiles))
    greet()
    norm_backward(x1, dh, small(block, GAIN2), cot, grad, sums, GAIN2, SHIFT2, dab)
    load("x1", x1_in, x1)
    da[...] = dot(dab[...], resident(3), 1, 1).astype(bf16)
    sums[BIAS_OUT : BIAS_OUT + 1, :] += column_sum(dab[...])
    attention_backward(dzb, some_probs, da, dzb, sums, 0, 3)
    load("fa", fa_in, fa)
    attention_backward(dzb, more_probs, da, dzb, sums, 3, 6, 3)
    input_gradient(dzb, residents(0, 3))
    norm_backward(x, dh, small(block, GAIN1), grad, grad, sums, GAIN1, SHIFT1)

    copies[0].wait()
    gm[...] = grad[...].astype(bf16)

    @pl.when(end)
    def _():
        pl.semaphore_wait(barrier, 4)

    @pl.when(middle)
    def _():
        pl.semaphore_wait(barrier, 5)

    loads["fa"].wait()
    proj_chunk(0)
    proj_chunk(1)
    b(0)
    proj_chunk(2)
    b(1)
    loads["slope"].wait()
    hidden_backward(gm, slope, 0)
    next_tile(0)
    period(0)
    proj_chunk(3)
    load("probs", probs_in, probs)
    sums[BIAS_PROJ : BIAS_PROJ + 1, :] += column_sum(gm[...])
    hidden_backward(gm, slope, 1)
    next_tile(1)
    period(1)
    for t in range(2, ff_tiles):
        hidden_backward(gm, slope, t)
        next_tile(t)
    n = ff_tiles

    def fc_chunk(t):
        other_chunk(projs + t, h2a, slope, h2b, dub, t * width)

    loads["h2a"].wait()
    fc_chunk(0)
    period(2)
    input_gradient(slope, streamed(n, ff_tiles))
    for t in range(ff_tiles):
        next_tile(n + t)
    n += ff_tiles
    fc_chunk(1)
    period(3)
    loads["x1"].wait()
    norm_backward(x1, dh, small(block, GAIN2), grad, grad, sums, GAIN2, SHIFT2, da)
    do = cot
    do[...] = dot(da[...], tile(n), 1, 1).astype(bf16)
    n += 1
    sums[BIAS_OUT : BIAS_OUT + 1, :] += column_sum(da[...])
    fc_chunk(2)
    period(4)
    loads["qkv"].wait()
    loads["probs"].wait()
    attention_backward(qkv, probs, do, qkv, sums, 0, 2)
    fc_chunk(3)
    period(5)
    attention_backward(qkv, probs, do, qkv, sums, 2, 4)
    loads["oa"].wait()
    other_chunk(8, oa, da, ob, dab, 0)
    period(6)
    attention_backward(qkv, probs, do, qkv, sums, 4, 6)
    loads["h1a"].wait()
    other_chunk(9, h1a, qkv, h1b, dzb, 0)
    period(7)
    input_gradient(qkv, streamed(n, 3))
    other_chunk(10, h1a, qkv, h1b, dzb, width)
    period(8)
    loads["tokens"].wait()
    norm_backward(tokens, dh, small(block, GAIN1), grad, grad, sums, GAIN1, SHIFT1)
    store(copies, out_sem, grad, grad_out)
    other_chunk(11, h1a, qkv, h1b, dzb, 2 * width)

    def small_copy(step, src, peer):
        return pltpu.make_async_remote_copy(
            src_ref=src, dst_ref=small_in.at[step], send_sem=small_send.at[step], recv_sem=small_recv.at[step],
            device_id=peer, device_id_type=MESH,
        )

    own_peers = (core_peer, x_peer, y_peer)

    def small_next(step):
        small_copy(step, small_tot.at[step], own_peers[step]).wait_recv()
        small_tot[step + 1] = small_tot[step] + small_in[step]
        if step + 1 < 3:
            small_copy(step + 1, small_tot.at[step + 1], own_peers[step + 1]).start()
        else:

            @pl.when(end)
            def _():
                small_copy(3, small_tot.at[3], inward).start()

    def small_middle():
        @pl.when(middle)
        def _():
            small_copy(3, small_tot.at[3], inward).wait_recv()
            small_tot[4] = small_tot[3] + small_in[3]
            small_copy(4, small_tot.at[4], across).start()

    def small_last():
        @pl.when(middle)
        def _():
            small_copy(4, small_tot.at[4], across).wait_recv()
            small_tot[5] = small_tot[4] + small_in[4]
            small_copy(5, small_tot.at[5], outward).start()
            sums_out[...] = small_tot[5]

    small_tot[0] = sums[...]
    small_copy(0, small_tot.at[0], own_peers[0]).start()
    period(9)
    other_chunk(12, h1a, qkv, h1b, dzb, 2 * width + 2 * third_width)
    small_next(0)
    period(10)
    small_next(1)
    period(11)
    small_next(2)
    period(12)
    small_middle()
    period(13)
    small_last()
    for k in range(14, chunks + 5):
        period(k)

    @pl.when(end)
    def _():
        small_copy(5, small_tot.at[5], outward).wait_recv()
        sums_out[...] = small_in[5]

    for i in range(chunks):
        Chunk(i).finish()
    for step in range(3):
        small_copy(step, small_tot.at[step], own_peers[step]).wait_send()

    @pl.when(end)
    def _():
        small_copy(3, small_tot.at[3], inward).wait_send()

    @pl.when(middle)
    def _():
        small_copy(4, small_tot.at[4], across).wait_send()
        small_copy(5, small_tot.at[5], outward).wait_send()

    for copy in copies[1:]:
        copy.wait()


def last_kernel(
    act, tokens_grad, sums, gqkv, gout, gfc, gproj,
    act_out, tokens_grad_out, gqkv_out, gout_out, gfc_out, gproj_out,
    g1, s1, gbq, gbv, gbo, g2, s2, gbp, gbfc,
    lqkv, lout, lfc, lproj, fqkv, fout, ffc, fproj, in_sem, out_sem,
):
    lows = (lqkv, lout, lfc, lproj)
    loads = [
        pltpu.make_async_copy(src, dst, in_sem.at[i]) for i, (src, dst) in enumerate(zip((gqkv, gout, gfc, gproj), lows))
    ]
    for i in (3, 2, 0, 1):
        loads[i].start()
    copies = []
    store(copies, out_sem, tokens_grad, tokens_grad_out)
    store(copies, out_sem, act, act_out)
    wides = ((fqkv, gqkv_out), (fout, gout_out), (ffc, gfc_out), (fproj, gproj_out))
    for i in (3, 2, 0, 1):
        loads[i].wait()
        wide, place = wides[i]
        wide[...] = lows[i][...].astype(f32)
        store(copies, out_sem, wide, place)
    owners = lax.axis_size("own")
    me = lax.axis_index("own")
    size, ff_size = g1.shape[0], gbfc.shape[0]
    across = sums.shape[1] // ff_size
    mine = jnp.zeros((8, size), f32)
    mine_ff = jnp.zeros((1, ff_size), f32)
    for owner in range(owners):
        here = me == owner
        mine = jnp.where(here, sums[:8, owner * size : (owner + 1) * size], mine)
        row, col = BIAS_FC + owner // across, owner % across * ff_size
        mine_ff = jnp.where(here, sums[row : row + 1, col : col + ff_size], mine_ff)
    for row, place in enumerate((g1, s1, gbq, gbv, gbo, g2, s2, gbp)):
        place[...] = mine[row]
    gbfc[...] = mine_ff[0]
    for copy in copies:
        copy.wait()


VMEM_BYTES = 65_200 * 1024


def spec(shape, dtype):
    return jax.ShapeDtypeStruct(shape, dtype)


def kernels_body(*args):
    tokens, doc, cotangent = args[:3]
    gain1, shift1, sqkv, bq, bv, sout, bo, gain2, shift2, sfc, bfc, sproj, bp = args[3:]
    count, width = tokens.shape
    ff = sfc.shape[1]
    owners = lax.axis_size("own")
    me = lax.axis_index("own")
    rows = [gain1, shift1, bq, bv, bo, gain2, shift2, bp]
    stacked = jnp.tile(jnp.stack(rows), (1, owners))
    mine = lax.broadcasted_iota(jnp.int32, stacked.shape, 1) // gain1.shape[0] == me
    stacked = jnp.where(mine, stacked, jnp.zeros_like(stacked))
    tiled = jnp.tile(bfc, owners)
    mine = lax.broadcasted_iota(jnp.int32, tiled.shape, 0) // bfc.shape[0] == me
    tiled = jnp.where(mine, tiled, jnp.zeros_like(tiled)).reshape(ff // width, width)
    packed = jnp.concatenate([stacked, tiled, jnp.zeros((16 - 8 - ff // width, width), bf16)])

    hbm = pl.BlockSpec(memory_space=pl.ANY)
    vmem = pl.BlockSpec(memory_space=pltpu.VMEM)
    V = pltpu.VMEM
    half = count // 2
    x_s = ((count, width), f32)
    low_s = ((count, width), bf16)
    qkv_s = ((count, 3 * width), bf16)
    ff_s = ((count, ff), bf16)
    probs_s = ((HEADS // 2, count, count + half), bf16)
    f_s = ((3, count, 8 * (sproj.shape[0] // 3)), bf16)
    mask_s = ((half, count + half), f32)
    block_s = ((16, width), f32)
    w_s = [((width, 3 * width), bf16), ((width, width), bf16), ((width, ff), bf16), ((ff, width), bf16)]
    units = 3 + 1 + ff // width + 3
    dma = pltpu.SemaphoreType.DMA

    def call(kernel, inputs, outs, scratch, in_specs, out_specs, **params):
        return pl.pallas_call(
            kernel,
            out_shape=[spec(*s) for s in outs],
            in_specs=in_specs,
            out_specs=out_specs,
            scratch_shapes=scratch,
            compiler_params=pltpu.CompilerParams(vmem_limit_bytes=VMEM_BYTES, **params),
        )(*inputs)

    w_all = ((4 + 2 * (ff // width), width, width), bf16)
    outs = [x_s, block_s, mask_s, w_all, low_s, qkv_s, probs_s, low_s, x_s, low_s, ff_s, f_s]
    (x2, block, mask, w, h1a, qkva, probsa, oa, x1a, h2a, slopea, fa) = call(
        first_kernel,
        (tokens, doc.reshape(1, count), packed, sqkv, sout, sfc, sproj),
        outs,
        [V(*s) for s in w_s]
        + [V(*s) for s in (block_s, mask_s, low_s, qkv_s, probs_s, low_s, x_s, low_s, ff_s, f_s, x_s)]
        + [V((8, 16, width), bf16)]
        + [dma((units, 6)), dma((units, 6)), dma((units, 7)), dma((units, 7)), dma((units,)), dma((7,)), dma((7,))]
        + [dma((len(outs) + 11,))],
        [vmem] * 3 + [hbm] * 4,
        [hbm] * len(outs),
        collective_id=0,
        has_side_effects=True,
    )
    shard = sqkv.shape[0]
    third = sproj.shape[0] // 3
    tiles = 1 + 3 + ff // width

    half_rows = [((3, 2, 2, third // 2, width), bf16), ((tiles, 2, 2, shard // 2, width), bf16)]
    half_rows2 = [((3, 2, third // 2, width), bf16), ((tiles, 2, shard // 2, width), bf16)]
    blocks = [((3, third, width), bf16), ((tiles, shard, width), bf16)]
    outs = [low_s, x_s, block_s, *[(s.shape, bf16) for s in (sqkv, sout, sfc, sproj)]]
    scratch = [x_s, low_s, low_s, x_s, x_s, x_s, ((4, width, width), bf16), low_s, qkv_s, low_s, low_s, ff_s]
    scratch += [low_s, qkv_s, low_s, low_s, ff_s, ((2 * f_s[0][0], *f_s[0][1:]), bf16)]
    scratch += [((HEADS // 4, count, count + half), bf16), low_s, low_s, low_s, block_s]
    scratch += [((2, 2, 2, 2, third, width), bf16), ((2, 2, 2, 2, shard, width), bf16)]
    scratch += [((3, 2, 2, third, width), bf16), ((tiles, 2, 2, shard, width), bf16)]
    scratch += half_rows + half_rows2 + blocks * 2
    scratch += [((6, 16, width), f32), ((6, 16, width), f32)]
    act, tokens_grad, sums, *grads = call(
        second_kernel,
        (
            x2, tokens, cotangent, mask, block, w, w.reshape(-1, 2, 2, 2, shard, width),
            w.reshape(-1, 3, 2, third, width),
            h1a, qkva, probsa, oa, x1a, h2a, slopea, fa,
        ),
        outs,
        [V(*s) for s in scratch]
        + [dma((24,)), dma((4,)), dma((16,)), dma((13, 8)), dma((13, 8)), dma((6,)), dma((6,))],
        [hbm] * 4 + [vmem] + [hbm] * 11,
        [hbm, hbm, vmem] + [hbm] * 4,
        collective_id=1,
        has_side_effects=True,
    )
    shards = [(s.shape, f32) for s in (sqkv, sout, sfc, sproj)]
    vectors = [(gain1.shape, f32)] * 8 + [(bfc.shape, f32)]
    act, tokens_grad, gqkv, gout, gfc, gproj, *small_grads = call(
        last_kernel,
        (act, tokens_grad, sums, *grads),
        [low_s, x_s, *shards, *vectors],
        [V(s.shape, bf16) for s in (sqkv, sout, sfc, sproj)] + [V(*s) for s in shards] + [dma((4,)), dma((6,))],
        [hbm, hbm, vmem] + [hbm] * 4,
        [hbm] * 6 + [vmem] * 9,
    )
    g1, s1, gbq, gbv, gbo, g2, s2, gbp, gbfc = small_grads
    return act, tokens_grad, g1, s1, gqkv, gbq, gbv, gout, gbo, g2, s2, gfc, gbfc, gproj, gbp


def as_sent(shard):
    return jax.tree.map(lambda a: a.astype(jnp.bfloat16) if a.dtype == jnp.float32 else a, shard)


def normalize(x, gain, shift):
    centre = x - jnp.mean(x, axis=-1, keepdims=True)
    spread = jnp.mean(centre * centre, axis=-1, keepdims=True)
    return centre * lax.rsqrt(spread + EPSILON) * gain + shift


def smooth(inner):
    return jax.nn.gelu(inner, approximate=True)


def visible(doc):
    count = doc.shape[0]
    row = lax.broadcasted_iota(jnp.int32, (count, count), 0)
    col = lax.broadcasted_iota(jnp.int32, (count, count), 1)
    same = doc[:, None] == doc[None, :]
    return same & (col <= row) & ((doc[None, :] != 0) | (row == col))


def plain_forward(x, weights, mask):
    (
        gain_one,
        shift_one,
        w_qkv,
        bias_query,
        bias_value,
        w_out,
        bias_out,
        gain_two,
        shift_two,
        w_fc,
        bias_fc,
        w_proj,
        bias_proj,
    ) = weights
    width = w_qkv.shape[0]
    count = x.shape[0]
    scale = HEAD_DIM ** (-0.5)
    f32 = jnp.float32
    h_one = normalize(x, gain_one.astype(f32), shift_one.astype(f32)).astype(jnp.bfloat16)
    qkv_bias = jnp.concatenate(
        [bias_query.astype(f32), jnp.zeros((width,), f32), bias_value.astype(f32)]
    )
    packed = (jnp.dot(h_one, w_qkv, preferred_element_type=f32) + qkv_bias).astype(jnp.bfloat16)
    query = packed[:, :width].reshape(count, HEADS, HEAD_DIM)
    key = packed[:, width : 2 * width].reshape(count, HEADS, HEAD_DIM)
    value = packed[:, 2 * width :].reshape(count, HEADS, HEAD_DIM)
    scores = jnp.einsum("thd,shd->hts", query, key, preferred_element_type=f32) * scale
    scores = jnp.where(mask[None], scores, -1e30)
    probs = jax.nn.softmax(scores, axis=-1)
    probs_low = probs.astype(jnp.bfloat16)
    mixed = jnp.einsum("hts,shd->thd", probs_low, value, preferred_element_type=f32)
    mixed = mixed.reshape(count, width).astype(jnp.bfloat16)
    middle = x + (jnp.dot(mixed, w_out, preferred_element_type=f32) + bias_out.astype(f32))
    h_two = normalize(middle, gain_two.astype(f32), shift_two.astype(f32)).astype(jnp.bfloat16)
    inner = jnp.dot(h_two, w_fc, preferred_element_type=f32) + bias_fc.astype(f32)
    active = smooth(inner).astype(jnp.bfloat16)
    result = middle + (jnp.dot(active, w_proj, preferred_element_type=f32) + bias_proj.astype(f32))
    kept = (h_one, query, key, value, probs, probs_low, mixed, middle, h_two, inner, active)
    return (result, kept)


def plain_backward(x, weights, mask, grad):
    (
        gain_one,
        shift_one,
        w_qkv,
        bias_query,
        bias_value,
        w_out,
        bias_out,
        gain_two,
        shift_two,
        w_fc,
        bias_fc,
        w_proj,
        bias_proj,
    ) = weights
    result, kept = plain_forward(x, weights, mask)
    h_one, query, key, value, probs, probs_low, mixed, middle, h_two, inner, active = kept
    width = w_qkv.shape[0]
    count = x.shape[0]
    scale = HEAD_DIM ** (-0.5)
    f32 = jnp.float32
    grad_branch = grad.astype(jnp.bfloat16)
    g_wproj = jnp.einsum("tf,td->fd", active, grad_branch, preferred_element_type=f32)
    g_bproj = jnp.sum(grad_branch.astype(f32), axis=0)
    d_active = jnp.einsum("td,fd->tf", grad_branch, w_proj, preferred_element_type=f32)
    unused, pull_smooth = jax.vjp(smooth, inner)
    d_inner = pull_smooth(d_active)[0].astype(jnp.bfloat16)
    g_wfc = jnp.einsum("td,tf->df", h_two, d_inner, preferred_element_type=f32)
    g_bfc = jnp.sum(d_inner.astype(f32), axis=0)
    d_htwo = jnp.einsum("tf,df->td", d_inner, w_fc, preferred_element_type=f32)
    unused, pull_two = jax.vjp(normalize, middle, gain_two.astype(f32), shift_two.astype(f32))
    d_mid, g_gain2, g_shift2 = pull_two(d_htwo)
    d_middle = grad + d_mid
    d_attn = d_middle.astype(jnp.bfloat16)
    g_wout = jnp.einsum("td,te->de", mixed, d_attn, preferred_element_type=f32)
    g_bout = jnp.sum(d_attn.astype(f32), axis=0)
    d_mixed = jnp.einsum("te,de->td", d_attn, w_out, preferred_element_type=f32).astype(
        jnp.bfloat16
    )
    d_mixed = d_mixed.reshape(count, HEADS, HEAD_DIM)
    d_probs = jnp.einsum("thd,shd->hts", d_mixed, value, preferred_element_type=f32)
    d_value = jnp.einsum("hts,thd->shd", probs_low, d_mixed, preferred_element_type=f32)
    d_scores = probs * (d_probs - jnp.sum(d_probs * probs, axis=-1, keepdims=True))
    d_scores = d_scores.astype(jnp.bfloat16)
    d_query = jnp.einsum("hts,shd->thd", d_scores, key, preferred_element_type=f32) * scale
    d_key = jnp.einsum("hts,thd->shd", d_scores, query, preferred_element_type=f32) * scale
    d_packed = jnp.concatenate(
        [d_query.reshape(count, width), d_key.reshape(count, width), d_value.reshape(count, width)],
        axis=1,
    ).astype(jnp.bfloat16)
    g_wqkv = jnp.einsum("td,te->de", h_one, d_packed, preferred_element_type=f32)
    column_sums = jnp.sum(d_packed.astype(f32), axis=0)
    g_bquery = column_sums[:width]
    g_bvalue = column_sums[2 * width :]
    d_hone = jnp.einsum("te,de->td", d_packed, w_qkv, preferred_element_type=f32)
    unused, pull_one = jax.vjp(normalize, x, gain_one.astype(f32), shift_one.astype(f32))
    d_input, g_gain1, g_shift1 = pull_one(d_hone)
    terms = (
        g_gain1,
        g_shift1,
        g_wqkv,
        g_bquery,
        g_bvalue,
        g_wout,
        g_bout,
        g_gain2,
        g_shift2,
        g_wfc,
        g_bfc,
        g_wproj,
        g_bproj,
    )
    return (d_middle + d_input, terms)


def plain_body(
    tokens,
    doc_ids,
    cotangent,
    norm1_gain,
    norm1_shift,
    qkv_weight,
    query_bias,
    value_bias,
    out_weight,
    out_bias,
    norm2_gain,
    norm2_shift,
    fc_weight,
    fc_bias,
    proj_weight,
    proj_bias,
):
    shards = (
        norm1_gain,
        norm1_shift,
        qkv_weight,
        query_bias,
        value_bias,
        out_weight,
        out_bias,
        norm2_gain,
        norm2_shift,
        fc_weight,
        fc_bias,
        proj_weight,
        proj_bias,
    )
    mask = visible(doc_ids)

    def fetch():
        return (
            lax.all_gather(shards[0], "own", axis=0, tiled=True),
            lax.all_gather(shards[1], "own", axis=0, tiled=True),
            lax.all_gather(shards[2], "own", axis=0, tiled=True),
            lax.all_gather(shards[3], "own", axis=0, tiled=True),
            lax.all_gather(shards[4], "own", axis=0, tiled=True),
            lax.all_gather(shards[5], "own", axis=0, tiled=True),
            lax.all_gather(shards[6], "own", axis=0, tiled=True),
            lax.all_gather(shards[7], "own", axis=0, tiled=True),
            lax.all_gather(shards[8], "own", axis=0, tiled=True),
            lax.all_gather(shards[9], "own", axis=0, tiled=True),
            lax.all_gather(shards[10], "own", axis=0, tiled=True),
            lax.all_gather(shards[11], "own", axis=0, tiled=True),
            lax.all_gather(shards[12], "own", axis=0, tiled=True),
        )

    current = tokens.astype(jnp.float32)
    saved = []
    for use in range(USES):
        saved.append(current)
        current, kept = plain_forward(current, fetch(), mask)
    grad = cotangent.astype(jnp.float32)
    summed = None
    for use in reversed(range(USES)):
        grad, terms = plain_backward(saved[use], fetch(), mask, grad)
        if summed is None:
            summed = terms
        else:
            summed = tuple((first + second for first, second in zip(summed, terms)))
    owned = (
        lax.psum_scatter(summed[0], "own", scatter_dimension=0, tiled=True),
        lax.psum_scatter(summed[1], "own", scatter_dimension=0, tiled=True),
        lax.psum_scatter(summed[2], "own", scatter_dimension=0, tiled=True),
        lax.psum_scatter(summed[3], "own", scatter_dimension=0, tiled=True),
        lax.psum_scatter(summed[4], "own", scatter_dimension=0, tiled=True),
        lax.psum_scatter(summed[5], "own", scatter_dimension=0, tiled=True),
        lax.psum_scatter(summed[6], "own", scatter_dimension=0, tiled=True),
        lax.psum_scatter(summed[7], "own", scatter_dimension=0, tiled=True),
        lax.psum_scatter(summed[8], "own", scatter_dimension=0, tiled=True),
        lax.psum_scatter(summed[9], "own", scatter_dimension=0, tiled=True),
        lax.psum_scatter(summed[10], "own", scatter_dimension=0, tiled=True),
        lax.psum_scatter(summed[11], "own", scatter_dimension=0, tiled=True),
        lax.psum_scatter(summed[12], "own", scatter_dimension=0, tiled=True),
    )
    final = jax.tree.map(lambda part: part.astype(jnp.float32), lax.psum(as_sent(owned), "grp"))
    return (current.astype(jnp.bfloat16), grad) + tuple(final)


def solution(mesh):
    return jax.shard_map(
        kernels_body if tuple(mesh.axis_sizes) == (4, 8) else plain_body,
        mesh=mesh,
        in_specs=(
            P(("grp", "own"), None),
            P(("grp", "own")),
            P(("grp", "own"), None),
            P("own"),
            P("own"),
            P("own", None),
            P("own"),
            P("own"),
            P("own", None),
            P("own"),
            P("own"),
            P("own"),
            P("own", None),
            P("own"),
            P("own", None),
            P("own"),
        ),
        out_specs=(
            P(("grp", "own"), None),
            P(("grp", "own"), None),
            P("own"),
            P("own"),
            P("own", None),
            P("own"),
            P("own"),
            P("own", None),
            P("own"),
            P("own"),
            P("own"),
            P("own", None),
            P("own"),
            P("own", None),
            P("own"),
        ),
        check_vma=False,
    )
```

```python
import functools

import jax
import jax.numpy as jnp
from jax import lax
from jax.experimental import pallas as pl
from jax.experimental.pallas import tpu as pltpu
from jax.sharding import PartitionSpec as P

HEADS = 12
HEAD_DIM = 64
USES = 2
EPSILON = 1e-05
SCALE = HEAD_DIM ** (-0.5)
TANH_SCALE = 0.7978845608028654
TANH_CUBIC = 0.044715
MESH = pl.DeviceIdType.MESH
f32 = jnp.float32
bf16 = jnp.bfloat16

GAIN1, SHIFT1, BIAS_Q, BIAS_V, BIAS_OUT, GAIN2, SHIFT2, BIAS_PROJ, BIAS_FC = range(9)


def dot(a, b, ca=1, cb=0):
    return lax.dot_general(a, b, (((ca,), (cb,)), ((), ())), preferred_element_type=f32)


def loop(count, body):
    def step(i, carry):
        body(i)
        return carry

    lax.fori_loop(0, count, step, 0)


def span(begin, end, body):
    def step(i, carry):
        body(i)
        return carry

    lax.fori_loop(begin, end, step, 0)


def part(i, size):
    return pl.ds(pl.multiple_of(i * size, size), size)


def centred(x):
    centre = x - jnp.mean(x, axis=-1, keepdims=True)
    spread = jnp.mean(centre * centre, axis=-1, keepdims=True)
    return centre, lax.rsqrt(spread + EPSILON)


def norm_forward(x, gain, shift, h, unroll=True):
    rows = 128

    def step(i):
        these = pl.ds(i * rows, rows) if unroll else part(i, rows)
        centre, r = centred(x[these, :].astype(f32))
        h[these, :] = (centre * r * gain + shift).astype(bf16)

    if unroll:
        for i in range(x.shape[0] // rows):
            step(i)
    else:
        loop(x.shape[0] // rows, step)


def norm_backward(x, dh, gain, grad, out, sums, gain_row, shift_row, low=None):
    rows = 128

    def step(i):
        these = pl.ds(i * rows, rows)
        centre, r = centred(x[these, :].astype(f32))
        n = centre * r
        d = dh[these, :]
        sums[gain_row : gain_row + 1, :] += jnp.sum(d * n, axis=0, keepdims=True)
        sums[shift_row : shift_row + 1, :] += jnp.sum(d, axis=0, keepdims=True)
        e = d * gain
        inner = e - jnp.mean(e, axis=-1, keepdims=True) - n * jnp.mean(e * n, axis=-1, keepdims=True)
        result = grad[these, :].astype(f32) + r * inner
        out[these, :] = result
        if low is not None:
            low[these, :] = result.astype(bf16)

    for i in range(x.shape[0] // rows):
        step(i)


def column_sum(x):
    return jnp.sum(x.astype(f32), axis=0, keepdims=True)


def make_mask(doc, mask):
    count = doc.shape[1]
    half = count // 2
    ids = doc[0:1, :].astype(f32)
    keys = jnp.broadcast_to(ids, (128, count)).T[:, :1]
    for k0, q0, place in ((0, 0, 0), (half, half, count)):
        width = count - q0
        row = lax.broadcasted_iota(jnp.int32, (half, width), 0) + k0
        col = lax.broadcasted_iota(jnp.int32, (half, width), 1) + q0
        key = keys[k0 : k0 + half]
        same = (key == ids[:, q0:]) & (row <= col) & ((key != 0.0) | (row == col))
        mask[:, place : place + width] = jnp.where(same, 0.0, -1e30)


def head_lanes(h, x):
    lane = lax.broadcasted_iota(jnp.int32, (1, 2 * HEAD_DIM), 1)
    keep = (lane < HEAD_DIM) if h == 0 else (lane >= HEAD_DIM)
    return jnp.where(keep, x, jnp.zeros_like(x))


def attention_forward(qkv, mask, probs, o, begin=0, end=6, shift=0):
    count, width = o.shape
    half = count // 2
    pair = 2 * HEAD_DIM

    def step(i):
        col = pl.ds(i * pair, pair)
        q = qkv[:, col]
        k = qkv[:, pl.ds(width + i * pair, pair)]
        v = qkv[:, pl.ds(2 * width + i * pair, pair)]
        vt = v.T
        outs = []
        for h in range(2):
            kh = head_lanes(h, k)
            s0 = dot(kh[:half], q, 1, 1) + mask[:, :count]
            s1 = dot(kh[half:], q[half:], 1, 1) + mask[:, count:]
            m0 = jnp.max(s0, axis=0, keepdims=True)
            m1 = jnp.max(s1, axis=0, keepdims=True)
            top = jnp.concatenate([m0[:, :half], jnp.maximum(m0[:, half:], m1)], axis=1)
            e0 = jnp.exp(s0 - top)
            e1 = jnp.exp(s1 - top[:, half:])
            l0 = jnp.sum(e0, axis=0, keepdims=True)
            l1 = jnp.sum(e1, axis=0, keepdims=True)
            r = 1.0 / jnp.concatenate([l0[:, :half], l0[:, half:] + l1], axis=1)
            p0 = (e0 * r).astype(bf16)
            p1 = (e1 * r[:, half:]).astype(bf16)
            row = pl.ds(h * half, half)
            probs[i - shift, row, :count] = p0
            probs[i - shift, row, count:] = p1
            vh = vt[h * HEAD_DIM : (h + 1) * HEAD_DIM]
            first = dot(vh[:, :half], p0)
            second = dot(vh[:, half:], p1)
            outs.append(jnp.concatenate([first[:, :half], first[:, half:] + second], axis=1))
        o[:, col] = jnp.concatenate(outs, axis=0).astype(bf16).T

    for i in range(begin, end):
        step(i)


def attention_backward(qkv, probs, do, dz, sums, begin=0, end=6, shift=0):
    count, width = do.shape
    half = count // 2
    pair = 2 * HEAD_DIM

    def step(i):
        cq = pl.ds(i * pair, pair)
        ck = pl.ds(width + i * pair, pair)
        cv = pl.ds(2 * width + i * pair, pair)
        q, k, v, d = qkv[:, cq], qkv[:, ck], qkv[:, cv], do[:, cq]
        dq = dk = dv = None
        for h in range(2):
            dh, kh, qh = head_lanes(h, d), head_lanes(h, k), head_lanes(h, q)
            row = pl.ds(h * half, half)
            p0 = probs[i - shift, row, :count]
            p1 = probs[i - shift, row, count:]
            d0 = dot(v[:half], dh, 1, 1)
            d1 = dot(v[half:], dh[half:], 1, 1)
            w0 = p0.astype(f32)
            w1 = p1.astype(f32)
            t0 = jnp.sum(d0 * w0, axis=0, keepdims=True)
            t1 = jnp.sum(d1 * w1, axis=0, keepdims=True)
            t = jnp.concatenate([t0[:, :half], t0[:, half:] + t1], axis=1)
            s0 = (w0 * (d0 - t)).astype(bf16)
            s1 = (w1 * (d1 - t[:, half:])).astype(bf16)
            v_term = jnp.concatenate([dot(p0, dh), dot(p1, dh[half:])], axis=0)
            k_term = jnp.concatenate([dot(s0, qh), dot(s1, qh[half:])], axis=0)
            qa = dot(s0, kh[:half], 0, 0)
            qb = dot(s1, kh[half:], 0, 0)
            q_term = jnp.concatenate([qa[:half], qa[half:] + qb], axis=0)
            dq = q_term if dq is None else dq + q_term
            dk = k_term if dk is None else dk + k_term
            dv = v_term if dv is None else dv + v_term
        dq = (dq * SCALE).astype(bf16)
        dv = dv.astype(bf16)
        dz[:, cq] = dq
        dz[:, ck] = dk.astype(bf16)
        dz[:, cv] = dv
        sums[BIAS_Q : BIAS_Q + 1, cq] += column_sum(dq)
        sums[BIAS_V : BIAS_V + 1, cq] += column_sum(dv)

    for i in range(begin, end):
        step(i)


def small(block, row):
    return block[row : row + 1, :]


def hidden_tile(h2, weight, bias, f, slope, i):
    count, width = h2.shape
    rows = 128
    third = f.shape[2] // 8
    for first in range(0, count, rows):
        these = pl.ds(first, rows)
        u = dot(h2[these, :], weight) + bias
        square = u * u
        t = jnp.tanh(u * (TANH_SCALE + (TANH_SCALE * TANH_CUBIC) * square))
        rise = 0.5 + 0.5 * t
        active = (u * rise).astype(bf16)
        for place in range(width // third):
            owner = i * (width // third // 3) + place // 3
            f[place % 3, these, part(owner, third)] = active[:, place * third : (place + 1) * third]
        inner = TANH_SCALE + (3.0 * TANH_SCALE * TANH_CUBIC) * square
        slope[these, part(i, width)] = (rise + (0.5 * u) * (1.0 - t * t) * inner).astype(bf16)


def hidden_forward(h2, wfc, block, f, slope, begin, end):
    width = h2.shape[1]

    def hidden(i):
        hidden_tile(h2, wfc[:, part(i, width)], block[pl.ds(BIAS_FC + i, 1), :], f, slope, i)

    span(begin, end, hidden)


def project(f, wproj, i):
    third = f.shape[2] // 8
    rows = [wproj[pl.ds((owner * 3 + i) * third, third), :] for owner in range(8)]
    return dot(f[i], jnp.concatenate(rows, axis=0))


def coords():
    own = lax.axis_index("own")
    return lax.axis_index("grp"), own // 2, lax.rem(own, 2)


class Unit:
    def __init__(self, shard, full, row, rows, col, cols, shared=True):
        self.shard, self.full, self.shared = shard, full, shared
        self.row, self.rows, self.col, self.cols = row, rows, col, cols

    def mine(self, half=None):
        rows = self.rows if half is None else self.rows // 2
        start = self.row + (0 if half is None else half * rows)
        return self.shard.at[pl.ds(start, rows), pl.ds(self.col, self.cols)]

    def block(self, owner, half=None):
        rows = self.rows if half is None else self.rows // 2
        start = owner * self.shard.shape[0] + self.row + (0 if half is None else half * rows)
        return self.full.at[pl.ds(pl.multiple_of(start, 16), rows), pl.ds(self.col, self.cols)]


PIECES = [(1, 0), (1, 1), (2, 0), (2, 1), (3, 0), (3, 1)]


class Gather:
    def __init__(self, units, link_send, link_recv, core_send, core_recv, own_sem):
        self.units = units
        self.link_send, self.link_recv = link_send, link_recv
        self.core_send, self.core_recv, self.own_sem = core_send, core_recv, own_sem
        self.grp, self.chip, self.core = coords()
        self.odd = lax.rem(self.grp, 2)
        self.sent = []

    def owner(self, offset):
        return jnp.bitwise_xor(self.chip, offset) * 2 + self.core

    def device(self, chip_offset, along_z=False):
        own = jnp.bitwise_xor(self.chip, chip_offset) * 2 + self.core
        grp = self.grp + 1 - 2 * self.odd if along_z else self.grp
        return (grp, own)

    def link(self, k, src, dst, piece, out, device):
        return pltpu.make_async_remote_copy(
            src_ref=src,
            dst_ref=dst,
            send_sem=self.link_send.at[k, out],
            recv_sem=self.link_recv.at[k, piece],
            device_id=device,
            device_id_type=MESH,
        )

    def across(self, k, src, dst, slot):
        return pltpu.make_async_remote_copy(
            src_ref=src,
            dst_ref=dst,
            send_sem=self.core_send.at[k, slot],
            recv_sem=self.core_recv.at[k, slot],
            device_id=(self.grp, self.chip * 2 + 1 - self.core),
            device_id_type=MESH,
        )

    def own(self, k):
        unit = self.units[k]
        return pltpu.make_async_copy(unit.mine(), unit.block(self.owner(0)), self.own_sem.at[k])

    def first(self, k, offset, half, out):
        unit = self.units[k]
        piece = PIECES.index((offset, half))
        return self.link(
            k, unit.mine(half), unit.block(self.owner(0), half), piece, out, self.device(offset)
        )

    def relay(self, k, offset, half, way, out):
        unit = self.units[k]
        piece = unit.block(self.owner(offset), half)
        return self.link(k, piece, piece, PIECES.index((3, half)), out, self.device(way))

    def pair(self, k, offset, half, out):
        unit = self.units[k]
        piece = unit.block(self.owner(offset), half)
        return self.link(k, piece, piece, PIECES.index((offset, half)), out, self.device(0, True))

    def hand(self, k, offset, half):
        unit = self.units[k]
        piece = unit.block(self.owner(offset), half)
        return self.across(k, piece, piece, PIECES.index((offset, half)))

    def arrived(self, k, offset, half):
        unit = self.units[k]
        piece = unit.block(self.owner(offset), half)
        self.link(k, piece, piece, PIECES.index((offset, half)), 0, self.device(1)).wait_recv()

    def sends(self, k, odd):
        own = [(1, 0), (2, 1), (1, 1), (2, 0)]
        if not self.units[k].shared:
            own = [(2, 0), (1, 1), (1, 0), (2, 1)]
        elif odd:
            own = [(1, 1), (2, 0)]
        calls = [functools.partial(self.first, k, *what) for what in own]
        if odd or not self.units[k].shared:
            calls += [functools.partial(self.relay, k, *what) for what in ((2, 0, 1), (1, 1, 2))]
        if self.units[k].shared:
            pairs = ((3, 0), (3, 1)) if odd else ((1, 0), (2, 1))
            calls += [functools.partial(self.pair, k, *what) for what in pairs]
        return len(own), [functools.partial(call, out) for out, call in enumerate(calls)]

    def each_kind(self, k, body):
        if not self.units[k].shared:
            body(True)
            return

        @pl.when(self.odd == 0)
        def _():
            body(False)

        @pl.when(self.odd == 1)
        def _():
            body(True)

    def start(self, k):
        def body(odd):
            own, calls = self.sends(k, odd)
            for call in calls[:own]:
                call().start()

        self.each_kind(k, body)
        unit = self.units[k]
        self.across(k, unit.mine(), unit.block(self.owner(0)), len(PIECES)).start()
        self.own(k).start()

    def serve(self, k, odd, pieces, then):
        for piece in pieces:
            self.arrived(k, *piece)
            if piece in then:
                then[piece]().start()
            self.hand(k, *piece).start()

    def serve_first(self, k):
        def body(odd):
            own, calls = self.sends(k, odd)
            if odd:
                then = {(2, 0): calls[own], (1, 1): calls[own + 1]}
                self.serve(k, odd, ((2, 0), (1, 1)), then)
            else:
                then = {(1, 0): calls[own], (2, 1): calls[own + 1]}
                self.serve(k, odd, ((1, 0), (2, 1), (1, 1), (2, 0)), then)

        self.each_kind(k, body)

    def serve_second(self, k):
        def body(odd):
            own, calls = self.sends(k, odd)
            if not self.units[k].shared:
                self.serve(k, odd, ((1, 0), (2, 1), (3, 0), (3, 1)), {})
            elif odd:
                then = {(3, 0): calls[own + 2], (3, 1): calls[own + 3]}
                self.serve(k, odd, ((3, 0), (3, 1), (1, 0), (2, 1)), then)
            else:
                self.serve(k, odd, ((3, 0), (3, 1)), {})

        self.each_kind(k, body)

    def finish(self, k):
        unit = self.units[k]
        other = 1 - 2 * self.core
        self.own(k).wait()
        whole = unit.block(self.owner(0) + other)
        self.across(k, whole, whole, len(PIECES)).wait_recv()
        for slot, (offset, half) in enumerate(PIECES):
            piece = unit.block(self.owner(offset) + other, half)
            self.across(k, piece, piece, slot).wait_recv()

    def drain(self, k):
        def body(odd):
            own, calls = self.sends(k, odd)
            for call in calls:
                call().wait_send()

        self.each_kind(k, body)
        unit = self.units[k]
        self.across(k, unit.mine(), unit.block(self.owner(0)), len(PIECES)).wait_send()
        for offset, half in PIECES:
            self.hand(k, offset, half).wait_send()


def store(copies, sem, src, dst):
    copy = pltpu.make_async_copy(src, dst, sem.at[len(copies)])
    copy.start()
    copies.append(copy)


def first_kernel(
    tokens, doc, packed, sqkv, sout, sfc, sproj,
    x2_out, block_out, mask_out, w_out,
    h1_out, qkv_out, probs_out, o_out, x1_out, h2_out, slope_out, f_out,
    wqkv, wout, wfc, wproj, block, mask, h1, qkv, probs, o, x1, h2, slope, f, x2, many,
    link_send, link_recv, core_send, core_recv, own_sem, small_send, small_recv, out_sem,
):
    grp, chip, core = coords()
    me = chip * 2 + core
    width = tokens.shape[1]
    barrier = pltpu.get_barrier_semaphore()
    peers = [(grp, jnp.bitwise_xor(me, j)) for j in range(1, 8)]
    peers.append((grp + 1 - 2 * lax.rem(grp, 2), me))
    for peer in peers:
        pl.semaphore_signal(barrier, inc=1, device_id=peer, device_id_type=MESH)
    pl.semaphore_wait(barrier, len(peers))

    units = [Unit(sqkv, wqkv, 0, sqkv.shape[0], i * width, width) for i in range(3)]
    units += [Unit(sout, wout, 0, sout.shape[0], 0, width)]
    units += [Unit(sfc, wfc, 0, sfc.shape[0], i * width, width) for i in range(sfc.shape[1] // width)]
    thirds = sproj.shape[0] // 3
    units += [Unit(sproj, wproj, i * thirds, thirds, 0, width, False) for i in range(3)]
    gather = Gather(units, link_send, link_recv, core_send, core_recv, own_sem)
    count = len(units)

    def small_copy(j, slot):
        return pltpu.make_async_remote_copy(
            src_ref=packed,
            dst_ref=many.at[slot],
            send_sem=small_send.at[j - 1],
            recv_sem=small_recv.at[j - 1],
            device_id=(grp, jnp.bitwise_xor(me, j)),
            device_id_type=MESH,
        )

    for j in range(1, 8):
        small_copy(j, j).start()
    gather.start(0)
    gather.start(1)
    copies = []

    def slot(s):
        if s < count:
            gather.serve_first(s)
        if s + 2 < count:
            gather.start(s + 2)
        if 0 <= s - 2 < count:
            gather.serve_second(s - 2)
        if 0 <= s - 3 < count:
            gather.finish(s - 3)

    make_mask(doc, mask)
    store(copies, out_sem, mask, mask_out)
    slot(0)
    total = packed[...].astype(f32)
    for j in range(1, 8):
        small_copy(j, j).wait_recv()
        total = total + many[j].astype(f32)
    block[...] = total
    store(copies, out_sem, block, block_out)
    slot(1)
    norm_forward(tokens, small(block, GAIN1), small(block, SHIFT1), h1, False)
    store(copies, out_sem, h1, h1_out)
    slot(2)
    slot(3)
    qkv[:, :width] = (dot(h1[...], wqkv[:, :width]) + small(block, BIAS_Q)).astype(bf16) * SCALE
    slot(4)
    qkv[:, width : 2 * width] = dot(h1[...], wqkv[:, width : 2 * width]).astype(bf16)
    slot(5)
    for i in range(3):
        store(copies, out_sem, wqkv.at[:, pl.ds(i * width, width)], w_out.at[i])
    qkv[:, 2 * width :] = (dot(h1[...], wqkv[:, 2 * width :]) + small(block, BIAS_V)).astype(bf16)
    store(copies, out_sem, qkv, qkv_out)
    attention_forward(qkv, mask, probs, o, 0, 1)
    slot(6)
    store(copies, out_sem, wout, w_out.at[3])
    attention_forward(qkv, mask, probs, o, 1, 3)
    slot(7)
    attention_forward(qkv, mask, probs, o, 3, 5)
    slot(8)
    attention_forward(qkv, mask, probs, o, 5, 6)
    store(copies, out_sem, probs, probs_out)
    store(copies, out_sem, o, o_out)
    x1[...] = tokens[...].astype(f32) + (dot(o[...], wout[...]) + small(block, BIAS_OUT))
    norm_forward(x1, small(block, GAIN2), small(block, SHIFT2), h2, False)
    store(copies, out_sem, x1, x1_out)
    store(copies, out_sem, h2, h2_out)
    slot(9)
    hidden_forward(h2, wfc, block, f, slope, 0, 2)
    slot(10)
    fc_tiles = wfc.shape[1] // width
    for i in range(fc_tiles):
        store(copies, out_sem, wfc.at[:, pl.ds(i * width, width)], w_out.at[4 + i])
    hidden_forward(h2, wfc, block, f, slope, 2, 4)
    store(copies, out_sem, f, f_out)
    store(copies, out_sem, slope, slope_out)

    slot(11)
    x2[...] = x1[...] + (project(f, wproj, 0) + small(block, BIAS_PROJ))
    slot(12)
    x2[...] += project(f, wproj, 1)
    slot(13)
    for i in range(fc_tiles):
        store(copies, out_sem, wproj.at[pl.ds(i * width, width), :], w_out.at[4 + fc_tiles + i])
    x2[...] += project(f, wproj, 2)
    store(copies, out_sem, x2, x2_out)
    for k in range(count):
        gather.drain(k)
    for j in range(1, 8):
        small_copy(j, j).wait_send()
    for copy in copies:
        copy.wait()


def second_kernel(
    x2_in, tokens_in, cot_in, mask_in, block, w_in, w_parts_in, w_thirds_in,
    h1a_in, qkv_in, probs_in, oa_in, x1_in, h2a_in, slope_in, fa_in,
    act_out, grad_out, sums_out, gqkv_out, gout_out, gfc_out, gproj_out,
    x, tokens, cot, grad, x1, dh, tiles, h1a, qkv, oa, h2a, slope, h1b, dzb, ob, h2b, dub, shared, more_probs,
    gm, da, dab, sums,
    buf_p, buf_o, recv_p, recv_o, hop1_p, hop1_o, hop2_p, hop2_o, zmid_p, zmid_o, tot_p, tot_o,
    small_in, small_tot,
    in_sem, tile_sem, out_sem, send, recv, small_send, small_recv,
):
    grp, chip, core = coords()
    yy, xx = chip // 2, lax.rem(chip, 2)
    me = chip * 2 + core
    width = x.shape[1]
    loads = {}

    def load(name, src, dst):
        copy = pltpu.make_async_copy(src, dst, in_sem.at[len(loads)])
        copy.start()
        loads[name] = copy

    fb, fa = shared.at[pl.ds(0, 3)], shared.at[pl.ds(3, 3)]
    probs = shared.at[:, :, pl.ds(0, probs_in.shape[2])]
    some_probs = shared.at[pl.ds(3, 3), :, pl.ds(0, probs_in.shape[2])]
    half = x.shape[0] // 2
    mask = dh.at[pl.ds(0, half), :]
    load("x", x2_in, x)

    ff_tiles = w_in.shape[0] - 8
    ring = tiles.shape[0]
    fc_at, proj_at = 4, 4 + ff_tiles
    order = [proj_at + t for t in range(ff_tiles)] + [fc_at + t for t in range(ff_tiles)] + [3, 0, 1, 2]

    def tile_copy(t):
        return pltpu.make_async_copy(w_in.at[order[t]], tiles.at[t % ring], tile_sem.at[t % ring])

    def tile(t):
        tile_copy(t).wait()
        return tiles[t % ring]

    def next_tile(t):
        if t + ring < len(order):
            tile_copy(t + ring).start()

    def square(value):
        return value.reshape(width, width)

    def resident(t):
        if t < 2:
            return square(buf_o[t])
        if t < 4:
            return jnp.concatenate(
                [buf_p[t - 2, 0].reshape(-1, width), buf_p[t - 2, 1, 0].reshape(-1, width)], axis=0
            )
        return square(recv_o[2 * (t - 4) : 2 * (t - 4) + 2])

    for t in range(2):
        load(f"w{t}", w_parts_in.at[t], buf_o.at[t])
    load("w2", w_thirds_in.at[2, pl.ds(0, 2)], buf_p.at[0, 0])
    load("w2b", w_thirds_in.at[2, 2], buf_p.at[0, 1, 0])
    load("mask", mask_in, mask)
    load("w3", w_thirds_in.at[3, pl.ds(0, 2)], buf_p.at[1, 0])
    load("w3b", w_thirds_in.at[3, 2], buf_p.at[1, 1, 0])
    for t in range(ff_tiles):
        load(f"w{fc_at + t}", w_parts_in.at[fc_at + t], recv_o.at[pl.ds(2 * t, 2)])
    for t in range(ring):
        tile_copy(t).start()
    core_peer = (grp, jnp.bitwise_xor(me, 1))
    x_peer = (grp, jnp.bitwise_xor(me, 2))
    y_peer = (grp, jnp.bitwise_xor(me, 4))
    low = grp == 1
    middle = (grp == 1) | (grp == 2)
    end = jnp.logical_not(middle)
    inward = (jnp.where(grp == 0, 1, 2), me)
    outward = (jnp.where(low, 0, 3), me)
    across = (jnp.where(low, 2, 1), me)

    barrier = pltpu.get_barrier_semaphore()

    def greet():
        for peer in (core_peer, x_peer, y_peer):
            pl.semaphore_signal(barrier, inc=1, device_id=peer, device_id_type=MESH)

        @pl.when(end)
        def _():
            pl.semaphore_signal(barrier, inc=1, device_id=inward, device_id_type=MESH)

        @pl.when(middle)
        def _():
            pl.semaphore_signal(barrier, inc=1, device_id=outward, device_id_type=MESH)
            pl.semaphore_signal(barrier, inc=1, device_id=across, device_id_type=MESH)

    def remote(src, dst, i, stage, peer):
        return pltpu.make_async_remote_copy(
            src_ref=src, dst_ref=dst, send_sem=send.at[i, stage], recv_sem=recv.at[i, stage],
            device_id=peer, device_id_type=MESH,
        )

    third_width = width // 3
    specs = [(True, 0, 0, width // 2), (True, 0, width // 2, width // 2), (True, 1, 0, width), (True, 2, 0, width)]
    projs = len(specs)
    specs += [(False, j, 0, width) for j in range(ff_tiles + 3)]
    specs += [(False, ff_tiles + 3, 0, 2 * third_width), (False, ff_tiles + 3, 2 * third_width, third_width)]
    chunks = len(specs)
    copies = []

    buffers = (
        (buf_p, buf_o), (recv_p, recv_o), (hop1_p, hop1_o), (hop2_p, hop2_o), (zmid_p, zmid_o),
        (tot_p, tot_o),
    )

    class Chunk:
        def __init__(self, i):
            self.i = i
            self.proj, self.at, col, self.width = specs[i]
            cols = pl.ds(col, self.width)
            sets = [pair[0 if self.proj else 1] for pair in buffers]
            ring = sets[0].shape[0]
            order = i if self.proj else i - projs
            self.previous = i - ring if order >= ring else None
            self.last = i + ring >= (projs if self.proj else chunks)
            self.rows = sets[1].shape[3]
            self.buf = sets[0].at[order % ring, :, :, :, :, cols]
            self.recv = sets[1].at[self.at, :, :, :, cols]
            self.hop1 = sets[2].at[self.at, :, :, :, cols]
            self.hop2, self.zmid, self.tot = (
                s.at[self.at, :, :, cols] if len(s.shape) == 4 else s.at[self.at, :, cols] for s in sets[3:]
            )
            half = self.rows // 2
            self.top, self.bottom = pl.ds(0, half), pl.ds(half, half)
            self.cols = cols

        def to_core(self):
            return remote(self.buf.at[1 - core], self.recv, self.i, 0, core_peer)

        def first(self):
            return (
                remote(self.recv.at[:, 1 - xx, self.top, :], self.hop1.at[0], self.i, 1, x_peer),
                remote(self.recv.at[1 - yy, :, self.bottom, :], self.hop1.at[1], self.i, 2, y_peer),
            )

        def second(self):
            return (
                remote(self.recv.at[1 - yy, xx, self.top, :], self.hop2.at[0], self.i, 3, y_peer),
                remote(self.recv.at[yy, 1 - xx, self.bottom, :], self.hop2.at[1], self.i, 4, x_peer),
            )

        def to_middle(self):
            return remote(self.recv.at[yy, xx], self.tot, self.i, 5, inward)

        def between(self):
            return remote(self.recv.at[yy, xx], self.zmid, self.i, 6, across)

        def to_end(self):
            return remote(self.tot, self.tot, self.i, 7, outward)

        def begin(self):
            if self.previous is not None:
                Chunk(self.previous).to_core().wait_send()

        def stage_b(self):
            self.to_core().wait_recv()
            self.recv[...] = self.recv[...] + self.buf[core]
            for copy in self.first():
                copy.start()

        def stage_c(self):
            for copy in self.first():
                copy.wait_recv()
            self.recv[:, xx, self.top, :] = self.recv[:, xx, self.top, :] + self.hop1[0]
            self.recv[yy, :, self.bottom, :] = self.recv[yy, :, self.bottom, :] + self.hop1[1]
            for copy in self.second():
                copy.start()

        def stage_d(self):
            for copy in self.second():
                copy.wait_recv()
            self.recv[yy, xx, self.top, :] = self.recv[yy, xx, self.top, :] + self.hop2[0]
            self.recv[yy, xx, self.bottom, :] = self.recv[yy, xx, self.bottom, :] + self.hop2[1]

            @pl.when(end)
            def _():
                self.to_middle().start()

        def stage_e(self):
            @pl.when(middle)
            def _():
                self.to_middle().wait_recv()
                self.recv[yy, xx] = self.recv[yy, xx] + self.tot[...]
                self.between().start()

        def stage_f(self):
            @pl.when(middle)
            def _():
                self.between().wait_recv()
                self.tot[...] = self.recv[yy, xx] + self.zmid[...]
                self.to_end().start()

        def stage_g(self):
            @pl.when(end)
            def _():
                self.to_end().wait_recv()

            if self.proj:
                place = gproj_out.at[pl.ds(self.at * self.rows, self.rows), self.cols]
            elif self.at < ff_tiles:
                place = gfc_out.at[:, pl.ds(self.at * width, width)]
            elif self.at == ff_tiles:
                place = gout_out
            else:
                place = gqkv_out.at[:, pl.ds((self.at - ff_tiles - 1) * width + specs[self.i][2], self.width)]
            store(copies, out_sem, self.tot, place)

        def finish(self):
            if self.last:
                self.to_core().wait_send()
            for copy in self.first() + self.second():
                copy.wait_send()

            @pl.when(end)
            def _():
                self.to_middle().wait_send()

            @pl.when(middle)
            def _():
                self.between().wait_send()
                self.to_end().wait_send()

    def made(i):
        Chunk(i).to_core().start()

    def proj_chunk(i):
        chunk = Chunk(i)
        chunk.begin()
        rows = chunk.rows
        yb, ya = cot[:, chunk.cols], gm[:, chunk.cols]
        for owner in range(8):
            col = pl.ds(owner * rows, rows)
            value = dot(fb[chunk.at, :, col], yb, 0, 0) + dot(fa[chunk.at, :, col], ya, 0, 0)
            chunk.buf[owner % 2, owner // 4, (owner // 2) % 2] = value.astype(bf16)
        made(i)

    def other_chunk(i, xa, ya, xb, yb, col):
        chunk = Chunk(i)
        chunk.begin()
        cols = pl.ds(col, chunk.width)
        rows = chunk.rows
        for first in (0, 4):
            these = pl.ds(first * rows, 4 * rows)
            value = dot(xa[:, these], ya[:, cols], 0, 0) + dot(xb[:, these], yb[:, cols], 0, 0)
            for at in range(4):
                owner = first + at
                piece = value[at * rows : (at + 1) * rows].astype(bf16)
                chunk.buf[owner % 2, owner // 4, (owner // 2) % 2] = piece
        made(i)

    def b(i):
        Chunk(i).stage_b()

    def period(k):
        if k < chunks:
            Chunk(k).stage_c()
        if 2 <= k + 2 < chunks:
            b(k + 2)
        for lag, name in ((1, "stage_d"), (2, "stage_e"), (3, "stage_f"), (5, "stage_g")):
            if 0 <= k - lag < chunks:
                getattr(Chunk(k - lag), name)()

    sums[...] = jnp.zeros_like(sums)
    loads["x"].wait()
    norm_forward(x, small(block, GAIN1), small(block, SHIFT1), h1b)
    for name in ("w0", "w1", "w2", "w2b"):
        loads[name].wait()
    for t, (bias, scale) in enumerate(((small(block, BIAS_Q), SCALE), (None, None), (small(block, BIAS_V), None))):
        z = dot(h1b[...], resident(t))
        z = z if bias is None else z + bias
        z = z.astype(bf16)
        dzb[:, t * width : (t + 1) * width] = z if scale is None else z * scale
    loads["mask"].wait()
    attention_forward(dzb, mask, some_probs, ob, 0, 3)
    load("cot", cot_in, cot)
    for name, src, dst in (
        ("h2a", h2a_in, h2a), ("slope", slope_in, slope), ("qkv", qkv_in, qkv), ("oa", oa_in, oa), ("h1a", h1a_in, h1a),
        ("tokens", tokens_in, tokens),
    ):
        load(name, src, dst)
    attention_forward(dzb, mask, more_probs, ob, 3, 6, 3)
    loads["w3"].wait()
    loads["w3b"].wait()
    for first in range(0, x.shape[0], 128):
        these = pl.ds(first, 128)
        x1[these, :] = x[these, :] + (dot(ob[these, :], resident(3)) + small(block, BIAS_OUT))
    norm_forward(x1, small(block, GAIN2), small(block, SHIFT2), h2b)
    for t in range(ff_tiles):
        loads[f"w{fc_at + t}"].wait()
    for t in range(ff_tiles):
        hidden_tile(h2b, resident(fc_at + t), block[BIAS_FC + t : BIAS_FC + t + 1, :], fb, dub, t)
    third = fb.shape[2] // 8

    def hidden_rows(t):
        owners = width // (3 * third)
        pieces = [
            fb[j, :, pl.ds((t * owners + owner) * third, third)] for owner in range(owners) for j in range(3)
        ]
        return jnp.concatenate(pieces, axis=1)

    for t in range(ff_tiles):
        tile_copy(t).wait()
    dh[...] = dot(hidden_rows(0), tiles[0])
    for t in range(1, ff_tiles):
        dh[...] += dot(hidden_rows(t), tiles[t])
    for first in range(0, x.shape[0], 128):
        these = pl.ds(first, 128)
        gm[these, :] = (x1[these, :] + (dh[these, :] + small(block, BIAS_PROJ))).astype(bf16)
    store(copies, out_sem, gm, act_out)

    def hidden_backward(g, held, t):
        cols = pl.ds(t * width, width)
        d = (dot(g[...], tiles[t], 1, 1) * held[:, cols].astype(f32)).astype(bf16)
        held[:, cols] = d
        sums[BIAS_FC + t : BIAS_FC + t + 1, :] += column_sum(d)

    def input_gradient(held, weights, first=0):
        for t, weight in enumerate(weights, first):
            term = dot(held[:, t * width : (t + 1) * width], weight(), 1, 1)
            dh[...] = term if t == 0 else dh[...] + term

    def residents(first, number):
        return [functools.partial(resident, first + t) for t in range(number)]

    def streamed(first, number):
        return [functools.partial(tile, first + t) for t in range(number)]

    loads["cot"].wait()
    sums[BIAS_PROJ : BIAS_PROJ + 1, :] += column_sum(cot[...])
    for t in range(ff_tiles):
        hidden_backward(cot, dub, t)
    input_gradient(dub, residents(fc_at, ff_tiles))
    greet()
    norm_backward(x1, dh, small(block, GAIN2), cot, grad, sums, GAIN2, SHIFT2, dab)
    load("x1", x1_in, x1)
    da[...] = dot(dab[...], resident(3), 1, 1).astype(bf16)
    sums[BIAS_OUT : BIAS_OUT + 1, :] += column_sum(dab[...])
    attention_backward(dzb, some_probs, da, dzb, sums, 0, 3)
    load("fa", fa_in, fa)
    attention_backward(dzb, more_probs, da, dzb, sums, 3, 6, 3)
    input_gradient(dzb, residents(0, 3))
    norm_backward(x, dh, small(block, GAIN1), grad, grad, sums, GAIN1, SHIFT1)

    copies[0].wait()
    gm[...] = grad[...].astype(bf16)

    @pl.when(end)
    def _():
        pl.semaphore_wait(barrier, 4)

    @pl.when(middle)
    def _():
        pl.semaphore_wait(barrier, 5)

    loads["fa"].wait()
    proj_chunk(0)
    proj_chunk(1)
    b(0)
    proj_chunk(2)
    b(1)
    loads["slope"].wait()
    hidden_backward(gm, slope, 0)
    next_tile(0)
    period(0)
    proj_chunk(3)
    load("probs", probs_in, probs)
    sums[BIAS_PROJ : BIAS_PROJ + 1, :] += column_sum(gm[...])
    hidden_backward(gm, slope, 1)
    next_tile(1)
    period(1)
    for t in range(2, ff_tiles):
        hidden_backward(gm, slope, t)
        next_tile(t)
    n = ff_tiles

    def fc_chunk(t):
        other_chunk(projs + t, h2a, slope, h2b, dub, t * width)

    loads["h2a"].wait()
    fc_chunk(0)
    input_gradient(slope, streamed(n, ff_tiles // 2))
    period(2)
    fc_chunk(1)
    input_gradient(slope, streamed(n + ff_tiles // 2, ff_tiles // 2), ff_tiles // 2)
    for t in range(ff_tiles):
        next_tile(n + t)
    n += ff_tiles
    loads["x1"].wait()
    norm_backward(x1, dh, small(block, GAIN2), grad, grad, sums, GAIN2, SHIFT2, da)
    period(3)
    fc_chunk(2)
    do = cot
    do[...] = dot(da[...], tile(n), 1, 1).astype(bf16)
    n += 1
    sums[BIAS_OUT : BIAS_OUT + 1, :] += column_sum(da[...])
    loads["qkv"].wait()
    loads["probs"].wait()
    attention_backward(qkv, probs, do, qkv, sums, 0, 1)
    period(4)
    fc_chunk(3)
    attention_backward(qkv, probs, do, qkv, sums, 1, 3)
    period(5)
    loads["oa"].wait()
    other_chunk(8, oa, da, ob, dab, 0)
    attention_backward(qkv, probs, do, qkv, sums, 3, 5)
    period(6)
    attention_backward(qkv, probs, do, qkv, sums, 5, 6)
    loads["h1a"].wait()
    other_chunk(9, h1a, qkv, h1b, dzb, 0)
    period(7)
    other_chunk(10, h1a, qkv, h1b, dzb, width)
    input_gradient(qkv, streamed(n, 3))
    period(8)
    other_chunk(11, h1a, qkv, h1b, dzb, 2 * width)
    loads["tokens"].wait()
    norm_backward(tokens, dh, small(block, GAIN1), grad, grad, sums, GAIN1, SHIFT1)
    store(copies, out_sem, grad, grad_out)

    def small_copy(step, src, peer):
        return pltpu.make_async_remote_copy(
            src_ref=src, dst_ref=small_in.at[step], send_sem=small_send.at[step], recv_sem=small_recv.at[step],
            device_id=peer, device_id_type=MESH,
        )

    own_peers = (core_peer, x_peer, y_peer)

    def small_next(step):
        small_copy(step, small_tot.at[step], own_peers[step]).wait_recv()
        small_tot[step + 1] = small_tot[step] + small_in[step]
        if step + 1 < 3:
            small_copy(step + 1, small_tot.at[step + 1], own_peers[step + 1]).start()
        else:

            @pl.when(end)
            def _():
                small_copy(3, small_tot.at[3], inward).start()

    def small_middle():
        @pl.when(middle)
        def _():
            small_copy(3, small_tot.at[3], inward).wait_recv()
            small_tot[4] = small_tot[3] + small_in[3]
            small_copy(4, small_tot.at[4], across).start()

    def small_last():
        @pl.when(middle)
        def _():
            small_copy(4, small_tot.at[4], across).wait_recv()
            small_tot[5] = small_tot[4] + small_in[4]
            small_copy(5, small_tot.at[5], outward).start()
            sums_out[...] = small_tot[5]

    small_tot[0] = sums[...]
    small_copy(0, small_tot.at[0], own_peers[0]).start()
    period(9)
    other_chunk(12, h1a, qkv, h1b, dzb, 2 * width + 2 * third_width)
    small_next(0)
    period(10)
    small_next(1)
    period(11)
    small_next(2)
    period(12)
    small_middle()
    period(13)
    small_last()
    for k in range(14, chunks + 5):
        period(k)

    @pl.when(end)
    def _():
        small_copy(5, small_tot.at[5], outward).wait_recv()
        sums_out[...] = small_in[5]

    for i in range(chunks):
        Chunk(i).finish()
    for step in range(3):
        small_copy(step, small_tot.at[step], own_peers[step]).wait_send()

    @pl.when(end)
    def _():
        small_copy(3, small_tot.at[3], inward).wait_send()

    @pl.when(middle)
    def _():
        small_copy(4, small_tot.at[4], across).wait_send()
        small_copy(5, small_tot.at[5], outward).wait_send()

    for copy in copies[1:]:
        copy.wait()


def last_kernel(
    act, tokens_grad, sums, gqkv, gout, gfc, gproj,
    act_out, tokens_grad_out, gqkv_out, gout_out, gfc_out, gproj_out,
    g1, s1, gbq, gbv, gbo, g2, s2, gbp, gbfc,
    lqkv, lout, lfc, lproj, fqkv, fout, ffc, fproj, act_here, grad_here, in_sem, out_sem,
):
    lows = (lqkv, lout, lfc, lproj)
    loads = [
        pltpu.make_async_copy(src, dst, in_sem.at[i]) for i, (src, dst) in enumerate(zip((gqkv, gout, gfc, gproj), lows))
    ]
    passing = [
        pltpu.make_async_copy(act, act_here, in_sem.at[4]), pltpu.make_async_copy(tokens_grad, grad_here, in_sem.at[5])
    ]
    for copy in passing + [loads[i] for i in (3, 2, 0, 1)]:
        copy.start()
    copies = []
    for copy, here, place in zip(passing, (act_here, grad_here), (act_out, tokens_grad_out)):
        copy.wait()
        store(copies, out_sem, here, place)
    wides = ((fqkv, gqkv_out), (fout, gout_out), (ffc, gfc_out), (fproj, gproj_out))
    for i in (3, 2, 0, 1):
        loads[i].wait()
        wide, place = wides[i]
        wide[...] = lows[i][...].astype(f32)
        store(copies, out_sem, wide, place)
    owners = lax.axis_size("own")
    me = lax.axis_index("own")
    size, ff_size = g1.shape[0], gbfc.shape[0]
    across = sums.shape[1] // ff_size
    mine = jnp.zeros((8, size), f32)
    mine_ff = jnp.zeros((1, ff_size), f32)
    for owner in range(owners):
        here = me == owner
        mine = jnp.where(here, sums[:8, owner * size : (owner + 1) * size], mine)
        row, col = BIAS_FC + owner // across, owner % across * ff_size
        mine_ff = jnp.where(here, sums[row : row + 1, col : col + ff_size], mine_ff)
    for row, place in enumerate((g1, s1, gbq, gbv, gbo, g2, s2, gbp)):
        place[...] = mine[row]
    gbfc[...] = mine_ff[0]
    for copy in copies:
        copy.wait()


VMEM_BYTES = 65_200 * 1024


def spec(shape, dtype):
    return jax.ShapeDtypeStruct(shape, dtype)


def kernels_body(*args):
    tokens, doc, cotangent = args[:3]
    gain1, shift1, sqkv, bq, bv, sout, bo, gain2, shift2, sfc, bfc, sproj, bp = args[3:]
    count, width = tokens.shape
    ff = sfc.shape[1]
    owners = lax.axis_size("own")
    me = lax.axis_index("own")
    rows = [gain1, shift1, bq, bv, bo, gain2, shift2, bp]
    stacked = jnp.tile(jnp.stack(rows), (1, owners))
    mine = lax.broadcasted_iota(jnp.int32, stacked.shape, 1) // gain1.shape[0] == me
    stacked = jnp.where(mine, stacked, jnp.zeros_like(stacked))
    tiled = jnp.tile(bfc, owners)
    mine = lax.broadcasted_iota(jnp.int32, tiled.shape, 0) // bfc.shape[0] == me
    tiled = jnp.where(mine, tiled, jnp.zeros_like(tiled)).reshape(ff // width, width)
    packed = jnp.concatenate([stacked, tiled, jnp.zeros((16 - 8 - ff // width, width), bf16)])

    hbm = pl.BlockSpec(memory_space=pl.ANY)
    vmem = pl.BlockSpec(memory_space=pltpu.VMEM)
    V = pltpu.VMEM
    half = count // 2
    x_s = ((count, width), f32)
    low_s = ((count, width), bf16)
    qkv_s = ((count, 3 * width), bf16)
    ff_s = ((count, ff), bf16)
    probs_s = ((HEADS // 2, count, count + half), bf16)
    f_s = ((3, count, 8 * (sproj.shape[0] // 3)), bf16)
    mask_s = ((half, count + half), f32)
    block_s = ((16, width), f32)
    w_s = [((width, 3 * width), bf16), ((width, width), bf16), ((width, ff), bf16), ((ff, width), bf16)]
    units = 3 + 1 + ff // width + 3
    dma = pltpu.SemaphoreType.DMA

    def call(kernel, inputs, outs, scratch, in_specs, out_specs, **params):
        return pl.pallas_call(
            kernel,
            out_shape=[spec(*s) for s in outs],
            in_specs=in_specs,
            out_specs=out_specs,
            scratch_shapes=scratch,
            compiler_params=pltpu.CompilerParams(vmem_limit_bytes=VMEM_BYTES, **params),
        )(*inputs)

    w_all = ((4 + 2 * (ff // width), width, width), bf16)
    outs = [x_s, block_s, mask_s, w_all, low_s, qkv_s, probs_s, low_s, x_s, low_s, ff_s, f_s]
    (x2, block, mask, w, h1a, qkva, probsa, oa, x1a, h2a, slopea, fa) = call(
        first_kernel,
        (tokens, doc.reshape(1, count), packed, sqkv, sout, sfc, sproj),
        outs,
        [V(*s) for s in w_s]
        + [V(*s) for s in (block_s, mask_s, low_s, qkv_s, probs_s, low_s, x_s, low_s, ff_s, f_s, x_s)]
        + [V((8, 16, width), bf16)]
        + [dma((units, 6)), dma((units, 6)), dma((units, 7)), dma((units, 7)), dma((units,)), dma((7,)), dma((7,))]
        + [dma((len(outs) + 11,))],
        [vmem] * 3 + [hbm] * 4,
        [hbm] * len(outs),
        collective_id=0,
        has_side_effects=True,
    )
    shard = sqkv.shape[0]
    third = sproj.shape[0] // 3
    tiles = 1 + 3 + ff // width

    half_rows = [((3, 2, 2, third // 2, width), bf16), ((tiles, 2, 2, shard // 2, width), bf16)]
    half_rows2 = [((3, 2, third // 2, width), bf16), ((tiles, 2, shard // 2, width), bf16)]
    blocks = [((3, third, width), bf16), ((tiles, shard, width), bf16)]
    outs = [low_s, x_s, block_s, *[(s.shape, bf16) for s in (sqkv, sout, sfc, sproj)]]
    scratch = [x_s, low_s, low_s, x_s, x_s, x_s, ((4, width, width), bf16), low_s, qkv_s, low_s, low_s, ff_s]
    scratch += [low_s, qkv_s, low_s, low_s, ff_s, ((2 * f_s[0][0], *f_s[0][1:]), bf16)]
    scratch += [((HEADS // 4, count, count + half), bf16), low_s, low_s, low_s, block_s]
    scratch += [((2, 2, 2, 2, third, width), bf16), ((2, 2, 2, 2, shard, width), bf16)]
    scratch += [((3, 2, 2, third, width), bf16), ((tiles, 2, 2, shard, width), bf16)]
    scratch += half_rows + half_rows2 + blocks * 2
    scratch += [((6, 16, width), f32), ((6, 16, width), f32)]
    act, tokens_grad, sums, *grads = call(
        second_kernel,
        (
            x2, tokens, cotangent, mask, block, w, w.reshape(-1, 2, 2, 2, shard, width),
            w.reshape(-1, 3, 2, third, width),
            h1a, qkva, probsa, oa, x1a, h2a, slopea, fa,
        ),
        outs,
        [V(*s) for s in scratch]
        + [dma((24,)), dma((4,)), dma((16,)), dma((13, 8)), dma((13, 8)), dma((6,)), dma((6,))],
        [hbm] * 4 + [vmem] + [hbm] * 11,
        [hbm, hbm, vmem] + [hbm] * 4,
        collective_id=1,
        has_side_effects=True,
    )
    shards = [(s.shape, f32) for s in (sqkv, sout, sfc, sproj)]
    vectors = [(gain1.shape, f32)] * 8 + [(bfc.shape, f32)]
    act, tokens_grad, gqkv, gout, gfc, gproj, *small_grads = call(
        last_kernel,
        (act, tokens_grad, sums, *grads),
        [low_s, x_s, *shards, *vectors],
        [V(s.shape, bf16) for s in (sqkv, sout, sfc, sproj)] + [V(*s) for s in shards]
        + [V(*low_s), V(*x_s), dma((6,)), dma((6,))],
        [hbm, hbm, vmem] + [hbm] * 4,
        [hbm] * 6 + [vmem] * 9,
    )
    g1, s1, gbq, gbv, gbo, g2, s2, gbp, gbfc = small_grads
    return act, tokens_grad, g1, s1, gqkv, gbq, gbv, gout, gbo, g2, s2, gfc, gbfc, gproj, gbp


def as_sent(shard):
    return jax.tree.map(lambda a: a.astype(jnp.bfloat16) if a.dtype == jnp.float32 else a, shard)


def normalize(x, gain, shift):
    centre = x - jnp.mean(x, axis=-1, keepdims=True)
    spread = jnp.mean(centre * centre, axis=-1, keepdims=True)
    return centre * lax.rsqrt(spread + EPSILON) * gain + shift


def smooth(inner):
    return jax.nn.gelu(inner, approximate=True)


def visible(doc):
    count = doc.shape[0]
    row = lax.broadcasted_iota(jnp.int32, (count, count), 0)
    col = lax.broadcasted_iota(jnp.int32, (count, count), 1)
    same = doc[:, None] == doc[None, :]
    return same & (col <= row) & ((doc[None, :] != 0) | (row == col))


def plain_forward(x, weights, mask):
    (
        gain_one,
        shift_one,
        w_qkv,
        bias_query,
        bias_value,
        w_out,
        bias_out,
        gain_two,
        shift_two,
        w_fc,
        bias_fc,
        w_proj,
        bias_proj,
    ) = weights
    width = w_qkv.shape[0]
    count = x.shape[0]
    scale = HEAD_DIM ** (-0.5)
    f32 = jnp.float32
    h_one = normalize(x, gain_one.astype(f32), shift_one.astype(f32)).astype(jnp.bfloat16)
    qkv_bias = jnp.concatenate(
        [bias_query.astype(f32), jnp.zeros((width,), f32), bias_value.astype(f32)]
    )
    packed = (jnp.dot(h_one, w_qkv, preferred_element_type=f32) + qkv_bias).astype(jnp.bfloat16)
    query = packed[:, :width].reshape(count, HEADS, HEAD_DIM)
    key = packed[:, width : 2 * width].reshape(count, HEADS, HEAD_DIM)
    value = packed[:, 2 * width :].reshape(count, HEADS, HEAD_DIM)
    scores = jnp.einsum("thd,shd->hts", query, key, preferred_element_type=f32) * scale
    scores = jnp.where(mask[None], scores, -1e30)
    probs = jax.nn.softmax(scores, axis=-1)
    probs_low = probs.astype(jnp.bfloat16)
    mixed = jnp.einsum("hts,shd->thd", probs_low, value, preferred_element_type=f32)
    mixed = mixed.reshape(count, width).astype(jnp.bfloat16)
    middle = x + (jnp.dot(mixed, w_out, preferred_element_type=f32) + bias_out.astype(f32))
    h_two = normalize(middle, gain_two.astype(f32), shift_two.astype(f32)).astype(jnp.bfloat16)
    inner = jnp.dot(h_two, w_fc, preferred_element_type=f32) + bias_fc.astype(f32)
    active = smooth(inner).astype(jnp.bfloat16)
    result = middle + (jnp.dot(active, w_proj, preferred_element_type=f32) + bias_proj.astype(f32))
    kept = (h_one, query, key, value, probs, probs_low, mixed, middle, h_two, inner, active)
    return (result, kept)


def plain_backward(x, weights, mask, grad):
    (
        gain_one,
        shift_one,
        w_qkv,
        bias_query,
        bias_value,
        w_out,
        bias_out,
        gain_two,
        shift_two,
        w_fc,
        bias_fc,
        w_proj,
        bias_proj,
    ) = weights
    result, kept = plain_forward(x, weights, mask)
    h_one, query, key, value, probs, probs_low, mixed, middle, h_two, inner, active = kept
    width = w_qkv.shape[0]
    count = x.shape[0]
    scale = HEAD_DIM ** (-0.5)
    f32 = jnp.float32
    grad_branch = grad.astype(jnp.bfloat16)
    g_wproj = jnp.einsum("tf,td->fd", active, grad_branch, preferred_element_type=f32)
    g_bproj = jnp.sum(grad_branch.astype(f32), axis=0)
    d_active = jnp.einsum("td,fd->tf", grad_branch, w_proj, preferred_element_type=f32)
    unused, pull_smooth = jax.vjp(smooth, inner)
    d_inner = pull_smooth(d_active)[0].astype(jnp.bfloat16)
    g_wfc = jnp.einsum("td,tf->df", h_two, d_inner, preferred_element_type=f32)
    g_bfc = jnp.sum(d_inner.astype(f32), axis=0)
    d_htwo = jnp.einsum("tf,df->td", d_inner, w_fc, preferred_element_type=f32)
    unused, pull_two = jax.vjp(normalize, middle, gain_two.astype(f32), shift_two.astype(f32))
    d_mid, g_gain2, g_shift2 = pull_two(d_htwo)
    d_middle = grad + d_mid
    d_attn = d_middle.astype(jnp.bfloat16)
    g_wout = jnp.einsum("td,te->de", mixed, d_attn, preferred_element_type=f32)
    g_bout = jnp.sum(d_attn.astype(f32), axis=0)
    d_mixed = jnp.einsum("te,de->td", d_attn, w_out, preferred_element_type=f32).astype(
        jnp.bfloat16
    )
    d_mixed = d_mixed.reshape(count, HEADS, HEAD_DIM)
    d_probs = jnp.einsum("thd,shd->hts", d_mixed, value, preferred_element_type=f32)
    d_value = jnp.einsum("hts,thd->shd", probs_low, d_mixed, preferred_element_type=f32)
    d_scores = probs * (d_probs - jnp.sum(d_probs * probs, axis=-1, keepdims=True))
    d_scores = d_scores.astype(jnp.bfloat16)
    d_query = jnp.einsum("hts,shd->thd", d_scores, key, preferred_element_type=f32) * scale
    d_key = jnp.einsum("hts,thd->shd", d_scores, query, preferred_element_type=f32) * scale
    d_packed = jnp.concatenate(
        [d_query.reshape(count, width), d_key.reshape(count, width), d_value.reshape(count, width)],
        axis=1,
    ).astype(jnp.bfloat16)
    g_wqkv = jnp.einsum("td,te->de", h_one, d_packed, preferred_element_type=f32)
    column_sums = jnp.sum(d_packed.astype(f32), axis=0)
    g_bquery = column_sums[:width]
    g_bvalue = column_sums[2 * width :]
    d_hone = jnp.einsum("te,de->td", d_packed, w_qkv, preferred_element_type=f32)
    unused, pull_one = jax.vjp(normalize, x, gain_one.astype(f32), shift_one.astype(f32))
    d_input, g_gain1, g_shift1 = pull_one(d_hone)
    terms = (
        g_gain1,
        g_shift1,
        g_wqkv,
        g_bquery,
        g_bvalue,
        g_wout,
        g_bout,
        g_gain2,
        g_shift2,
        g_wfc,
        g_bfc,
        g_wproj,
        g_bproj,
    )
    return (d_middle + d_input, terms)


def plain_body(
    tokens,
    doc_ids,
    cotangent,
    norm1_gain,
    norm1_shift,
    qkv_weight,
    query_bias,
    value_bias,
    out_weight,
    out_bias,
    norm2_gain,
    norm2_shift,
    fc_weight,
    fc_bias,
    proj_weight,
    proj_bias,
):
    shards = (
        norm1_gain,
        norm1_shift,
        qkv_weight,
        query_bias,
        value_bias,
        out_weight,
        out_bias,
        norm2_gain,
        norm2_shift,
        fc_weight,
        fc_bias,
        proj_weight,
        proj_bias,
    )
    mask = visible(doc_ids)

    def fetch():
        return (
            lax.all_gather(shards[0], "own", axis=0, tiled=True),
            lax.all_gather(shards[1], "own", axis=0, tiled=True),
            lax.all_gather(shards[2], "own", axis=0, tiled=True),
            lax.all_gather(shards[3], "own", axis=0, tiled=True),
            lax.all_gather(shards[4], "own", axis=0, tiled=True),
            lax.all_gather(shards[5], "own", axis=0, tiled=True),
            lax.all_gather(shards[6], "own", axis=0, tiled=True),
            lax.all_gather(shards[7], "own", axis=0, tiled=True),
            lax.all_gather(shards[8], "own", axis=0, tiled=True),
            lax.all_gather(shards[9], "own", axis=0, tiled=True),
            lax.all_gather(shards[10], "own", axis=0, tiled=True),
            lax.all_gather(shards[11], "own", axis=0, tiled=True),
            lax.all_gather(shards[12], "own", axis=0, tiled=True),
        )

    current = tokens.astype(jnp.float32)
    saved = []
    for use in range(USES):
        saved.append(current)
        current, kept = plain_forward(current, fetch(), mask)
    grad = cotangent.astype(jnp.float32)
    summed = None
    for use in reversed(range(USES)):
        grad, terms = plain_backward(saved[use], fetch(), mask, grad)
        if summed is None:
            summed = terms
        else:
            summed = tuple((first + second for first, second in zip(summed, terms)))
    owned = (
        lax.psum_scatter(summed[0], "own", scatter_dimension=0, tiled=True),
        lax.psum_scatter(summed[1], "own", scatter_dimension=0, tiled=True),
        lax.psum_scatter(summed[2], "own", scatter_dimension=0, tiled=True),
        lax.psum_scatter(summed[3], "own", scatter_dimension=0, tiled=True),
        lax.psum_scatter(summed[4], "own", scatter_dimension=0, tiled=True),
        lax.psum_scatter(summed[5], "own", scatter_dimension=0, tiled=True),
        lax.psum_scatter(summed[6], "own", scatter_dimension=0, tiled=True),
        lax.psum_scatter(summed[7], "own", scatter_dimension=0, tiled=True),
        lax.psum_scatter(summed[8], "own", scatter_dimension=0, tiled=True),
        lax.psum_scatter(summed[9], "own", scatter_dimension=0, tiled=True),
        lax.psum_scatter(summed[10], "own", scatter_dimension=0, tiled=True),
        lax.psum_scatter(summed[11], "own", scatter_dimension=0, tiled=True),
        lax.psum_scatter(summed[12], "own", scatter_dimension=0, tiled=True),
    )
    final = jax.tree.map(lambda part: part.astype(jnp.float32), lax.psum(as_sent(owned), "grp"))
    return (current.astype(jnp.bfloat16), grad) + tuple(final)


def solution(mesh):
    return jax.shard_map(
        kernels_body if tuple(mesh.axis_sizes) == (4, 8) else plain_body,
        mesh=mesh,
        in_specs=(
            P(("grp", "own"), None),
            P(("grp", "own")),
            P(("grp", "own"), None),
            P("own"),
            P("own"),
            P("own", None),
            P("own"),
            P("own"),
            P("own", None),
            P("own"),
            P("own"),
            P("own"),
            P("own", None),
            P("own"),
            P("own", None),
            P("own"),
        ),
        out_specs=(
            P(("grp", "own"), None),
            P(("grp", "own"), None),
            P("own"),
            P("own"),
            P("own", None),
            P("own"),
            P("own"),
            P("own", None),
            P("own"),
            P("own"),
            P("own"),
            P("own", None),
            P("own"),
            P("own", None),
            P("own"),
        ),
        check_vma=False,
    )
```

```python
import functools

import jax
import jax.numpy as jnp
from jax import lax
from jax.experimental import pallas as pl
from jax.experimental.pallas import tpu as pltpu
from jax.sharding import PartitionSpec as P

HEADS = 12
HEAD_DIM = 64
USES = 2
EPSILON = 1e-05
SCALE = HEAD_DIM ** (-0.5)
TANH_SCALE = 0.7978845608028654
TANH_CUBIC = 0.044715
MESH = pl.DeviceIdType.MESH
f32 = jnp.float32
bf16 = jnp.bfloat16

GAIN1, SHIFT1, BIAS_Q, BIAS_V, BIAS_OUT, GAIN2, SHIFT2, BIAS_PROJ, BIAS_FC = range(9)


def dot(a, b, ca=1, cb=0):
    return lax.dot_general(a, b, (((ca,), (cb,)), ((), ())), preferred_element_type=f32)


def loop(count, body):
    def step(i, carry):
        body(i)
        return carry

    lax.fori_loop(0, count, step, 0)


def span(begin, end, body):
    def step(i, carry):
        body(i)
        return carry

    lax.fori_loop(begin, end, step, 0)


def part(i, size):
    return pl.ds(pl.multiple_of(i * size, size), size)


def centred(x):
    centre = x - jnp.mean(x, axis=-1, keepdims=True)
    spread = jnp.mean(centre * centre, axis=-1, keepdims=True)
    return centre, lax.rsqrt(spread + EPSILON)


def norm_forward(x, gain, shift, h, unroll=True):
    rows = 128

    def step(i):
        these = pl.ds(i * rows, rows) if unroll else part(i, rows)
        centre, r = centred(x[these, :].astype(f32))
        h[these, :] = (centre * r * gain + shift).astype(bf16)

    if unroll:
        for i in range(x.shape[0] // rows):
            step(i)
    else:
        loop(x.shape[0] // rows, step)


def norm_backward(x, dh, gain, grad, out, sums, gain_row, shift_row, low=None):
    rows = 128

    def step(i):
        these = pl.ds(i * rows, rows)
        centre, r = centred(x[these, :].astype(f32))
        n = centre * r
        d = dh[these, :]
        sums[gain_row : gain_row + 1, :] += jnp.sum(d * n, axis=0, keepdims=True)
        sums[shift_row : shift_row + 1, :] += jnp.sum(d, axis=0, keepdims=True)
        e = d * gain
        inner = e - jnp.mean(e, axis=-1, keepdims=True) - n * jnp.mean(e * n, axis=-1, keepdims=True)
        result = grad[these, :].astype(f32) + r * inner
        out[these, :] = result
        if low is not None:
            low[these, :] = result.astype(bf16)

    for i in range(x.shape[0] // rows):
        step(i)


def column_sum(x):
    return jnp.sum(x.astype(f32), axis=0, keepdims=True)


def make_mask(doc, mask):
    count = doc.shape[1]
    half = count // 2
    ids = doc[0:1, :].astype(f32)
    keys = jnp.broadcast_to(ids, (128, count)).T[:, :1]
    for k0, q0, place in ((0, 0, 0), (half, half, count)):
        width = count - q0
        row = lax.broadcasted_iota(jnp.int32, (half, width), 0) + k0
        col = lax.broadcasted_iota(jnp.int32, (half, width), 1) + q0
        key = keys[k0 : k0 + half]
        same = (key == ids[:, q0:]) & (row <= col) & ((key != 0.0) | (row == col))
        mask[:, place : place + width] = jnp.where(same, 0.0, -1e30)


def head_lanes(h, x):
    lane = lax.broadcasted_iota(jnp.int32, (1, 2 * HEAD_DIM), 1)
    keep = (lane < HEAD_DIM) if h == 0 else (lane >= HEAD_DIM)
    return jnp.where(keep, x, jnp.zeros_like(x))


def attention_forward(qkv, mask, probs, o, begin=0, end=6, shift=0):
    count, width = o.shape
    half = count // 2
    pair = 2 * HEAD_DIM

    def step(i):
        col = pl.ds(i * pair, pair)
        q = qkv[:, col]
        k = qkv[:, pl.ds(width + i * pair, pair)]
        v = qkv[:, pl.ds(2 * width + i * pair, pair)]
        vt = v.T
        outs = []
        for h in range(2):
            kh = head_lanes(h, k)
            s0 = dot(kh[:half], q, 1, 1) + mask[:, :count]
            s1 = dot(kh[half:], q[half:], 1, 1) + mask[:, count:]
            m0 = jnp.max(s0, axis=0, keepdims=True)
            m1 = jnp.max(s1, axis=0, keepdims=True)
            top = jnp.concatenate([m0[:, :half], jnp.maximum(m0[:, half:], m1)], axis=1)
            e0 = jnp.exp(s0 - top)
            e1 = jnp.exp(s1 - top[:, half:])
            l0 = jnp.sum(e0, axis=0, keepdims=True)
            l1 = jnp.sum(e1, axis=0, keepdims=True)
            r = 1.0 / jnp.concatenate([l0[:, :half], l0[:, half:] + l1], axis=1)
            p0 = (e0 * r).astype(bf16)
            p1 = (e1 * r[:, half:]).astype(bf16)
            row = pl.ds(h * half, half)
            probs[i - shift, row, :count] = p0
            probs[i - shift, row, count:] = p1
            vh = vt[h * HEAD_DIM : (h + 1) * HEAD_DIM]
            first = dot(vh[:, :half], p0)
            second = dot(vh[:, half:], p1)
            outs.append(jnp.concatenate([first[:, :half], first[:, half:] + second], axis=1))
        o[:, col] = jnp.concatenate(outs, axis=0).astype(bf16).T

    for i in range(begin, end):
        step(i)


def attention_backward(qkv, probs, do, dz, begin=0, end=6, shift=0):
    count, width = do.shape
    half = count // 2
    pair = 2 * HEAD_DIM

    def step(i):
        cq = pl.ds(i * pair, pair)
        ck = pl.ds(width + i * pair, pair)
        cv = pl.ds(2 * width + i * pair, pair)
        q, k, v, d = qkv[:, cq], qkv[:, ck], qkv[:, cv], do[:, cq]
        dq = dk = dv = None
        for h in range(2):
            dh, kh, qh = head_lanes(h, d), head_lanes(h, k), head_lanes(h, q)
            row = pl.ds(h * half, half)
            p0 = probs[i - shift, row, :count]
            p1 = probs[i - shift, row, count:]
            d0 = dot(v[:half], dh, 1, 1)
            d1 = dot(v[half:], dh[half:], 1, 1)
            w0 = p0.astype(f32)
            w1 = p1.astype(f32)
            t0 = jnp.sum(d0 * w0, axis=0, keepdims=True)
            t1 = jnp.sum(d1 * w1, axis=0, keepdims=True)
            t = jnp.concatenate([t0[:, :half], t0[:, half:] + t1], axis=1)
            s0 = (w0 * (d0 - t)).astype(bf16)
            s1 = (w1 * (d1 - t[:, half:])).astype(bf16)
            v_term = jnp.concatenate([dot(p0, dh), dot(p1, dh[half:])], axis=0)
            k_term = jnp.concatenate([dot(s0, qh), dot(s1, qh[half:])], axis=0)
            qa = dot(s0, kh[:half], 0, 0)
            qb = dot(s1, kh[half:], 0, 0)
            q_term = jnp.concatenate([qa[:half], qa[half:] + qb], axis=0)
            dq = q_term if dq is None else dq + q_term
            dk = k_term if dk is None else dk + k_term
            dv = v_term if dv is None else dv + v_term
        dq = (dq * SCALE).astype(bf16)
        dv = dv.astype(bf16)
        dz[:, cq] = dq
        dz[:, ck] = dk.astype(bf16)
        dz[:, cv] = dv

    for i in range(begin, end):
        step(i)


def small(block, row):
    return block[row : row + 1, :]


def hidden_tile(h2, weight, bias, f, slope, i):
    count, width = h2.shape
    rows = 128
    third = f.shape[2] // 8
    for first in range(0, count, rows):
        these = pl.ds(first, rows)
        u = dot(h2[these, :], weight) + bias
        square = u * u
        t = jnp.tanh(u * (TANH_SCALE + (TANH_SCALE * TANH_CUBIC) * square))
        rise = 0.5 + 0.5 * t
        active = (u * rise).astype(bf16)
        for place in range(width // third):
            owner = i * (width // third // 3) + place // 3
            f[place % 3, these, part(owner, third)] = active[:, place * third : (place + 1) * third]
        inner = TANH_SCALE + (3.0 * TANH_SCALE * TANH_CUBIC) * square
        slope[these, part(i, width)] = (rise + (0.5 * u) * (1.0 - t * t) * inner).astype(bf16)


def hidden_forward(h2, wfc, block, f, slope, begin, end):
    width = h2.shape[1]

    def hidden(i):
        hidden_tile(h2, wfc[:, part(i, width)], block[pl.ds(BIAS_FC + i, 1), :], f, slope, i)

    span(begin, end, hidden)


def project(f, wproj, i):
    third = f.shape[2] // 8
    rows = [wproj[pl.ds((owner * 3 + i) * third, third), :] for owner in range(8)]
    return dot(f[i], jnp.concatenate(rows, axis=0))


def coords():
    own = lax.axis_index("own")
    return lax.axis_index("grp"), own // 2, lax.rem(own, 2)


class Unit:
    def __init__(self, shard, full, row, rows, col, cols, shared=True):
        self.shard, self.full, self.shared = shard, full, shared
        self.row, self.rows, self.col, self.cols = row, rows, col, cols

    def mine(self, half=None):
        rows = self.rows if half is None else self.rows // 2
        start = self.row + (0 if half is None else half * rows)
        return self.shard.at[pl.ds(start, rows), pl.ds(self.col, self.cols)]

    def block(self, owner, half=None):
        rows = self.rows if half is None else self.rows // 2
        start = owner * self.shard.shape[0] + self.row + (0 if half is None else half * rows)
        return self.full.at[pl.ds(pl.multiple_of(start, 16), rows), pl.ds(self.col, self.cols)]


PIECES = [(1, 0), (1, 1), (2, 0), (2, 1), (3, 0), (3, 1)]


class Gather:
    def __init__(self, units, link_send, link_recv, core_send, core_recv, own_sem):
        self.units = units
        self.link_send, self.link_recv = link_send, link_recv
        self.core_send, self.core_recv, self.own_sem = core_send, core_recv, own_sem
        self.grp, self.chip, self.core = coords()
        self.odd = lax.rem(self.grp, 2)
        self.sent = []

    def owner(self, offset):
        return jnp.bitwise_xor(self.chip, offset) * 2 + self.core

    def device(self, chip_offset, along_z=False):
        own = jnp.bitwise_xor(self.chip, chip_offset) * 2 + self.core
        grp = self.grp + 1 - 2 * self.odd if along_z else self.grp
        return (grp, own)

    def link(self, k, src, dst, piece, out, device):
        return pltpu.make_async_remote_copy(
            src_ref=src,
            dst_ref=dst,
            send_sem=self.link_send.at[k, out],
            recv_sem=self.link_recv.at[k, piece],
            device_id=device,
            device_id_type=MESH,
        )

    def across(self, k, src, dst, slot):
        return pltpu.make_async_remote_copy(
            src_ref=src,
            dst_ref=dst,
            send_sem=self.core_send.at[k, slot],
            recv_sem=self.core_recv.at[k, slot],
            device_id=(self.grp, self.chip * 2 + 1 - self.core),
            device_id_type=MESH,
        )

    def own(self, k):
        unit = self.units[k]
        return pltpu.make_async_copy(unit.mine(), unit.block(self.owner(0)), self.own_sem.at[k])

    def first(self, k, offset, half, out):
        unit = self.units[k]
        piece = PIECES.index((offset, half))
        return self.link(
            k, unit.mine(half), unit.block(self.owner(0), half), piece, out, self.device(offset)
        )

    def relay(self, k, offset, half, way, out):
        unit = self.units[k]
        piece = unit.block(self.owner(offset), half)
        return self.link(k, piece, piece, PIECES.index((3, half)), out, self.device(way))

    def pair(self, k, offset, half, out):
        unit = self.units[k]
        piece = unit.block(self.owner(offset), half)
        return self.link(k, piece, piece, PIECES.index((offset, half)), out, self.device(0, True))

    def hand(self, k, offset, half):
        unit = self.units[k]
        piece = unit.block(self.owner(offset), half)
        return self.across(k, piece, piece, PIECES.index((offset, half)))

    def arrived(self, k, offset, half):
        unit = self.units[k]
        piece = unit.block(self.owner(offset), half)
        self.link(k, piece, piece, PIECES.index((offset, half)), 0, self.device(1)).wait_recv()

    def sends(self, k, odd):
        own = [(1, 0), (2, 1), (1, 1), (2, 0)]
        if not self.units[k].shared:
            own = [(2, 0), (1, 1), (1, 0), (2, 1)]
        elif odd:
            own = [(1, 1), (2, 0)]
        calls = [functools.partial(self.first, k, *what) for what in own]
        if odd or not self.units[k].shared:
            calls += [functools.partial(self.relay, k, *what) for what in ((2, 0, 1), (1, 1, 2))]
        if self.units[k].shared:
            pairs = ((3, 0), (3, 1)) if odd else ((1, 0), (2, 1))
            calls += [functools.partial(self.pair, k, *what) for what in pairs]
        return len(own), [functools.partial(call, out) for out, call in enumerate(calls)]

    def each_kind(self, k, body):
        if not self.units[k].shared:
            body(True)
            return

        @pl.when(self.odd == 0)
        def _():
            body(False)

        @pl.when(self.odd == 1)
        def _():
            body(True)

    def start(self, k):
        def body(odd):
            own, calls = self.sends(k, odd)
            for call in calls[:own]:
                call().start()

        self.each_kind(k, body)
        unit = self.units[k]
        self.across(k, unit.mine(), unit.block(self.owner(0)), len(PIECES)).start()
        self.own(k).start()

    def serve(self, k, odd, pieces, then):
        for piece in pieces:
            self.arrived(k, *piece)
            if piece in then:
                then[piece]().start()
            self.hand(k, *piece).start()

    def serve_first(self, k):
        def body(odd):
            own, calls = self.sends(k, odd)
            if odd:
                then = {(2, 0): calls[own], (1, 1): calls[own + 1]}
                self.serve(k, odd, ((2, 0), (1, 1)), then)
            else:
                then = {(1, 0): calls[own], (2, 1): calls[own + 1]}
                self.serve(k, odd, ((1, 0), (2, 1), (1, 1), (2, 0)), then)

        self.each_kind(k, body)

    def serve_second(self, k):
        def body(odd):
            own, calls = self.sends(k, odd)
            if not self.units[k].shared:
                self.serve(k, odd, ((1, 0), (2, 1), (3, 0), (3, 1)), {})
            elif odd:
                then = {(3, 0): calls[own + 2], (3, 1): calls[own + 3]}
                self.serve(k, odd, ((3, 0), (3, 1), (1, 0), (2, 1)), then)
            else:
                self.serve(k, odd, ((3, 0), (3, 1)), {})

        self.each_kind(k, body)

    def finish(self, k):
        unit = self.units[k]
        other = 1 - 2 * self.core
        self.own(k).wait()
        whole = unit.block(self.owner(0) + other)
        self.across(k, whole, whole, len(PIECES)).wait_recv()
        for slot, (offset, half) in enumerate(PIECES):
            piece = unit.block(self.owner(offset) + other, half)
            self.across(k, piece, piece, slot).wait_recv()

    def drain(self, k):
        def body(odd):
            own, calls = self.sends(k, odd)
            for call in calls:
                call().wait_send()

        self.each_kind(k, body)
        unit = self.units[k]
        self.across(k, unit.mine(), unit.block(self.owner(0)), len(PIECES)).wait_send()
        for offset, half in PIECES:
            self.hand(k, offset, half).wait_send()


def store(copies, sem, src, dst):
    copy = pltpu.make_async_copy(src, dst, sem.at[len(copies)])
    copy.start()
    copies.append(copy)


def first_kernel(
    tokens, doc, packed, sqkv, sout, sfc, sproj,
    x2_out, block_out, mask_out, w_out,
    h1_out, qkv_out, probs_out, o_out, x1_out, h2_out, slope_out, f_out,
    wqkv, wout, wfc, wproj, block, mask, h1, qkv, probs, o, x1, h2, slope, f, x2, many,
    link_send, link_recv, core_send, core_recv, own_sem, small_send, small_recv, out_sem,
):
    grp, chip, core = coords()
    me = chip * 2 + core
    width = tokens.shape[1]
    barrier = pltpu.get_barrier_semaphore()
    peers = [(grp, jnp.bitwise_xor(me, j)) for j in range(1, 8)]
    peers.append((grp + 1 - 2 * lax.rem(grp, 2), me))
    for peer in peers:
        pl.semaphore_signal(barrier, inc=1, device_id=peer, device_id_type=MESH)
    pl.semaphore_wait(barrier, len(peers))

    units = [Unit(sqkv, wqkv, 0, sqkv.shape[0], i * width, width) for i in range(3)]
    units += [Unit(sout, wout, 0, sout.shape[0], 0, width)]
    units += [Unit(sfc, wfc, 0, sfc.shape[0], i * width, width) for i in range(sfc.shape[1] // width)]
    thirds = sproj.shape[0] // 3
    units += [Unit(sproj, wproj, i * thirds, thirds, 0, width, False) for i in range(3)]
    gather = Gather(units, link_send, link_recv, core_send, core_recv, own_sem)
    count = len(units)

    def small_copy(j):
        return pltpu.make_async_remote_copy(
            src_ref=packed,
            dst_ref=many.at[me],
            send_sem=small_send.at[j - 1],
            recv_sem=small_recv.at[j - 1],
            device_id=(grp, jnp.bitwise_xor(me, j)),
            device_id_type=MESH,
        )

    for j in range(1, 8):
        small_copy(j).start()
    gather.start(0)
    gather.start(1)
    copies = []

    def slot(s):
        if s < count:
            gather.serve_first(s)
        if s + 2 < count:
            gather.start(s + 2)
        if 0 <= s - 2 < count:
            gather.serve_second(s - 2)
        if 0 <= s - 3 < count:
            gather.finish(s - 3)

    make_mask(doc, mask)
    store(copies, out_sem, mask, mask_out)
    slot(0)
    many[me] = packed[...]
    for j in range(1, 8):
        small_copy(j).wait_recv()
    lanes = packed.shape[1]
    size, ff_size = sqkv.shape[0], sproj.shape[0]
    block[12:16, :] = jnp.zeros((4, width), f32)
    for owner in range(8):
        rows = many[owner].astype(f32)
        block[:8, owner * size : (owner + 1) * size] = rows[:8, :size]
        row, col = BIAS_FC + owner * ff_size // width, owner * ff_size % width
        for j in range(ff_size // lanes):
            block[row : row + 1, col + j * lanes : col + (j + 1) * lanes] = rows[8 + j : 9 + j, :]
    store(copies, out_sem, block, block_out)
    slot(1)
    norm_forward(tokens, small(block, GAIN1), small(block, SHIFT1), h1, False)
    store(copies, out_sem, h1, h1_out)
    slot(2)
    slot(3)
    qkv[:, :width] = (dot(h1[...], wqkv[:, :width]) + small(block, BIAS_Q)).astype(bf16) * SCALE
    slot(4)
    qkv[:, width : 2 * width] = dot(h1[...], wqkv[:, width : 2 * width]).astype(bf16)
    slot(5)
    for i in range(3):
        store(copies, out_sem, wqkv.at[:, pl.ds(i * width, width)], w_out.at[i])
    qkv[:, 2 * width :] = (dot(h1[...], wqkv[:, 2 * width :]) + small(block, BIAS_V)).astype(bf16)
    store(copies, out_sem, qkv, qkv_out)
    attention_forward(qkv, mask, probs, o, 0, 1)
    slot(6)
    store(copies, out_sem, wout, w_out.at[3])
    attention_forward(qkv, mask, probs, o, 1, 3)
    slot(7)
    attention_forward(qkv, mask, probs, o, 3, 5)
    slot(8)
    attention_forward(qkv, mask, probs, o, 5, 6)
    store(copies, out_sem, probs, probs_out)
    store(copies, out_sem, o, o_out)
    x1[...] = tokens[...].astype(f32) + (dot(o[...], wout[...]) + small(block, BIAS_OUT))
    norm_forward(x1, small(block, GAIN2), small(block, SHIFT2), h2, False)
    store(copies, out_sem, x1, x1_out)
    store(copies, out_sem, h2, h2_out)
    slot(9)
    hidden_forward(h2, wfc, block, f, slope, 0, 2)
    slot(10)
    fc_tiles = wfc.shape[1] // width
    for i in range(fc_tiles):
        store(copies, out_sem, wfc.at[:, pl.ds(i * width, width)], w_out.at[4 + i])
    hidden_forward(h2, wfc, block, f, slope, 2, 4)
    store(copies, out_sem, f, f_out)
    store(copies, out_sem, slope, slope_out)

    slot(11)
    x2[...] = x1[...] + (project(f, wproj, 0) + small(block, BIAS_PROJ))
    slot(12)
    x2[...] += project(f, wproj, 1)
    slot(13)
    for i in range(fc_tiles):
        store(copies, out_sem, wproj.at[pl.ds(i * width, width), :], w_out.at[4 + fc_tiles + i])
    x2[...] += project(f, wproj, 2)
    store(copies, out_sem, x2, x2_out)
    for k in range(count):
        gather.drain(k)
    for j in range(1, 8):
        small_copy(j).wait_send()
    for copy in copies:
        copy.wait()


def second_kernel(
    x2_in, tokens_in, cot_in, mask_in, block, w_in, w_parts_in, w_thirds_in,
    h1a_in, qkv_in, probs_in, oa_in, x1_in, h2a_in, slope_in, fa_in,
    act_out, grad_out, sums_out, gqkv_out, gout_out, gfc_out, gproj_out,
    x, tokens, cot, grad, x1, dh, tiles, h1a, qkv, oa, h2a, slope, h1b, dzb, ob, h2b, dub, shared, more_probs,
    gm, da, dab, sums,
    buf_p, buf_o, recv_p, recv_o, hop1_p, hop1_o, hop2_p, hop2_o, zmid_p, zmid_o, tot_p, tot_o,
    small_in, small_tot,
    in_sem, tile_sem, out_sem, send, recv, small_send, small_recv,
):
    grp, chip, core = coords()
    yy, xx = chip // 2, lax.rem(chip, 2)
    me = chip * 2 + core
    width = x.shape[1]
    loads = {}

    def load(name, src, dst):
        copy = pltpu.make_async_copy(src, dst, in_sem.at[len(loads)])
        copy.start()
        loads[name] = copy

    fb, fa = shared.at[pl.ds(0, 3)], shared.at[pl.ds(3, 3)]
    probs = shared.at[:, :, pl.ds(0, probs_in.shape[2])]
    some_probs = shared.at[pl.ds(3, 3), :, pl.ds(0, probs_in.shape[2])]
    half = x.shape[0] // 2
    mask = dh.at[pl.ds(0, half), :]
    load("x", x2_in, x)

    ff_tiles = w_in.shape[0] - 8
    ring = tiles.shape[0]
    fc_at, proj_at = 4, 4 + ff_tiles
    order = [proj_at + t for t in range(ff_tiles)] + [fc_at + t for t in range(ff_tiles)] + [3, 0, 1, 2]

    def tile_copy(t):
        return pltpu.make_async_copy(w_in.at[order[t]], tiles.at[t % ring], tile_sem.at[t % ring])

    def tile(t):
        tile_copy(t).wait()
        return tiles[t % ring]

    def next_tile(t):
        if t + ring < len(order):
            tile_copy(t + ring).start()

    def square(value):
        return value.reshape(width, width)

    def resident(t):
        if t < 2:
            return square(buf_o[t])
        if t < 4:
            return jnp.concatenate(
                [buf_p[t - 2, 0].reshape(-1, width), buf_p[t - 2, 1, 0].reshape(-1, width)], axis=0
            )
        return square(recv_o[2 * (t - 4) : 2 * (t - 4) + 2])

    for t in range(2):
        load(f"w{t}", w_parts_in.at[t], buf_o.at[t])
    load("w2", w_thirds_in.at[2, pl.ds(0, 2)], buf_p.at[0, 0])
    load("w2b", w_thirds_in.at[2, 2], buf_p.at[0, 1, 0])
    load("mask", mask_in, mask)
    load("w3", w_thirds_in.at[3, pl.ds(0, 2)], buf_p.at[1, 0])
    load("w3b", w_thirds_in.at[3, 2], buf_p.at[1, 1, 0])
    for t in range(ff_tiles):
        load(f"w{fc_at + t}", w_parts_in.at[fc_at + t], recv_o.at[pl.ds(2 * t, 2)])
    for t in range(ring):
        tile_copy(t).start()
    core_peer = (grp, jnp.bitwise_xor(me, 1))
    x_peer = (grp, jnp.bitwise_xor(me, 2))
    y_peer = (grp, jnp.bitwise_xor(me, 4))
    low = grp == 1
    middle = (grp == 1) | (grp == 2)
    end = jnp.logical_not(middle)
    inward = (jnp.where(grp == 0, 1, 2), me)
    outward = (jnp.where(low, 0, 3), me)
    across = (jnp.where(low, 2, 1), me)

    barrier = pltpu.get_barrier_semaphore()

    def greet():
        for peer in (core_peer, x_peer, y_peer):
            pl.semaphore_signal(barrier, inc=1, device_id=peer, device_id_type=MESH)

        @pl.when(end)
        def _():
            pl.semaphore_signal(barrier, inc=1, device_id=inward, device_id_type=MESH)

        @pl.when(middle)
        def _():
            pl.semaphore_signal(barrier, inc=1, device_id=outward, device_id_type=MESH)
            pl.semaphore_signal(barrier, inc=1, device_id=across, device_id_type=MESH)

    def remote(src, dst, i, stage, peer):
        return pltpu.make_async_remote_copy(
            src_ref=src, dst_ref=dst, send_sem=send.at[i, stage], recv_sem=recv.at[i, stage],
            device_id=peer, device_id_type=MESH,
        )

    third_width = width // 3
    specs = [(True, 0, 0, width // 2), (True, 0, width // 2, width // 2), (True, 1, 0, width), (True, 2, 0, width)]
    projs = len(specs)
    specs += [(False, j, 0, width) for j in range(ff_tiles + 3)]
    specs += [(False, ff_tiles + 3, 0, 2 * third_width), (False, ff_tiles + 3, 2 * third_width, third_width)]
    chunks = len(specs)
    copies = []

    buffers = (
        (buf_p, buf_o), (recv_p, recv_o), (hop1_p, hop1_o), (hop2_p, hop2_o), (zmid_p, zmid_o),
        (tot_p, tot_o),
    )

    class Chunk:
        def __init__(self, i):
            self.i = i
            self.proj, self.at, col, self.width = specs[i]
            cols = pl.ds(col, self.width)
            sets = [pair[0 if self.proj else 1] for pair in buffers]
            ring = sets[0].shape[0]
            order = i if self.proj else i - projs
            self.previous = i - ring if order >= ring else None
            self.last = i + ring >= (projs if self.proj else chunks)
            self.rows = sets[1].shape[3]
            self.buf = sets[0].at[order % ring, :, :, :, :, cols]
            self.recv = sets[1].at[self.at, :, :, :, cols]
            self.hop1 = sets[2].at[self.at, :, :, :, cols]
            self.hop2, self.zmid, self.tot = (
                s.at[self.at, :, :, cols] if len(s.shape) == 4 else s.at[self.at, :, cols] for s in sets[3:]
            )
            half = self.rows // 2
            self.top, self.bottom = pl.ds(0, half), pl.ds(half, half)
            self.cols = cols

        def to_core(self):
            return remote(self.buf.at[1 - core], self.recv, self.i, 0, core_peer)

        def first(self):
            return (
                remote(self.recv.at[:, 1 - xx, self.top, :], self.hop1.at[0], self.i, 1, x_peer),
                remote(self.recv.at[1 - yy, :, self.bottom, :], self.hop1.at[1], self.i, 2, y_peer),
            )

        def second(self):
            return (
                remote(self.recv.at[1 - yy, xx, self.top, :], self.hop2.at[0], self.i, 3, y_peer),
                remote(self.recv.at[yy, 1 - xx, self.bottom, :], self.hop2.at[1], self.i, 4, x_peer),
            )

        def to_middle(self):
            return remote(self.recv.at[yy, xx], self.tot, self.i, 5, inward)

        def between(self):
            return remote(self.recv.at[yy, xx], self.zmid, self.i, 6, across)

        def to_end(self):
            return remote(self.tot, self.tot, self.i, 7, outward)

        def begin(self):
            if self.previous is not None:
                Chunk(self.previous).to_core().wait_send()

        def stage_b(self):
            self.to_core().wait_recv()
            self.recv[...] = self.recv[...] + self.buf[core]
            for copy in self.first():
                copy.start()

        def stage_c(self):
            for copy in self.first():
                copy.wait_recv()
            self.recv[:, xx, self.top, :] = self.recv[:, xx, self.top, :] + self.hop1[0]
            self.recv[yy, :, self.bottom, :] = self.recv[yy, :, self.bottom, :] + self.hop1[1]
            for copy in self.second():
                copy.start()

        def stage_d(self):
            for copy in self.second():
                copy.wait_recv()
            self.recv[yy, xx, self.top, :] = self.recv[yy, xx, self.top, :] + self.hop2[0]
            self.recv[yy, xx, self.bottom, :] = self.recv[yy, xx, self.bottom, :] + self.hop2[1]

            @pl.when(end)
            def _():
                self.to_middle().start()

        def stage_e(self):
            @pl.when(middle)
            def _():
                self.to_middle().wait_recv()
                self.recv[yy, xx] = self.recv[yy, xx] + self.tot[...]
                self.between().start()

        def stage_f(self):
            @pl.when(middle)
            def _():
                self.between().wait_recv()
                self.tot[...] = self.recv[yy, xx] + self.zmid[...]
                self.to_end().start()

        def stage_g(self):
            @pl.when(end)
            def _():
                self.to_end().wait_recv()

            if self.proj:
                place = gproj_out.at[pl.ds(self.at * self.rows, self.rows), self.cols]
            elif self.at < ff_tiles:
                place = gfc_out.at[:, pl.ds(self.at * width, width)]
            elif self.at == ff_tiles:
                place = gout_out
            else:
                place = gqkv_out.at[:, pl.ds((self.at - ff_tiles - 1) * width + specs[self.i][2], self.width)]
            store(copies, out_sem, self.tot, place)

        def finish(self):
            if self.last:
                self.to_core().wait_send()
            for copy in self.first() + self.second():
                copy.wait_send()

            @pl.when(end)
            def _():
                self.to_middle().wait_send()

            @pl.when(middle)
            def _():
                self.between().wait_send()
                self.to_end().wait_send()

    def made(i):
        Chunk(i).to_core().start()

    def proj_chunk(i):
        chunk = Chunk(i)
        chunk.begin()
        rows = chunk.rows
        yb, ya = cot[:, chunk.cols], gm[:, chunk.cols]
        for owner in range(8):
            col = pl.ds(owner * rows, rows)
            value = dot(fb[chunk.at, :, col], yb, 0, 0) + dot(fa[chunk.at, :, col], ya, 0, 0)
            chunk.buf[owner % 2, owner // 4, (owner // 2) % 2] = value.astype(bf16)
        made(i)

    def other_chunk(i, xa, ya, xb, yb, col):
        chunk = Chunk(i)
        chunk.begin()
        cols = pl.ds(col, chunk.width)
        rows = chunk.rows
        for first in (0, 4):
            these = pl.ds(first * rows, 4 * rows)
            value = dot(xa[:, these], ya[:, cols], 0, 0) + dot(xb[:, these], yb[:, cols], 0, 0)
            for at in range(4):
                owner = first + at
                piece = value[at * rows : (at + 1) * rows].astype(bf16)
                chunk.buf[owner % 2, owner // 4, (owner // 2) % 2] = piece
        made(i)

    def b(i):
        Chunk(i).stage_b()

    def period(k):
        if k < chunks:
            Chunk(k).stage_c()
        if 2 <= k + 2 < chunks:
            b(k + 2)
        for lag, name in ((1, "stage_d"), (2, "stage_e"), (3, "stage_f"), (5, "stage_g")):
            if 0 <= k - lag < chunks:
                getattr(Chunk(k - lag), name)()

    sums[...] = jnp.zeros_like(sums)
    loads["x"].wait()
    norm_forward(x, small(block, GAIN1), small(block, SHIFT1), h1b)
    for name in ("w0", "w1", "w2", "w2b"):
        loads[name].wait()
    for t, (bias, scale) in enumerate(((small(block, BIAS_Q), SCALE), (None, None), (small(block, BIAS_V), None))):
        z = dot(h1b[...], resident(t))
        z = z if bias is None else z + bias
        z = z.astype(bf16)
        dzb[:, t * width : (t + 1) * width] = z if scale is None else z * scale
    loads["mask"].wait()
    attention_forward(dzb, mask, some_probs, ob, 0, 3)
    load("cot", cot_in, cot)
    for name, src, dst in (
        ("h2a", h2a_in, h2a), ("slope", slope_in, slope), ("qkv", qkv_in, qkv), ("oa", oa_in, oa), ("h1a", h1a_in, h1a),
        ("tokens", tokens_in, tokens),
    ):
        load(name, src, dst)
    attention_forward(dzb, mask, more_probs, ob, 3, 6, 3)
    loads["w3"].wait()
    loads["w3b"].wait()
    for first in range(0, x.shape[0], 128):
        these = pl.ds(first, 128)
        x1[these, :] = x[these, :] + (dot(ob[these, :], resident(3)) + small(block, BIAS_OUT))
    norm_forward(x1, small(block, GAIN2), small(block, SHIFT2), h2b)
    for t in range(ff_tiles):
        loads[f"w{fc_at + t}"].wait()
    for t in range(ff_tiles):
        hidden_tile(h2b, resident(fc_at + t), block[BIAS_FC + t : BIAS_FC + t + 1, :], fb, dub, t)
    third = fb.shape[2] // 8

    def hidden_rows(t):
        owners = width // (3 * third)
        pieces = [
            fb[j, :, pl.ds((t * owners + owner) * third, third)] for owner in range(owners) for j in range(3)
        ]
        return jnp.concatenate(pieces, axis=1)

    for t in range(ff_tiles):
        tile_copy(t).wait()
    dh[...] = dot(hidden_rows(0), tiles[0])
    for t in range(1, ff_tiles):
        dh[...] += dot(hidden_rows(t), tiles[t])
    for first in range(0, x.shape[0], 128):
        these = pl.ds(first, 128)
        gm[these, :] = (x1[these, :] + (dh[these, :] + small(block, BIAS_PROJ))).astype(bf16)
    store(copies, out_sem, gm, act_out)

    def hidden_backward(g, held, t):
        cols = pl.ds(t * width, width)
        d = (dot(g[...], tiles[t], 1, 1) * held[:, cols].astype(f32)).astype(bf16)
        held[:, cols] = d

    def add_sums(row, second, first):
        sums[row : row + 1, :] += column_sum(second) + column_sum(first)

    def input_gradient(held, weights, first=0):
        for t, weight in enumerate(weights, first):
            term = dot(held[:, t * width : (t + 1) * width], weight(), 1, 1)
            dh[...] = term if t == 0 else dh[...] + term

    def residents(first, number):
        return [functools.partial(resident, first + t) for t in range(number)]

    def streamed(first, number):
        return [functools.partial(tile, first + t) for t in range(number)]

    loads["cot"].wait()
    for t in range(ff_tiles):
        hidden_backward(cot, dub, t)
    input_gradient(dub, residents(fc_at, ff_tiles))
    greet()
    norm_backward(x1, dh, small(block, GAIN2), cot, grad, sums, GAIN2, SHIFT2, dab)
    load("x1", x1_in, x1)
    da[...] = dot(dab[...], resident(3), 1, 1).astype(bf16)
    attention_backward(dzb, some_probs, da, dzb, 0, 3)
    load("fa", fa_in, fa)
    attention_backward(dzb, more_probs, da, dzb, 3, 6, 3)
    input_gradient(dzb, residents(0, 3))
    norm_backward(x, dh, small(block, GAIN1), grad, grad, sums, GAIN1, SHIFT1)

    copies[0].wait()
    gm[...] = grad[...].astype(bf16)

    @pl.when(end)
    def _():
        pl.semaphore_wait(barrier, 4)

    @pl.when(middle)
    def _():
        pl.semaphore_wait(barrier, 5)

    loads["fa"].wait()
    proj_chunk(0)
    proj_chunk(1)
    b(0)
    proj_chunk(2)
    b(1)
    loads["slope"].wait()
    hidden_backward(gm, slope, 0)
    next_tile(0)
    period(0)
    proj_chunk(3)
    load("probs", probs_in, probs)
    add_sums(BIAS_PROJ, cot[...], gm[...])
    hidden_backward(gm, slope, 1)
    next_tile(1)
    period(1)
    for t in range(2, ff_tiles):
        hidden_backward(gm, slope, t)
        next_tile(t)
    n = ff_tiles

    def fc_chunk(t):
        other_chunk(projs + t, h2a, slope, h2b, dub, t * width)
        cols = pl.ds(t * width, width)
        add_sums(BIAS_FC + t, dub[:, cols], slope[:, cols])

    loads["h2a"].wait()
    fc_chunk(0)
    input_gradient(slope, streamed(n, ff_tiles // 2))
    period(2)
    fc_chunk(1)
    input_gradient(slope, streamed(n + ff_tiles // 2, ff_tiles // 2), ff_tiles // 2)
    for t in range(ff_tiles):
        next_tile(n + t)
    n += ff_tiles
    loads["x1"].wait()
    norm_backward(x1, dh, small(block, GAIN2), grad, grad, sums, GAIN2, SHIFT2, da)
    period(3)
    fc_chunk(2)
    do = cot
    do[...] = dot(da[...], tile(n), 1, 1).astype(bf16)
    n += 1
    add_sums(BIAS_OUT, dab[...], da[...])
    loads["qkv"].wait()
    loads["probs"].wait()
    attention_backward(qkv, probs, do, qkv, 0, 1)
    period(4)
    fc_chunk(3)
    attention_backward(qkv, probs, do, qkv, 1, 3)
    period(5)
    loads["oa"].wait()
    other_chunk(8, oa, da, ob, dab, 0)
    attention_backward(qkv, probs, do, qkv, 3, 5)
    period(6)
    attention_backward(qkv, probs, do, qkv, 5, 6)
    loads["h1a"].wait()
    other_chunk(9, h1a, qkv, h1b, dzb, 0)
    add_sums(BIAS_Q, dzb[:, :width], qkv[:, :width])
    period(7)
    other_chunk(10, h1a, qkv, h1b, dzb, width)
    input_gradient(qkv, streamed(n, 3))
    period(8)
    other_chunk(11, h1a, qkv, h1b, dzb, 2 * width)
    add_sums(BIAS_V, dzb[:, 2 * width :], qkv[:, 2 * width :])
    loads["tokens"].wait()
    norm_backward(tokens, dh, small(block, GAIN1), grad, grad, sums, GAIN1, SHIFT1)
    store(copies, out_sem, grad, grad_out)

    def small_copy(step, src, peer):
        return pltpu.make_async_remote_copy(
            src_ref=src, dst_ref=small_in.at[step], send_sem=small_send.at[step], recv_sem=small_recv.at[step],
            device_id=peer, device_id_type=MESH,
        )

    own_peers = (core_peer, x_peer, y_peer)

    def small_next(step):
        small_copy(step, small_tot.at[step], own_peers[step]).wait_recv()
        small_tot[step + 1] = small_tot[step] + small_in[step]
        if step + 1 < 3:
            small_copy(step + 1, small_tot.at[step + 1], own_peers[step + 1]).start()
        else:

            @pl.when(end)
            def _():
                small_copy(3, small_tot.at[3], inward).start()

    def small_middle():
        @pl.when(middle)
        def _():
            small_copy(3, small_tot.at[3], inward).wait_recv()
            small_tot[4] = small_tot[3] + small_in[3]
            small_copy(4, small_tot.at[4], across).start()

    def small_last():
        @pl.when(middle)
        def _():
            small_copy(4, small_tot.at[4], across).wait_recv()
            small_tot[5] = small_tot[4] + small_in[4]
            small_copy(5, small_tot.at[5], outward).start()
            sums_out[...] = small_tot[5]

    small_tot[0] = sums[...]
    small_copy(0, small_tot.at[0], own_peers[0]).start()
    period(9)
    other_chunk(12, h1a, qkv, h1b, dzb, 2 * width + 2 * third_width)
    small_next(0)
    period(10)
    small_next(1)
    period(11)
    small_next(2)
    period(12)
    small_middle()
    period(13)
    small_last()
    for k in range(14, chunks + 5):
        period(k)

    @pl.when(end)
    def _():
        small_copy(5, small_tot.at[5], outward).wait_recv()
        sums_out[...] = small_in[5]

    for i in range(chunks):
        Chunk(i).finish()
    for step in range(3):
        small_copy(step, small_tot.at[step], own_peers[step]).wait_send()

    @pl.when(end)
    def _():
        small_copy(3, small_tot.at[3], inward).wait_send()

    @pl.when(middle)
    def _():
        small_copy(4, small_tot.at[4], across).wait_send()
        small_copy(5, small_tot.at[5], outward).wait_send()

    for copy in copies[1:]:
        copy.wait()


def last_kernel(
    act, tokens_grad, sums, gqkv, gout, gfc, gproj,
    act_out, tokens_grad_out, gqkv_out, gout_out, gfc_out, gproj_out,
    g1, s1, gbq, gbv, gbo, g2, s2, gbp, gbfc,
    lqkv, lout, lfc, lproj, fqkv, fout, ffc, fproj, act_here, grad_here, in_sem, out_sem,
):
    lows = (lqkv, lout, lfc, lproj)
    loads = [
        pltpu.make_async_copy(src, dst, in_sem.at[i]) for i, (src, dst) in enumerate(zip((gqkv, gout, gfc, gproj), lows))
    ]
    passing = [
        pltpu.make_async_copy(act, act_here, in_sem.at[4]), pltpu.make_async_copy(tokens_grad, grad_here, in_sem.at[5])
    ]
    for copy in passing + [loads[i] for i in (3, 2, 0, 1)]:
        copy.start()
    copies = []
    for copy, here, place in zip(passing, (act_here, grad_here), (act_out, tokens_grad_out)):
        copy.wait()
        store(copies, out_sem, here, place)
    wides = ((fqkv, gqkv_out), (fout, gout_out), (ffc, gfc_out), (fproj, gproj_out))
    for i in (3, 2, 0, 1):
        loads[i].wait()
        wide, place = wides[i]
        wide[...] = lows[i][...].astype(f32)
        store(copies, out_sem, wide, place)
    owners = lax.axis_size("own")
    me = lax.axis_index("own")
    size, ff_size = g1.shape[0], gbfc.shape[0]
    across = sums.shape[1] // ff_size
    mine = jnp.zeros((8, size), f32)
    mine_ff = jnp.zeros((1, ff_size), f32)
    for owner in range(owners):
        here = me == owner
        mine = jnp.where(here, sums[:8, owner * size : (owner + 1) * size], mine)
        row, col = BIAS_FC + owner // across, owner % across * ff_size
        mine_ff = jnp.where(here, sums[row : row + 1, col : col + ff_size], mine_ff)
    for row, place in enumerate((g1, s1, gbq, gbv, gbo, g2, s2, gbp)):
        place[...] = mine[row]
    gbfc[...] = mine_ff[0]
    for copy in copies:
        copy.wait()


VMEM_BYTES = 65_200 * 1024


def spec(shape, dtype):
    return jax.ShapeDtypeStruct(shape, dtype)


def kernels_body(*args):
    tokens, doc, cotangent = args[:3]
    gain1, shift1, sqkv, bq, bv, sout, bo, gain2, shift2, sfc, bfc, sproj, bp = args[3:]
    count, width = tokens.shape
    ff = sfc.shape[1]
    rows = [gain1, shift1, bq, bv, bo, gain2, shift2, bp]
    lanes = 128
    stacked = jnp.pad(jnp.stack(rows), ((0, 0), (0, lanes - gain1.shape[0])))
    packed = jnp.concatenate([stacked, bfc.reshape(-1, lanes)])
    packed = jnp.pad(packed, ((0, 16 - packed.shape[0]), (0, 0)))

    hbm = pl.BlockSpec(memory_space=pl.ANY)
    vmem = pl.BlockSpec(memory_space=pltpu.VMEM)
    V = pltpu.VMEM
    half = count // 2
    x_s = ((count, width), f32)
    low_s = ((count, width), bf16)
    qkv_s = ((count, 3 * width), bf16)
    ff_s = ((count, ff), bf16)
    probs_s = ((HEADS // 2, count, count + half), bf16)
    f_s = ((3, count, 8 * (sproj.shape[0] // 3)), bf16)
    mask_s = ((half, count + half), f32)
    block_s = ((16, width), f32)
    w_s = [((width, 3 * width), bf16), ((width, width), bf16), ((width, ff), bf16), ((ff, width), bf16)]
    units = 3 + 1 + ff // width + 3
    dma = pltpu.SemaphoreType.DMA

    def call(kernel, inputs, outs, scratch, in_specs, out_specs, **params):
        return pl.pallas_call(
            kernel,
            out_shape=[spec(*s) for s in outs],
            in_specs=in_specs,
            out_specs=out_specs,
            scratch_shapes=scratch,
            compiler_params=pltpu.CompilerParams(vmem_limit_bytes=VMEM_BYTES, **params),
        )(*inputs)

    w_all = ((4 + 2 * (ff // width), width, width), bf16)
    outs = [x_s, block_s, mask_s, w_all, low_s, qkv_s, probs_s, low_s, x_s, low_s, ff_s, f_s]
    (x2, block, mask, w, h1a, qkva, probsa, oa, x1a, h2a, slopea, fa) = call(
        first_kernel,
        (tokens, doc.reshape(1, count), packed, sqkv, sout, sfc, sproj),
        outs,
        [V(*s) for s in w_s]
        + [V(*s) for s in (block_s, mask_s, low_s, qkv_s, probs_s, low_s, x_s, low_s, ff_s, f_s, x_s)]
        + [V((8, 16, lanes), bf16)]
        + [dma((units, 6)), dma((units, 6)), dma((units, 7)), dma((units, 7)), dma((units,)), dma((7,)), dma((7,))]
        + [dma((len(outs) + 11,))],
        [vmem] * 3 + [hbm] * 4,
        [hbm] * len(outs),
        collective_id=0,
        has_side_effects=True,
    )
    shard = sqkv.shape[0]
    third = sproj.shape[0] // 3
    tiles = 1 + 3 + ff // width

    half_rows = [((3, 2, 2, third // 2, width), bf16), ((tiles, 2, 2, shard // 2, width), bf16)]
    half_rows2 = [((3, 2, third // 2, width), bf16), ((tiles, 2, shard // 2, width), bf16)]
    blocks = [((3, third, width), bf16), ((tiles, shard, width), bf16)]
    outs = [low_s, x_s, block_s, *[(s.shape, bf16) for s in (sqkv, sout, sfc, sproj)]]
    scratch = [x_s, low_s, low_s, x_s, x_s, x_s, ((4, width, width), bf16), low_s, qkv_s, low_s, low_s, ff_s]
    scratch += [low_s, qkv_s, low_s, low_s, ff_s, ((2 * f_s[0][0], *f_s[0][1:]), bf16)]
    scratch += [((HEADS // 4, count, count + half), bf16), low_s, low_s, low_s, block_s]
    scratch += [((2, 2, 2, 2, third, width), bf16), ((2, 2, 2, 2, shard, width), bf16)]
    scratch += [((3, 2, 2, third, width), bf16), ((tiles, 2, 2, shard, width), bf16)]
    scratch += half_rows + half_rows2 + blocks * 2
    scratch += [((6, 16, width), f32), ((6, 16, width), f32)]
    act, tokens_grad, sums, *grads = call(
        second_kernel,
        (
            x2, tokens, cotangent, mask, block, w, w.reshape(-1, 2, 2, 2, shard, width),
            w.reshape(-1, 3, 2, third, width),
            h1a, qkva, probsa, oa, x1a, h2a, slopea, fa,
        ),
        outs,
        [V(*s) for s in scratch]
        + [dma((24,)), dma((4,)), dma((16,)), dma((13, 8)), dma((13, 8)), dma((6,)), dma((6,))],
        [hbm] * 4 + [vmem] + [hbm] * 11,
        [hbm, hbm, vmem] + [hbm] * 4,
        collective_id=1,
        has_side_effects=True,
    )
    shards = [(s.shape, f32) for s in (sqkv, sout, sfc, sproj)]
    vectors = [(gain1.shape, f32)] * 8 + [(bfc.shape, f32)]
    act, tokens_grad, gqkv, gout, gfc, gproj, *small_grads = call(
        last_kernel,
        (act, tokens_grad, sums, *grads),
        [low_s, x_s, *shards, *vectors],
        [V(s.shape, bf16) for s in (sqkv, sout, sfc, sproj)] + [V(*s) for s in shards]
        + [V(*low_s), V(*x_s), dma((6,)), dma((6,))],
        [hbm, hbm, vmem] + [hbm] * 4,
        [hbm] * 6 + [vmem] * 9,
    )
    g1, s1, gbq, gbv, gbo, g2, s2, gbp, gbfc = small_grads
    return act, tokens_grad, g1, s1, gqkv, gbq, gbv, gout, gbo, g2, s2, gfc, gbfc, gproj, gbp


def as_sent(shard):
    return jax.tree.map(lambda a: a.astype(jnp.bfloat16) if a.dtype == jnp.float32 else a, shard)


def normalize(x, gain, shift):
    centre = x - jnp.mean(x, axis=-1, keepdims=True)
    spread = jnp.mean(centre * centre, axis=-1, keepdims=True)
    return centre * lax.rsqrt(spread + EPSILON) * gain + shift


def smooth(inner):
    return jax.nn.gelu(inner, approximate=True)


def visible(doc):
    count = doc.shape[0]
    row = lax.broadcasted_iota(jnp.int32, (count, count), 0)
    col = lax.broadcasted_iota(jnp.int32, (count, count), 1)
    same = doc[:, None] == doc[None, :]
    return same & (col <= row) & ((doc[None, :] != 0) | (row == col))


def plain_forward(x, weights, mask):
    (
        gain_one,
        shift_one,
        w_qkv,
        bias_query,
        bias_value,
        w_out,
        bias_out,
        gain_two,
        shift_two,
        w_fc,
        bias_fc,
        w_proj,
        bias_proj,
    ) = weights
    width = w_qkv.shape[0]
    count = x.shape[0]
    scale = HEAD_DIM ** (-0.5)
    f32 = jnp.float32
    h_one = normalize(x, gain_one.astype(f32), shift_one.astype(f32)).astype(jnp.bfloat16)
    qkv_bias = jnp.concatenate(
        [bias_query.astype(f32), jnp.zeros((width,), f32), bias_value.astype(f32)]
    )
    packed = (jnp.dot(h_one, w_qkv, preferred_element_type=f32) + qkv_bias).astype(jnp.bfloat16)
    query = packed[:, :width].reshape(count, HEADS, HEAD_DIM)
    key = packed[:, width : 2 * width].reshape(count, HEADS, HEAD_DIM)
    value = packed[:, 2 * width :].reshape(count, HEADS, HEAD_DIM)
    scores = jnp.einsum("thd,shd->hts", query, key, preferred_element_type=f32) * scale
    scores = jnp.where(mask[None], scores, -1e30)
    probs = jax.nn.softmax(scores, axis=-1)
    probs_low = probs.astype(jnp.bfloat16)
    mixed = jnp.einsum("hts,shd->thd", probs_low, value, preferred_element_type=f32)
    mixed = mixed.reshape(count, width).astype(jnp.bfloat16)
    middle = x + (jnp.dot(mixed, w_out, preferred_element_type=f32) + bias_out.astype(f32))
    h_two = normalize(middle, gain_two.astype(f32), shift_two.astype(f32)).astype(jnp.bfloat16)
    inner = jnp.dot(h_two, w_fc, preferred_element_type=f32) + bias_fc.astype(f32)
    active = smooth(inner).astype(jnp.bfloat16)
    result = middle + (jnp.dot(active, w_proj, preferred_element_type=f32) + bias_proj.astype(f32))
    kept = (h_one, query, key, value, probs, probs_low, mixed, middle, h_two, inner, active)
    return (result, kept)


def plain_backward(x, weights, mask, grad):
    (
        gain_one,
        shift_one,
        w_qkv,
        bias_query,
        bias_value,
        w_out,
        bias_out,
        gain_two,
        shift_two,
        w_fc,
        bias_fc,
        w_proj,
        bias_proj,
    ) = weights
    result, kept = plain_forward(x, weights, mask)
    h_one, query, key, value, probs, probs_low, mixed, middle, h_two, inner, active = kept
    width = w_qkv.shape[0]
    count = x.shape[0]
    scale = HEAD_DIM ** (-0.5)
    f32 = jnp.float32
    grad_branch = grad.astype(jnp.bfloat16)
    g_wproj = jnp.einsum("tf,td->fd", active, grad_branch, preferred_element_type=f32)
    g_bproj = jnp.sum(grad_branch.astype(f32), axis=0)
    d_active = jnp.einsum("td,fd->tf", grad_branch, w_proj, preferred_element_type=f32)
    unused, pull_smooth = jax.vjp(smooth, inner)
    d_inner = pull_smooth(d_active)[0].astype(jnp.bfloat16)
    g_wfc = jnp.einsum("td,tf->df", h_two, d_inner, preferred_element_type=f32)
    g_bfc = jnp.sum(d_inner.astype(f32), axis=0)
    d_htwo = jnp.einsum("tf,df->td", d_inner, w_fc, preferred_element_type=f32)
    unused, pull_two = jax.vjp(normalize, middle, gain_two.astype(f32), shift_two.astype(f32))
    d_mid, g_gain2, g_shift2 = pull_two(d_htwo)
    d_middle = grad + d_mid
    d_attn = d_middle.astype(jnp.bfloat16)
    g_wout = jnp.einsum("td,te->de", mixed, d_attn, preferred_element_type=f32)
    g_bout = jnp.sum(d_attn.astype(f32), axis=0)
    d_mixed = jnp.einsum("te,de->td", d_attn, w_out, preferred_element_type=f32).astype(
        jnp.bfloat16
    )
    d_mixed = d_mixed.reshape(count, HEADS, HEAD_DIM)
    d_probs = jnp.einsum("thd,shd->hts", d_mixed, value, preferred_element_type=f32)
    d_value = jnp.einsum("hts,thd->shd", probs_low, d_mixed, preferred_element_type=f32)
    d_scores = probs * (d_probs - jnp.sum(d_probs * probs, axis=-1, keepdims=True))
    d_scores = d_scores.astype(jnp.bfloat16)
    d_query = jnp.einsum("hts,shd->thd", d_scores, key, preferred_element_type=f32) * scale
    d_key = jnp.einsum("hts,thd->shd", d_scores, query, preferred_element_type=f32) * scale
    d_packed = jnp.concatenate(
        [d_query.reshape(count, width), d_key.reshape(count, width), d_value.reshape(count, width)],
        axis=1,
    ).astype(jnp.bfloat16)
    g_wqkv = jnp.einsum("td,te->de", h_one, d_packed, preferred_element_type=f32)
    column_sums = jnp.sum(d_packed.astype(f32), axis=0)
    g_bquery = column_sums[:width]
    g_bvalue = column_sums[2 * width :]
    d_hone = jnp.einsum("te,de->td", d_packed, w_qkv, preferred_element_type=f32)
    unused, pull_one = jax.vjp(normalize, x, gain_one.astype(f32), shift_one.astype(f32))
    d_input, g_gain1, g_shift1 = pull_one(d_hone)
    terms = (
        g_gain1,
        g_shift1,
        g_wqkv,
        g_bquery,
        g_bvalue,
        g_wout,
        g_bout,
        g_gain2,
        g_shift2,
        g_wfc,
        g_bfc,
        g_wproj,
        g_bproj,
    )
    return (d_middle + d_input, terms)


def plain_body(
    tokens,
    doc_ids,
    cotangent,
    norm1_gain,
    norm1_shift,
    qkv_weight,
    query_bias,
    value_bias,
    out_weight,
    out_bias,
    norm2_gain,
    norm2_shift,
    fc_weight,
    fc_bias,
    proj_weight,
    proj_bias,
):
    shards = (
        norm1_gain,
        norm1_shift,
        qkv_weight,
        query_bias,
        value_bias,
        out_weight,
        out_bias,
        norm2_gain,
        norm2_shift,
        fc_weight,
        fc_bias,
        proj_weight,
        proj_bias,
    )
    mask = visible(doc_ids)

    def fetch():
        return (
            lax.all_gather(shards[0], "own", axis=0, tiled=True),
            lax.all_gather(shards[1], "own", axis=0, tiled=True),
            lax.all_gather(shards[2], "own", axis=0, tiled=True),
            lax.all_gather(shards[3], "own", axis=0, tiled=True),
            lax.all_gather(shards[4], "own", axis=0, tiled=True),
            lax.all_gather(shards[5], "own", axis=0, tiled=True),
            lax.all_gather(shards[6], "own", axis=0, tiled=True),
            lax.all_gather(shards[7], "own", axis=0, tiled=True),
            lax.all_gather(shards[8], "own", axis=0, tiled=True),
            lax.all_gather(shards[9], "own", axis=0, tiled=True),
            lax.all_gather(shards[10], "own", axis=0, tiled=True),
            lax.all_gather(shards[11], "own", axis=0, tiled=True),
            lax.all_gather(shards[12], "own", axis=0, tiled=True),
        )

    current = tokens.astype(jnp.float32)
    saved = []
    for use in range(USES):
        saved.append(current)
        current, kept = plain_forward(current, fetch(), mask)
    grad = cotangent.astype(jnp.float32)
    summed = None
    for use in reversed(range(USES)):
        grad, terms = plain_backward(saved[use], fetch(), mask, grad)
        if summed is None:
            summed = terms
        else:
            summed = tuple((first + second for first, second in zip(summed, terms)))
    owned = (
        lax.psum_scatter(summed[0], "own", scatter_dimension=0, tiled=True),
        lax.psum_scatter(summed[1], "own", scatter_dimension=0, tiled=True),
        lax.psum_scatter(summed[2], "own", scatter_dimension=0, tiled=True),
        lax.psum_scatter(summed[3], "own", scatter_dimension=0, tiled=True),
        lax.psum_scatter(summed[4], "own", scatter_dimension=0, tiled=True),
        lax.psum_scatter(summed[5], "own", scatter_dimension=0, tiled=True),
        lax.psum_scatter(summed[6], "own", scatter_dimension=0, tiled=True),
        lax.psum_scatter(summed[7], "own", scatter_dimension=0, tiled=True),
        lax.psum_scatter(summed[8], "own", scatter_dimension=0, tiled=True),
        lax.psum_scatter(summed[9], "own", scatter_dimension=0, tiled=True),
        lax.psum_scatter(summed[10], "own", scatter_dimension=0, tiled=True),
        lax.psum_scatter(summed[11], "own", scatter_dimension=0, tiled=True),
        lax.psum_scatter(summed[12], "own", scatter_dimension=0, tiled=True),
    )
    final = jax.tree.map(lambda part: part.astype(jnp.float32), lax.psum(as_sent(owned), "grp"))
    return (current.astype(jnp.bfloat16), grad) + tuple(final)


def solution(mesh):
    return jax.shard_map(
        kernels_body if tuple(mesh.axis_sizes) == (4, 8) else plain_body,
        mesh=mesh,
        in_specs=(
            P(("grp", "own"), None),
            P(("grp", "own")),
            P(("grp", "own"), None),
            P("own"),
            P("own"),
            P("own", None),
            P("own"),
            P("own"),
            P("own", None),
            P("own"),
            P("own"),
            P("own"),
            P("own", None),
            P("own"),
            P("own", None),
            P("own"),
        ),
        out_specs=(
            P(("grp", "own"), None),
            P(("grp", "own"), None),
            P("own"),
            P("own"),
            P("own", None),
            P("own"),
            P("own"),
            P("own", None),
            P("own"),
            P("own"),
            P("own"),
            P("own", None),
            P("own"),
            P("own", None),
            P("own"),
        ),
        check_vma=False,
    )
```

```python
import functools

import jax
import jax.numpy as jnp
from jax import lax
from jax.experimental import pallas as pl
from jax.experimental.pallas import tpu as pltpu
from jax.sharding import PartitionSpec as P

HEADS = 12
HEAD_DIM = 64
USES = 2
EPSILON = 1e-05
SCALE = HEAD_DIM ** (-0.5)
TANH_SCALE = 0.7978845608028654
TANH_CUBIC = 0.044715
MESH = pl.DeviceIdType.MESH
f32 = jnp.float32
bf16 = jnp.bfloat16

GAIN1, SHIFT1, BIAS_Q, BIAS_V, BIAS_OUT, GAIN2, SHIFT2, BIAS_PROJ, BIAS_FC = range(9)


def dot(a, b, ca=1, cb=0):
    return lax.dot_general(a, b, (((ca,), (cb,)), ((), ())), preferred_element_type=f32)


def loop(count, body):
    def step(i, carry):
        body(i)
        return carry

    lax.fori_loop(0, count, step, 0)


def span(begin, end, body):
    def step(i, carry):
        body(i)
        return carry

    lax.fori_loop(begin, end, step, 0)


def part(i, size):
    return pl.ds(pl.multiple_of(i * size, size), size)


def centred(x):
    centre = x - jnp.mean(x, axis=-1, keepdims=True)
    spread = jnp.mean(centre * centre, axis=-1, keepdims=True)
    return centre, lax.rsqrt(spread + EPSILON)


def norm_forward(x, gain, shift, h, unroll=True):
    rows = 128

    def step(i):
        these = pl.ds(i * rows, rows) if unroll else part(i, rows)
        centre, r = centred(x[these, :].astype(f32))
        h[these, :] = (centre * r * gain + shift).astype(bf16)

    if unroll:
        for i in range(x.shape[0] // rows):
            step(i)
    else:
        loop(x.shape[0] // rows, step)


def norm_backward(x, dh, gain, grad, out, sums, gain_row, shift_row, low=None):
    rows = 128

    def step(i):
        these = pl.ds(i * rows, rows)
        centre, r = centred(x[these, :].astype(f32))
        n = centre * r
        d = dh[these, :]
        sums[gain_row : gain_row + 1, :] += jnp.sum(d * n, axis=0, keepdims=True)
        sums[shift_row : shift_row + 1, :] += jnp.sum(d, axis=0, keepdims=True)
        e = d * gain
        inner = e - jnp.mean(e, axis=-1, keepdims=True) - n * jnp.mean(e * n, axis=-1, keepdims=True)
        result = grad[these, :].astype(f32) + r * inner
        out[these, :] = result
        if low is not None:
            low[these, :] = result.astype(bf16)

    for i in range(x.shape[0] // rows):
        step(i)


def column_sum(x):
    return jnp.sum(x.astype(f32), axis=0, keepdims=True)


def make_mask(doc, mask):
    count = doc.shape[1]
    half = count // 2
    ids = doc[0:1, :].astype(f32)
    keys = jnp.broadcast_to(ids, (128, count)).T[:, :1]
    for k0, q0, place in ((0, 0, 0), (half, half, count)):
        width = count - q0
        row = lax.broadcasted_iota(jnp.int32, (half, width), 0) + k0
        col = lax.broadcasted_iota(jnp.int32, (half, width), 1) + q0
        key = keys[k0 : k0 + half]
        same = (key == ids[:, q0:]) & (row <= col) & ((key != 0.0) | (row == col))
        mask[:, place : place + width] = jnp.where(same, 0.0, -1e30)


def head_lanes(h, x):
    lane = lax.broadcasted_iota(jnp.int32, (1, 2 * HEAD_DIM), 1)
    keep = (lane < HEAD_DIM) if h == 0 else (lane >= HEAD_DIM)
    return jnp.where(keep, x, jnp.zeros_like(x))


def attention_forward(qkv, mask, probs, o, begin=0, end=6, shift=0):
    count, width = o.shape
    half = count // 2
    pair = 2 * HEAD_DIM

    def step(i):
        col = pl.ds(i * pair, pair)
        q = qkv[:, col]
        k = qkv[:, pl.ds(width + i * pair, pair)]
        v = qkv[:, pl.ds(2 * width + i * pair, pair)]
        vt = v.T
        outs = []
        for h in range(2):
            kh = head_lanes(h, k)
            s0 = dot(kh[:half], q, 1, 1) + mask[:, :count]
            s1 = dot(kh[half:], q[half:], 1, 1) + mask[:, count:]
            m0 = jnp.max(s0, axis=0, keepdims=True)
            m1 = jnp.max(s1, axis=0, keepdims=True)
            top = jnp.concatenate([m0[:, :half], jnp.maximum(m0[:, half:], m1)], axis=1)
            e0 = jnp.exp(s0 - top)
            e1 = jnp.exp(s1 - top[:, half:])
            l0 = jnp.sum(e0, axis=0, keepdims=True)
            l1 = jnp.sum(e1, axis=0, keepdims=True)
            r = 1.0 / jnp.concatenate([l0[:, :half], l0[:, half:] + l1], axis=1)
            p0 = (e0 * r).astype(bf16)
            p1 = (e1 * r[:, half:]).astype(bf16)
            row = pl.ds(h * half, half)
            probs[i - shift, row, :count] = p0
            probs[i - shift, row, count:] = p1
            vh = vt[h * HEAD_DIM : (h + 1) * HEAD_DIM]
            first = dot(vh[:, :half], p0)
            second = dot(vh[:, half:], p1)
            outs.append(jnp.concatenate([first[:, :half], first[:, half:] + second], axis=1))
        o[:, col] = jnp.concatenate(outs, axis=0).astype(bf16).T

    for i in range(begin, end):
        step(i)


def attention_backward(qkv, probs, do, dz, begin=0, end=6, shift=0):
    count, width = do.shape
    half = count // 2
    pair = 2 * HEAD_DIM

    def step(i):
        cq = pl.ds(i * pair, pair)
        ck = pl.ds(width + i * pair, pair)
        cv = pl.ds(2 * width + i * pair, pair)
        q, k, v, d = qkv[:, cq], qkv[:, ck], qkv[:, cv], do[:, cq]
        dq = dk = dv = None
        for h in range(2):
            dh, kh, qh = head_lanes(h, d), head_lanes(h, k), head_lanes(h, q)
            row = pl.ds(h * half, half)
            p0 = probs[i - shift, row, :count]
            p1 = probs[i - shift, row, count:]
            d0 = dot(v[:half], dh, 1, 1)
            d1 = dot(v[half:], dh[half:], 1, 1)
            w0 = p0.astype(f32)
            w1 = p1.astype(f32)
            t0 = jnp.sum(d0 * w0, axis=0, keepdims=True)
            t1 = jnp.sum(d1 * w1, axis=0, keepdims=True)
            t = jnp.concatenate([t0[:, :half], t0[:, half:] + t1], axis=1)
            s0 = (w0 * (d0 - t)).astype(bf16)
            s1 = (w1 * (d1 - t[:, half:])).astype(bf16)
            v_term = jnp.concatenate([dot(p0, dh), dot(p1, dh[half:])], axis=0)
            k_term = jnp.concatenate([dot(s0, qh), dot(s1, qh[half:])], axis=0)
            qa = dot(s0, kh[:half], 0, 0)
            qb = dot(s1, kh[half:], 0, 0)
            q_term = jnp.concatenate([qa[:half], qa[half:] + qb], axis=0)
            dq = q_term if dq is None else dq + q_term
            dk = k_term if dk is None else dk + k_term
            dv = v_term if dv is None else dv + v_term
        dq = (dq * SCALE).astype(bf16)
        dv = dv.astype(bf16)
        dz[:, cq] = dq
        dz[:, ck] = dk.astype(bf16)
        dz[:, cv] = dv

    for i in range(begin, end):
        step(i)


def small(block, row):
    return block[row : row + 1, :]


def hidden_tile(h2, weight, bias, f, slope, i):
    count, width = h2.shape
    rows = 128
    third = f.shape[2] // 8
    for first in range(0, count, rows):
        these = pl.ds(first, rows)
        u = dot(h2[these, :], weight) + bias
        square = u * u
        t = jnp.tanh(u * (TANH_SCALE + (TANH_SCALE * TANH_CUBIC) * square))
        rise = 0.5 + 0.5 * t
        active = (u * rise).astype(bf16)
        for place in range(width // third):
            owner = i * (width // third // 3) + place // 3
            f[place % 3, these, part(owner, third)] = active[:, place * third : (place + 1) * third]
        inner = TANH_SCALE + (3.0 * TANH_SCALE * TANH_CUBIC) * square
        slope[these, part(i, width)] = (rise + (0.5 * u) * (1.0 - t * t) * inner).astype(bf16)


def hidden_forward(h2, wfc, block, f, slope, begin, end):
    width = h2.shape[1]

    def hidden(i):
        hidden_tile(h2, wfc[:, part(i, width)], block[pl.ds(BIAS_FC + i, 1), :], f, slope, i)

    span(begin, end, hidden)


def project(f, wproj, i):
    third = f.shape[2] // 8
    rows = [wproj[pl.ds((owner * 3 + i) * third, third), :] for owner in range(8)]
    return dot(f[i], jnp.concatenate(rows, axis=0))


def coords():
    own = lax.axis_index("own")
    return lax.axis_index("grp"), own // 2, lax.rem(own, 2)


class Unit:
    def __init__(self, shard, full, row, rows, col, cols, shared=True):
        self.shard, self.full, self.shared = shard, full, shared
        self.row, self.rows, self.col, self.cols = row, rows, col, cols

    def mine(self, half=None):
        rows = self.rows if half is None else self.rows // 2
        start = self.row + (0 if half is None else half * rows)
        return self.shard.at[pl.ds(start, rows), pl.ds(self.col, self.cols)]

    def block(self, owner, half=None):
        rows = self.rows if half is None else self.rows // 2
        start = owner * self.shard.shape[0] + self.row + (0 if half is None else half * rows)
        return self.full.at[pl.ds(pl.multiple_of(start, 16), rows), pl.ds(self.col, self.cols)]


PIECES = [(1, 0), (1, 1), (2, 0), (2, 1), (3, 0), (3, 1)]


class Gather:
    def __init__(self, units, link_send, link_recv, core_send, core_recv, own_sem):
        self.units = units
        self.link_send, self.link_recv = link_send, link_recv
        self.core_send, self.core_recv, self.own_sem = core_send, core_recv, own_sem
        self.grp, self.chip, self.core = coords()
        self.odd = lax.rem(self.grp, 2)
        self.sent = []

    def owner(self, offset):
        return jnp.bitwise_xor(self.chip, offset) * 2 + self.core

    def device(self, chip_offset, along_z=False):
        own = jnp.bitwise_xor(self.chip, chip_offset) * 2 + self.core
        grp = self.grp + 1 - 2 * self.odd if along_z else self.grp
        return (grp, own)

    def link(self, k, src, dst, piece, out, device):
        return pltpu.make_async_remote_copy(
            src_ref=src,
            dst_ref=dst,
            send_sem=self.link_send.at[k, out],
            recv_sem=self.link_recv.at[k, piece],
            device_id=device,
            device_id_type=MESH,
        )

    def across(self, k, src, dst, slot):
        return pltpu.make_async_remote_copy(
            src_ref=src,
            dst_ref=dst,
            send_sem=self.core_send.at[k, slot],
            recv_sem=self.core_recv.at[k, slot],
            device_id=(self.grp, self.chip * 2 + 1 - self.core),
            device_id_type=MESH,
        )

    def own(self, k):
        unit = self.units[k]
        return pltpu.make_async_copy(unit.mine(), unit.block(self.owner(0)), self.own_sem.at[k])

    def first(self, k, offset, half, out):
        unit = self.units[k]
        piece = PIECES.index((offset, half))
        return self.link(
            k, unit.mine(half), unit.block(self.owner(0), half), piece, out, self.device(offset)
        )

    def relay(self, k, offset, half, way, out):
        unit = self.units[k]
        piece = unit.block(self.owner(offset), half)
        return self.link(k, piece, piece, PIECES.index((3, half)), out, self.device(way))

    def pair(self, k, offset, half, out):
        unit = self.units[k]
        piece = unit.block(self.owner(offset), half)
        return self.link(k, piece, piece, PIECES.index((offset, half)), out, self.device(0, True))

    def hand(self, k, offset, half):
        unit = self.units[k]
        piece = unit.block(self.owner(offset), half)
        return self.across(k, piece, piece, PIECES.index((offset, half)))

    def arrived(self, k, offset, half):
        unit = self.units[k]
        piece = unit.block(self.owner(offset), half)
        self.link(k, piece, piece, PIECES.index((offset, half)), 0, self.device(1)).wait_recv()

    def sends(self, k, odd):
        own = [(1, 0), (2, 1), (1, 1), (2, 0)]
        if not self.units[k].shared:
            own = [(2, 0), (1, 1), (1, 0), (2, 1)]
        elif odd:
            own = [(1, 1), (2, 0)]
        calls = [functools.partial(self.first, k, *what) for what in own]
        if odd or not self.units[k].shared:
            calls += [functools.partial(self.relay, k, *what) for what in ((2, 0, 1), (1, 1, 2))]
        if self.units[k].shared:
            pairs = ((3, 0), (3, 1)) if odd else ((1, 0), (2, 1))
            calls += [functools.partial(self.pair, k, *what) for what in pairs]
        return len(own), [functools.partial(call, out) for out, call in enumerate(calls)]

    def each_kind(self, k, body):
        if not self.units[k].shared:
            body(True)
            return

        @pl.when(self.odd == 0)
        def _():
            body(False)

        @pl.when(self.odd == 1)
        def _():
            body(True)

    def start(self, k):
        def body(odd):
            own, calls = self.sends(k, odd)
            for call in calls[:own]:
                call().start()

        self.each_kind(k, body)
        unit = self.units[k]
        self.across(k, unit.mine(), unit.block(self.owner(0)), len(PIECES)).start()
        self.own(k).start()

    def serve(self, k, odd, pieces, then):
        for piece in pieces:
            self.arrived(k, *piece)
            if piece in then:
                then[piece]().start()
            self.hand(k, *piece).start()

    def serve_first(self, k):
        def body(odd):
            own, calls = self.sends(k, odd)
            if odd:
                then = {(2, 0): calls[own], (1, 1): calls[own + 1]}
                self.serve(k, odd, ((2, 0), (1, 1)), then)
            else:
                then = {(1, 0): calls[own], (2, 1): calls[own + 1]}
                self.serve(k, odd, ((1, 0), (2, 1), (1, 1), (2, 0)), then)

        self.each_kind(k, body)

    def serve_second(self, k):
        def body(odd):
            own, calls = self.sends(k, odd)
            if not self.units[k].shared:
                self.serve(k, odd, ((1, 0), (2, 1), (3, 0), (3, 1)), {})
            elif odd:
                then = {(3, 0): calls[own + 2], (3, 1): calls[own + 3]}
                self.serve(k, odd, ((3, 0), (3, 1), (1, 0), (2, 1)), then)
            else:
                self.serve(k, odd, ((3, 0), (3, 1)), {})

        self.each_kind(k, body)

    def finish(self, k):
        unit = self.units[k]
        other = 1 - 2 * self.core
        self.own(k).wait()
        whole = unit.block(self.owner(0) + other)
        self.across(k, whole, whole, len(PIECES)).wait_recv()
        for slot, (offset, half) in enumerate(PIECES):
            piece = unit.block(self.owner(offset) + other, half)
            self.across(k, piece, piece, slot).wait_recv()

    def drain(self, k):
        def body(odd):
            own, calls = self.sends(k, odd)
            for call in calls:
                call().wait_send()

        self.each_kind(k, body)
        unit = self.units[k]
        self.across(k, unit.mine(), unit.block(self.owner(0)), len(PIECES)).wait_send()
        for offset, half in PIECES:
            self.hand(k, offset, half).wait_send()


def store(copies, sem, src, dst):
    copy = pltpu.make_async_copy(src, dst, sem.at[len(copies)])
    copy.start()
    copies.append(copy)


def first_kernel(
    tokens, doc, packed, sqkv, sout, sfc, sproj,
    x2_out, block_out, mask_out, w_out,
    h1_out, qkv_out, probs_out, o_out, x1_out, h2_out, slope_out, f_out,
    wqkv, wout, wfc, wproj, block, mask, h1, qkv, probs, o, x1, h2, slope, f, x2, many,
    link_send, link_recv, core_send, core_recv, own_sem, small_send, small_recv, out_sem,
):
    grp, chip, core = coords()
    me = chip * 2 + core
    width = tokens.shape[1]
    barrier = pltpu.get_barrier_semaphore()
    peers = [(grp, jnp.bitwise_xor(me, j)) for j in range(1, 8)]
    peers.append((grp + 1 - 2 * lax.rem(grp, 2), me))
    for peer in peers:
        pl.semaphore_signal(barrier, inc=1, device_id=peer, device_id_type=MESH)
    pl.semaphore_wait(barrier, len(peers))

    units = [Unit(sqkv, wqkv, 0, sqkv.shape[0], i * width, width) for i in range(3)]
    units += [Unit(sout, wout, 0, sout.shape[0], 0, width)]
    units += [Unit(sfc, wfc, 0, sfc.shape[0], i * width, width) for i in range(sfc.shape[1] // width)]
    thirds = sproj.shape[0] // 3
    units += [Unit(sproj, wproj, i * thirds, thirds, 0, width, False) for i in range(3)]
    gather = Gather(units, link_send, link_recv, core_send, core_recv, own_sem)
    count = len(units)

    def small_copy(j):
        return pltpu.make_async_remote_copy(
            src_ref=packed,
            dst_ref=many.at[me],
            send_sem=small_send.at[j - 1],
            recv_sem=small_recv.at[j - 1],
            device_id=(grp, jnp.bitwise_xor(me, j)),
            device_id_type=MESH,
        )

    for j in range(1, 8):
        small_copy(j).start()
    gather.start(0)
    gather.start(1)
    copies = []

    def slot(s):
        if s < count:
            gather.serve_first(s)
        if s + 2 < count:
            gather.start(s + 2)
        if 0 <= s - 2 < count:
            gather.serve_second(s - 2)
        if 0 <= s - 3 < count:
            gather.finish(s - 3)

    make_mask(doc, mask)
    store(copies, out_sem, mask, mask_out)
    slot(0)
    many[me] = packed[...]
    for j in range(1, 8):
        small_copy(j).wait_recv()
    lanes = packed.shape[1]
    size, ff_size = sqkv.shape[0], sproj.shape[0]
    block[12:16, :] = jnp.zeros((4, width), f32)
    for owner in range(8):
        rows = many[owner].astype(f32)
        block[:8, owner * size : (owner + 1) * size] = rows[:8, :size]
        row, col = BIAS_FC + owner * ff_size // width, owner * ff_size % width
        for j in range(ff_size // lanes):
            block[row : row + 1, col + j * lanes : col + (j + 1) * lanes] = rows[8 + j : 9 + j, :]
    store(copies, out_sem, block, block_out)
    slot(1)
    norm_forward(tokens, small(block, GAIN1), small(block, SHIFT1), h1, False)
    store(copies, out_sem, h1, h1_out)
    slot(2)
    slot(3)
    qkv[:, :width] = (dot(h1[...], wqkv[:, :width]) + small(block, BIAS_Q)).astype(bf16) * SCALE
    slot(4)
    qkv[:, width : 2 * width] = dot(h1[...], wqkv[:, width : 2 * width]).astype(bf16)
    slot(5)
    for i in range(3):
        store(copies, out_sem, wqkv.at[:, pl.ds(i * width, width)], w_out.at[i])
    qkv[:, 2 * width :] = (dot(h1[...], wqkv[:, 2 * width :]) + small(block, BIAS_V)).astype(bf16)
    store(copies, out_sem, qkv, qkv_out)
    attention_forward(qkv, mask, probs, o, 0, 1)
    slot(6)
    store(copies, out_sem, wout, w_out.at[3])
    attention_forward(qkv, mask, probs, o, 1, 3)
    slot(7)
    attention_forward(qkv, mask, probs, o, 3, 5)
    slot(8)
    attention_forward(qkv, mask, probs, o, 5, 6)
    store(copies, out_sem, probs, probs_out)
    store(copies, out_sem, o, o_out)
    x1[...] = tokens[...].astype(f32) + (dot(o[...], wout[...]) + small(block, BIAS_OUT))
    norm_forward(x1, small(block, GAIN2), small(block, SHIFT2), h2, False)
    store(copies, out_sem, x1, x1_out)
    store(copies, out_sem, h2, h2_out)
    slot(9)
    hidden_forward(h2, wfc, block, f, slope, 0, 2)
    slot(10)
    fc_tiles = wfc.shape[1] // width
    for i in range(fc_tiles):
        store(copies, out_sem, wfc.at[:, pl.ds(i * width, width)], w_out.at[4 + i])
    hidden_forward(h2, wfc, block, f, slope, 2, 4)
    store(copies, out_sem, f, f_out)
    store(copies, out_sem, slope, slope_out)

    slot(11)
    x2[...] = x1[...] + (project(f, wproj, 0) + small(block, BIAS_PROJ))
    slot(12)
    x2[...] += project(f, wproj, 1)
    slot(13)
    for i in range(fc_tiles):
        store(copies, out_sem, wproj.at[pl.ds(i * width, width), :], w_out.at[4 + fc_tiles + i])
    x2[...] += project(f, wproj, 2)
    store(copies, out_sem, x2, x2_out)
    for k in range(count):
        gather.drain(k)
    for j in range(1, 8):
        small_copy(j).wait_send()
    for copy in copies:
        copy.wait()


def second_kernel(
    x2_in, tokens_in, cot_in, mask_in, block, w_in, w_parts_in, w_thirds_in,
    h1a_in, qkv_in, probs_in, oa_in, x1_in, h2a_in, slope_in, fa_in,
    act_out, grad_out, sums_out, gqkv_out, gout_out, gfc_out, gproj_out,
    x, tokens, cot, grad, x1, dh, tiles, h1a, qkv, oa, h2a, slope, h1b, dzb, ob, h2b, dub, shared, more_probs,
    gm, da, dab, sums,
    buf_p, buf_o, recv_p, recv_o, hop1_p, hop1_o, hop2_p, hop2_o, zmid_p, zmid_o, tot_p, tot_o,
    small_in, small_tot,
    in_sem, tile_sem, out_sem, send, recv, small_send, small_recv,
):
    grp, chip, core = coords()
    yy, xx = chip // 2, lax.rem(chip, 2)
    me = chip * 2 + core
    width = x.shape[1]
    loads = {}

    def load(name, src, dst):
        copy = pltpu.make_async_copy(src, dst, in_sem.at[len(loads)])
        copy.start()
        loads[name] = copy

    fb, fa = shared.at[pl.ds(0, 3)], shared.at[pl.ds(3, 3)]
    probs = shared.at[:, :, pl.ds(0, probs_in.shape[2])]
    some_probs = shared.at[pl.ds(3, 3), :, pl.ds(0, probs_in.shape[2])]
    half = x.shape[0] // 2
    mask = dh.at[pl.ds(0, half), :]
    load("x", x2_in, x)

    ff_tiles = w_in.shape[0] - 8
    ring = tiles.shape[0]
    fc_at, proj_at = 4, 4 + ff_tiles
    order = [proj_at + t for t in range(ff_tiles)] + [fc_at + t for t in range(ff_tiles)] + [3, 0, 1, 2]

    def tile_copy(t):
        return pltpu.make_async_copy(w_in.at[order[t]], tiles.at[t % ring], tile_sem.at[t % ring])

    def tile(t):
        tile_copy(t).wait()
        return tiles[t % ring]

    def next_tile(t):
        if t + ring < len(order):
            tile_copy(t + ring).start()

    def square(value):
        return value.reshape(width, width)

    def resident(t):
        if t < 2:
            return square(buf_o[t])
        if t < 4:
            return jnp.concatenate(
                [buf_p[t - 2, 0].reshape(-1, width), buf_p[t - 2, 1, 0].reshape(-1, width)], axis=0
            )
        return square(recv_o[2 * (t - 4) : 2 * (t - 4) + 2])

    for t in range(2):
        load(f"w{t}", w_parts_in.at[t], buf_o.at[t])
    load("w2", w_thirds_in.at[2, pl.ds(0, 2)], buf_p.at[0, 0])
    load("w2b", w_thirds_in.at[2, 2], buf_p.at[0, 1, 0])
    load("mask", mask_in, mask)
    load("w3", w_thirds_in.at[3, pl.ds(0, 2)], buf_p.at[1, 0])
    load("w3b", w_thirds_in.at[3, 2], buf_p.at[1, 1, 0])
    for t in range(ff_tiles):
        load(f"w{fc_at + t}", w_parts_in.at[fc_at + t], recv_o.at[pl.ds(2 * t, 2)])
    for t in range(ring):
        tile_copy(t).start()
    core_peer = (grp, jnp.bitwise_xor(me, 1))
    x_peer = (grp, jnp.bitwise_xor(me, 2))
    y_peer = (grp, jnp.bitwise_xor(me, 4))
    low = grp == 1
    middle = (grp == 1) | (grp == 2)
    end = jnp.logical_not(middle)
    inward = (jnp.where(grp == 0, 1, 2), me)
    outward = (jnp.where(low, 0, 3), me)
    across = (jnp.where(low, 2, 1), me)

    barrier = pltpu.get_barrier_semaphore()

    def greet():
        for peer in (core_peer, x_peer, y_peer):
            pl.semaphore_signal(barrier, inc=1, device_id=peer, device_id_type=MESH)

        @pl.when(end)
        def _():
            pl.semaphore_signal(barrier, inc=1, device_id=inward, device_id_type=MESH)

        @pl.when(middle)
        def _():
            pl.semaphore_signal(barrier, inc=1, device_id=outward, device_id_type=MESH)
            pl.semaphore_signal(barrier, inc=1, device_id=across, device_id_type=MESH)

    def remote(src, dst, i, stage, peer):
        return pltpu.make_async_remote_copy(
            src_ref=src, dst_ref=dst, send_sem=send.at[i, stage], recv_sem=recv.at[i, stage],
            device_id=peer, device_id_type=MESH,
        )

    specs = [(True, 0, 0, width // 2), (True, 0, width // 2, width // 2), (True, 1, 0, width), (True, 2, 0, width)]
    projs = len(specs)
    specs += [(False, j, 0, width) for j in range(ff_tiles + 3)]
    specs += [(False, ff_tiles + 3, 0, width // 2), (False, ff_tiles + 3, width // 2, width // 2)]
    chunks = len(specs)
    copies = []

    buffers = (
        (buf_p, buf_o), (recv_p, recv_o), (hop1_p, hop1_o), (hop2_p, hop2_o), (zmid_p, zmid_o),
        (tot_p, tot_o),
    )

    class Chunk:
        def __init__(self, i):
            self.i = i
            self.proj, self.at, col, self.width = specs[i]
            cols = pl.ds(col, self.width)
            sets = [pair[0 if self.proj else 1] for pair in buffers]
            ring = sets[0].shape[0]
            order = i if self.proj else i - projs
            self.previous = i - ring if order >= ring else None
            self.last = i + ring >= (projs if self.proj else chunks)
            self.rows = sets[1].shape[3]
            self.buf = sets[0].at[order % ring, :, :, :, :, cols]
            self.recv = sets[1].at[self.at, :, :, :, cols]
            self.hop1 = sets[2].at[self.at, :, :, :, cols]
            self.hop2, self.zmid, self.tot = (
                s.at[self.at, :, :, cols] if len(s.shape) == 4 else s.at[self.at, :, cols] for s in sets[3:]
            )
            half = self.rows // 2
            self.top, self.bottom = pl.ds(0, half), pl.ds(half, half)
            self.cols = cols

        def to_core(self):
            return remote(self.buf.at[1 - core], self.recv, self.i, 0, core_peer)

        def first(self):
            return (
                remote(self.recv.at[:, 1 - xx, self.top, :], self.hop1.at[0], self.i, 1, x_peer),
                remote(self.recv.at[1 - yy, :, self.bottom, :], self.hop1.at[1], self.i, 2, y_peer),
            )

        def second(self):
            return (
                remote(self.recv.at[1 - yy, xx, self.top, :], self.hop2.at[0], self.i, 3, y_peer),
                remote(self.recv.at[yy, 1 - xx, self.bottom, :], self.hop2.at[1], self.i, 4, x_peer),
            )

        def to_middle(self):
            return remote(self.recv.at[yy, xx], self.tot, self.i, 5, inward)

        def between(self):
            return remote(self.recv.at[yy, xx], self.zmid, self.i, 6, across)

        def to_end(self):
            return remote(self.tot, self.tot, self.i, 7, outward)

        def begin(self):
            if self.previous is not None:
                Chunk(self.previous).to_core().wait_send()

        def stage_b(self):
            self.to_core().wait_recv()
            self.recv[...] = self.recv[...] + self.buf[core]
            for copy in self.first():
                copy.start()

        def stage_c(self):
            for copy in self.first():
                copy.wait_recv()
            self.recv[:, xx, self.top, :] = self.recv[:, xx, self.top, :] + self.hop1[0]
            self.recv[yy, :, self.bottom, :] = self.recv[yy, :, self.bottom, :] + self.hop1[1]
            for copy in self.second():
                copy.start()

        def stage_d(self):
            for copy in self.second():
                copy.wait_recv()
            self.recv[yy, xx, self.top, :] = self.recv[yy, xx, self.top, :] + self.hop2[0]
            self.recv[yy, xx, self.bottom, :] = self.recv[yy, xx, self.bottom, :] + self.hop2[1]

            @pl.when(end)
            def _():
                self.to_middle().start()

        def stage_e(self):
            @pl.when(middle)
            def _():
                self.to_middle().wait_recv()
                self.recv[yy, xx] = self.recv[yy, xx] + self.tot[...]
                self.between().start()

        def stage_f(self):
            @pl.when(middle)
            def _():
                self.between().wait_recv()
                self.tot[...] = self.recv[yy, xx] + self.zmid[...]
                self.to_end().start()

        def stage_g(self):
            @pl.when(end)
            def _():
                self.to_end().wait_recv()

            if self.proj:
                place = gproj_out.at[pl.ds(self.at * self.rows, self.rows), self.cols]
            elif self.at < ff_tiles:
                place = gfc_out.at[:, pl.ds(self.at * width, width)]
            elif self.at == ff_tiles:
                place = gout_out
            else:
                place = gqkv_out.at[:, pl.ds((self.at - ff_tiles - 1) * width + specs[self.i][2], self.width)]
            store(copies, out_sem, self.tot, place)

        def finish(self):
            if self.last:
                self.to_core().wait_send()
            for copy in self.first() + self.second():
                copy.wait_send()

            @pl.when(end)
            def _():
                self.to_middle().wait_send()

            @pl.when(middle)
            def _():
                self.between().wait_send()
                self.to_end().wait_send()

    def made(i):
        Chunk(i).to_core().start()

    def proj_chunk(i):
        chunk = Chunk(i)
        chunk.begin()
        rows = chunk.rows
        yb, ya = cot[:, chunk.cols], gm[:, chunk.cols]
        for owner in range(8):
            col = pl.ds(owner * rows, rows)
            value = dot(fb[chunk.at, :, col], yb, 0, 0) + dot(fa[chunk.at, :, col], ya, 0, 0)
            chunk.buf[owner % 2, owner // 4, (owner // 2) % 2] = value.astype(bf16)
        made(i)

    def other_chunk(i, xa, ya, xb, yb, col):
        chunk = Chunk(i)
        chunk.begin()
        cols = pl.ds(col, chunk.width)
        rows = chunk.rows
        for first in (0, 4):
            these = pl.ds(first * rows, 4 * rows)
            value = dot(xa[:, these], ya[:, cols], 0, 0) + dot(xb[:, these], yb[:, cols], 0, 0)
            for at in range(4):
                owner = first + at
                piece = value[at * rows : (at + 1) * rows].astype(bf16)
                chunk.buf[owner % 2, owner // 4, (owner // 2) % 2] = piece
        made(i)

    def b(i):
        Chunk(i).stage_b()

    def period(k):
        if k < chunks:
            Chunk(k).stage_c()
        if 2 <= k + 2 < chunks:
            b(k + 2)
        for lag, name in ((1, "stage_d"), (2, "stage_e"), (3, "stage_f"), (5, "stage_g")):
            if 0 <= k - lag < chunks:
                getattr(Chunk(k - lag), name)()

    sums[...] = jnp.zeros_like(sums)
    loads["x"].wait()
    norm_forward(x, small(block, GAIN1), small(block, SHIFT1), h1b)
    for name in ("w0", "w1", "w2", "w2b"):
        loads[name].wait()
    for t, (bias, scale) in enumerate(((small(block, BIAS_Q), SCALE), (None, None), (small(block, BIAS_V), None))):
        z = dot(h1b[...], resident(t))
        z = z if bias is None else z + bias
        z = z.astype(bf16)
        dzb[:, t * width : (t + 1) * width] = z if scale is None else z * scale
    loads["mask"].wait()
    attention_forward(dzb, mask, some_probs, ob, 0, 3)
    load("cot", cot_in, cot)
    for name, src, dst in (
        ("h2a", h2a_in, h2a), ("slope", slope_in, slope), ("qkv", qkv_in, qkv), ("oa", oa_in, oa), ("h1a", h1a_in, h1a),
        ("tokens", tokens_in, tokens),
    ):
        load(name, src, dst)
    attention_forward(dzb, mask, more_probs, ob, 3, 6, 3)
    loads["w3"].wait()
    loads["w3b"].wait()
    for first in range(0, x.shape[0], 128):
        these = pl.ds(first, 128)
        x1[these, :] = x[these, :] + (dot(ob[these, :], resident(3)) + small(block, BIAS_OUT))
    norm_forward(x1, small(block, GAIN2), small(block, SHIFT2), h2b)
    for t in range(ff_tiles):
        loads[f"w{fc_at + t}"].wait()
    for t in range(ff_tiles):
        hidden_tile(h2b, resident(fc_at + t), block[BIAS_FC + t : BIAS_FC + t + 1, :], fb, dub, t)
    third = fb.shape[2] // 8

    def hidden_rows(t):
        owners = width // (3 * third)
        pieces = [
            fb[j, :, pl.ds((t * owners + owner) * third, third)] for owner in range(owners) for j in range(3)
        ]
        return jnp.concatenate(pieces, axis=1)

    for t in range(ff_tiles):
        tile_copy(t).wait()
    dh[...] = dot(hidden_rows(0), tiles[0])
    for t in range(1, ff_tiles):
        dh[...] += dot(hidden_rows(t), tiles[t])
    for first in range(0, x.shape[0], 128):
        these = pl.ds(first, 128)
        gm[these, :] = (x1[these, :] + (dh[these, :] + small(block, BIAS_PROJ))).astype(bf16)
    store(copies, out_sem, gm, act_out)

    def hidden_backward(g, held, t):
        cols = pl.ds(t * width, width)
        d = (dot(g[...], tiles[t], 1, 1) * held[:, cols].astype(f32)).astype(bf16)
        held[:, cols] = d

    def add_sums(row, second, first):
        sums[row : row + 1, :] += column_sum(second) + column_sum(first)

    def input_gradient(held, weights, first=0):
        for t, weight in enumerate(weights, first):
            term = dot(held[:, t * width : (t + 1) * width], weight(), 1, 1)
            dh[...] = term if t == 0 else dh[...] + term

    def residents(first, number):
        return [functools.partial(resident, first + t) for t in range(number)]

    def streamed(first, number):
        return [functools.partial(tile, first + t) for t in range(number)]

    loads["cot"].wait()
    for t in range(ff_tiles):
        hidden_backward(cot, dub, t)
    input_gradient(dub, residents(fc_at, ff_tiles))
    greet()
    norm_backward(x1, dh, small(block, GAIN2), cot, grad, sums, GAIN2, SHIFT2, dab)
    load("x1", x1_in, x1)
    da[...] = dot(dab[...], resident(3), 1, 1).astype(bf16)
    attention_backward(dzb, some_probs, da, dzb, 0, 3)
    load("fa", fa_in, fa)
    attention_backward(dzb, more_probs, da, dzb, 3, 6, 3)
    input_gradient(dzb, residents(0, 3))
    norm_backward(x, dh, small(block, GAIN1), grad, grad, sums, GAIN1, SHIFT1)

    copies[0].wait()
    gm[...] = grad[...].astype(bf16)

    @pl.when(end)
    def _():
        pl.semaphore_wait(barrier, 4)

    @pl.when(middle)
    def _():
        pl.semaphore_wait(barrier, 5)

    loads["fa"].wait()
    proj_chunk(0)
    proj_chunk(1)
    b(0)
    proj_chunk(2)
    b(1)
    loads["slope"].wait()
    hidden_backward(gm, slope, 0)
    next_tile(0)
    period(0)
    proj_chunk(3)
    load("probs", probs_in, probs)
    add_sums(BIAS_PROJ, cot[...], gm[...])
    hidden_backward(gm, slope, 1)
    next_tile(1)
    period(1)
    for t in range(2, ff_tiles):
        hidden_backward(gm, slope, t)
        next_tile(t)
    n = ff_tiles

    def fc_chunk(t):
        other_chunk(projs + t, h2a, slope, h2b, dub, t * width)
        cols = pl.ds(t * width, width)
        add_sums(BIAS_FC + t, dub[:, cols], slope[:, cols])

    loads["h2a"].wait()
    fc_chunk(0)
    input_gradient(slope, streamed(n, ff_tiles // 2))
    period(2)
    fc_chunk(1)
    input_gradient(slope, streamed(n + ff_tiles // 2, ff_tiles // 2), ff_tiles // 2)
    for t in range(ff_tiles):
        next_tile(n + t)
    n += ff_tiles
    loads["x1"].wait()
    norm_backward(x1, dh, small(block, GAIN2), grad, grad, sums, GAIN2, SHIFT2, da)
    period(3)
    fc_chunk(2)
    do = cot
    do[...] = dot(da[...], tile(n), 1, 1).astype(bf16)
    n += 1
    add_sums(BIAS_OUT, dab[...], da[...])
    loads["qkv"].wait()
    loads["probs"].wait()
    attention_backward(qkv, probs, do, qkv, 0, 1)
    period(4)
    fc_chunk(3)
    attention_backward(qkv, probs, do, qkv, 1, 3)
    period(5)
    loads["oa"].wait()
    other_chunk(8, oa, da, ob, dab, 0)
    attention_backward(qkv, probs, do, qkv, 3, 5)
    period(6)
    attention_backward(qkv, probs, do, qkv, 5, 6)
    loads["h1a"].wait()
    other_chunk(9, h1a, qkv, h1b, dzb, 0)
    add_sums(BIAS_Q, dzb[:, :width], qkv[:, :width])
    period(7)
    other_chunk(10, h1a, qkv, h1b, dzb, width)
    input_gradient(qkv, streamed(n, 3))
    period(8)
    other_chunk(11, h1a, qkv, h1b, dzb, 2 * width)
    add_sums(BIAS_V, dzb[:, 2 * width :], qkv[:, 2 * width :])
    loads["tokens"].wait()
    norm_backward(tokens, dh, small(block, GAIN1), grad, grad, sums, GAIN1, SHIFT1)
    store(copies, out_sem, grad, grad_out)

    def small_copy(step, src, peer):
        return pltpu.make_async_remote_copy(
            src_ref=src, dst_ref=small_in.at[step], send_sem=small_send.at[step], recv_sem=small_recv.at[step],
            device_id=peer, device_id_type=MESH,
        )

    own_peers = (core_peer, x_peer, y_peer)

    def small_next(step):
        small_copy(step, small_tot.at[step], own_peers[step]).wait_recv()
        small_tot[step + 1] = small_tot[step] + small_in[step]
        if step + 1 < 3:
            small_copy(step + 1, small_tot.at[step + 1], own_peers[step + 1]).start()
        else:

            @pl.when(end)
            def _():
                small_copy(3, small_tot.at[3], inward).start()

    def small_middle():
        @pl.when(middle)
        def _():
            small_copy(3, small_tot.at[3], inward).wait_recv()
            small_tot[4] = small_tot[3] + small_in[3]
            small_copy(4, small_tot.at[4], across).start()

    def small_last():
        @pl.when(middle)
        def _():
            small_copy(4, small_tot.at[4], across).wait_recv()
            small_tot[5] = small_tot[4] + small_in[4]
            small_copy(5, small_tot.at[5], outward).start()
            sums_out[...] = small_tot[5]

    small_tot[0] = sums[...]
    small_copy(0, small_tot.at[0], own_peers[0]).start()
    period(9)
    other_chunk(12, h1a, qkv, h1b, dzb, 2 * width + width // 2)
    small_next(0)
    period(10)
    small_next(1)
    period(11)
    small_next(2)
    period(12)
    small_middle()
    period(13)
    small_last()
    for k in range(14, chunks + 5):
        period(k)

    @pl.when(end)
    def _():
        small_copy(5, small_tot.at[5], outward).wait_recv()
        sums_out[...] = small_in[5]

    for i in range(chunks):
        Chunk(i).finish()
    for step in range(3):
        small_copy(step, small_tot.at[step], own_peers[step]).wait_send()

    @pl.when(end)
    def _():
        small_copy(3, small_tot.at[3], inward).wait_send()

    @pl.when(middle)
    def _():
        small_copy(4, small_tot.at[4], across).wait_send()
        small_copy(5, small_tot.at[5], outward).wait_send()

    for copy in copies[1:]:
        copy.wait()


def last_kernel(
    act, tokens_grad, sums, gqkv, gout, gfc, gproj,
    act_out, tokens_grad_out, gqkv_out, gout_out, gfc_out, gproj_out,
    g1, s1, gbq, gbv, gbo, g2, s2, gbp, gbfc,
    lqkv, lout, lfc, lproj, fqkv, fout, ffc, fproj, act_here, grad_here, in_sem, out_sem,
):
    lows = (lqkv, lout, lfc, lproj)
    loads = [
        pltpu.make_async_copy(src, dst, in_sem.at[i]) for i, (src, dst) in enumerate(zip((gqkv, gout, gfc, gproj), lows))
    ]
    passing = [
        pltpu.make_async_copy(act, act_here, in_sem.at[4]), pltpu.make_async_copy(tokens_grad, grad_here, in_sem.at[5])
    ]
    for copy in passing + [loads[i] for i in (3, 2, 0, 1)]:
        copy.start()
    copies = []
    for copy, here, place in zip(passing, (act_here, grad_here), (act_out, tokens_grad_out)):
        copy.wait()
        store(copies, out_sem, here, place)
    wides = ((fqkv, gqkv_out), (fout, gout_out), (ffc, gfc_out), (fproj, gproj_out))
    for i in (3, 2, 0, 1):
        loads[i].wait()
        wide, place = wides[i]
        wide[...] = lows[i][...].astype(f32)
        store(copies, out_sem, wide, place)
    owners = lax.axis_size("own")
    me = lax.axis_index("own")
    size, ff_size = g1.shape[0], gbfc.shape[0]
    across = sums.shape[1] // ff_size
    mine = jnp.zeros((8, size), f32)
    mine_ff = jnp.zeros((1, ff_size), f32)
    for owner in range(owners):
        here = me == owner
        mine = jnp.where(here, sums[:8, owner * size : (owner + 1) * size], mine)
        row, col = BIAS_FC + owner // across, owner % across * ff_size
        mine_ff = jnp.where(here, sums[row : row + 1, col : col + ff_size], mine_ff)
    for row, place in enumerate((g1, s1, gbq, gbv, gbo, g2, s2, gbp)):
        place[...] = mine[row]
    gbfc[...] = mine_ff[0]
    for copy in copies:
        copy.wait()


VMEM_BYTES = 65_200 * 1024


def spec(shape, dtype):
    return jax.ShapeDtypeStruct(shape, dtype)


def kernels_body(*args):
    tokens, doc, cotangent = args[:3]
    gain1, shift1, sqkv, bq, bv, sout, bo, gain2, shift2, sfc, bfc, sproj, bp = args[3:]
    count, width = tokens.shape
    ff = sfc.shape[1]
    rows = [gain1, shift1, bq, bv, bo, gain2, shift2, bp]
    lanes = 128
    stacked = jnp.pad(jnp.stack(rows), ((0, 0), (0, lanes - gain1.shape[0])))
    packed = jnp.concatenate([stacked, bfc.reshape(-1, lanes)])
    packed = jnp.pad(packed, ((0, 16 - packed.shape[0]), (0, 0)))

    hbm = pl.BlockSpec(memory_space=pl.ANY)
    vmem = pl.BlockSpec(memory_space=pltpu.VMEM)
    V = pltpu.VMEM
    half = count // 2
    x_s = ((count, width), f32)
    low_s = ((count, width), bf16)
    qkv_s = ((count, 3 * width), bf16)
    ff_s = ((count, ff), bf16)
    probs_s = ((HEADS // 2, count, count + half), bf16)
    f_s = ((3, count, 8 * (sproj.shape[0] // 3)), bf16)
    mask_s = ((half, count + half), f32)
    block_s = ((16, width), f32)
    w_s = [((width, 3 * width), bf16), ((width, width), bf16), ((width, ff), bf16), ((ff, width), bf16)]
    units = 3 + 1 + ff // width + 3
    dma = pltpu.SemaphoreType.DMA

    def call(kernel, inputs, outs, scratch, in_specs, out_specs, **params):
        return pl.pallas_call(
            kernel,
            out_shape=[spec(*s) for s in outs],
            in_specs=in_specs,
            out_specs=out_specs,
            scratch_shapes=scratch,
            compiler_params=pltpu.CompilerParams(vmem_limit_bytes=VMEM_BYTES, **params),
        )(*inputs)

    w_all = ((4 + 2 * (ff // width), width, width), bf16)
    outs = [x_s, block_s, mask_s, w_all, low_s, qkv_s, probs_s, low_s, x_s, low_s, ff_s, f_s]
    (x2, block, mask, w, h1a, qkva, probsa, oa, x1a, h2a, slopea, fa) = call(
        first_kernel,
        (tokens, doc.reshape(1, count), packed, sqkv, sout, sfc, sproj),
        outs,
        [V(*s) for s in w_s]
        + [V(*s) for s in (block_s, mask_s, low_s, qkv_s, probs_s, low_s, x_s, low_s, ff_s, f_s, x_s)]
        + [V((8, 16, lanes), bf16)]
        + [dma((units, 6)), dma((units, 6)), dma((units, 7)), dma((units, 7)), dma((units,)), dma((7,)), dma((7,))]
        + [dma((len(outs) + 11,))],
        [vmem] * 3 + [hbm] * 4,
        [hbm] * len(outs),
        collective_id=0,
        has_side_effects=True,
    )
    shard = sqkv.shape[0]
    third = sproj.shape[0] // 3
    tiles = 1 + 3 + ff // width

    half_rows = [((3, 2, 2, third // 2, width), bf16), ((tiles, 2, 2, shard // 2, width), bf16)]
    half_rows2 = [((3, 2, third // 2, width), bf16), ((tiles, 2, shard // 2, width), bf16)]
    blocks = [((3, third, width), bf16), ((tiles, shard, width), bf16)]
    outs = [low_s, x_s, block_s, *[(s.shape, bf16) for s in (sqkv, sout, sfc, sproj)]]
    scratch = [x_s, low_s, low_s, x_s, x_s, x_s, ((4, width, width), bf16), low_s, qkv_s, low_s, low_s, ff_s]
    scratch += [low_s, qkv_s, low_s, low_s, ff_s, ((2 * f_s[0][0], *f_s[0][1:]), bf16)]
    scratch += [((HEADS // 4, count, count + half), bf16), low_s, low_s, low_s, block_s]
    scratch += [((2, 2, 2, 2, third, width), bf16), ((2, 2, 2, 2, shard, width), bf16)]
    scratch += [((3, 2, 2, third, width), bf16), ((tiles, 2, 2, shard, width), bf16)]
    scratch += half_rows + half_rows2 + blocks * 2
    scratch += [((6, 16, width), f32), ((6, 16, width), f32)]
    act, tokens_grad, sums, *grads = call(
        second_kernel,
        (
            x2, tokens, cotangent, mask, block, w, w.reshape(-1, 2, 2, 2, shard, width),
            w.reshape(-1, 3, 2, third, width),
            h1a, qkva, probsa, oa, x1a, h2a, slopea, fa,
        ),
        outs,
        [V(*s) for s in scratch]
        + [dma((24,)), dma((4,)), dma((16,)), dma((13, 8)), dma((13, 8)), dma((6,)), dma((6,))],
        [hbm] * 4 + [vmem] + [hbm] * 11,
        [hbm, hbm, vmem] + [hbm] * 4,
        collective_id=1,
        has_side_effects=True,
    )
    shards = [(s.shape, f32) for s in (sqkv, sout, sfc, sproj)]
    vectors = [(gain1.shape, f32)] * 8 + [(bfc.shape, f32)]
    act, tokens_grad, gqkv, gout, gfc, gproj, *small_grads = call(
        last_kernel,
        (act, tokens_grad, sums, *grads),
        [low_s, x_s, *shards, *vectors],
        [V(s.shape, bf16) for s in (sqkv, sout, sfc, sproj)] + [V(*s) for s in shards]
        + [V(*low_s), V(*x_s), dma((6,)), dma((6,))],
        [hbm, hbm, vmem] + [hbm] * 4,
        [hbm] * 6 + [vmem] * 9,
    )
    g1, s1, gbq, gbv, gbo, g2, s2, gbp, gbfc = small_grads
    return act, tokens_grad, g1, s1, gqkv, gbq, gbv, gout, gbo, g2, s2, gfc, gbfc, gproj, gbp


def as_sent(shard):
    return jax.tree.map(lambda a: a.astype(jnp.bfloat16) if a.dtype == jnp.float32 else a, shard)


def normalize(x, gain, shift):
    centre = x - jnp.mean(x, axis=-1, keepdims=True)
    spread = jnp.mean(centre * centre, axis=-1, keepdims=True)
    return centre * lax.rsqrt(spread + EPSILON) * gain + shift


def smooth(inner):
    return jax.nn.gelu(inner, approximate=True)


def visible(doc):
    count = doc.shape[0]
    row = lax.broadcasted_iota(jnp.int32, (count, count), 0)
    col = lax.broadcasted_iota(jnp.int32, (count, count), 1)
    same = doc[:, None] == doc[None, :]
    return same & (col <= row) & ((doc[None, :] != 0) | (row == col))


def plain_forward(x, weights, mask):
    (
        gain_one,
        shift_one,
        w_qkv,
        bias_query,
        bias_value,
        w_out,
        bias_out,
        gain_two,
        shift_two,
        w_fc,
        bias_fc,
        w_proj,
        bias_proj,
    ) = weights
    width = w_qkv.shape[0]
    count = x.shape[0]
    scale = HEAD_DIM ** (-0.5)
    f32 = jnp.float32
    h_one = normalize(x, gain_one.astype(f32), shift_one.astype(f32)).astype(jnp.bfloat16)
    qkv_bias = jnp.concatenate(
        [bias_query.astype(f32), jnp.zeros((width,), f32), bias_value.astype(f32)]
    )
    packed = (jnp.dot(h_one, w_qkv, preferred_element_type=f32) + qkv_bias).astype(jnp.bfloat16)
    query = packed[:, :width].reshape(count, HEADS, HEAD_DIM)
    key = packed[:, width : 2 * width].reshape(count, HEADS, HEAD_DIM)
    value = packed[:, 2 * width :].reshape(count, HEADS, HEAD_DIM)
    scores = jnp.einsum("thd,shd->hts", query, key, preferred_element_type=f32) * scale
    scores = jnp.where(mask[None], scores, -1e30)
    probs = jax.nn.softmax(scores, axis=-1)
    probs_low = probs.astype(jnp.bfloat16)
    mixed = jnp.einsum("hts,shd->thd", probs_low, value, preferred_element_type=f32)
    mixed = mixed.reshape(count, width).astype(jnp.bfloat16)
    middle = x + (jnp.dot(mixed, w_out, preferred_element_type=f32) + bias_out.astype(f32))
    h_two = normalize(middle, gain_two.astype(f32), shift_two.astype(f32)).astype(jnp.bfloat16)
    inner = jnp.dot(h_two, w_fc, preferred_element_type=f32) + bias_fc.astype(f32)
    active = smooth(inner).astype(jnp.bfloat16)
    result = middle + (jnp.dot(active, w_proj, preferred_element_type=f32) + bias_proj.astype(f32))
    kept = (h_one, query, key, value, probs, probs_low, mixed, middle, h_two, inner, active)
    return (result, kept)


def plain_backward(x, weights, mask, grad):
    (
        gain_one,
        shift_one,
        w_qkv,
        bias_query,
        bias_value,
        w_out,
        bias_out,
        gain_two,
        shift_two,
        w_fc,
        bias_fc,
        w_proj,
        bias_proj,
    ) = weights
    result, kept = plain_forward(x, weights, mask)
    h_one, query, key, value, probs, probs_low, mixed, middle, h_two, inner, active = kept
    width = w_qkv.shape[0]
    count = x.shape[0]
    scale = HEAD_DIM ** (-0.5)
    f32 = jnp.float32
    grad_branch = grad.astype(jnp.bfloat16)
    g_wproj = jnp.einsum("tf,td->fd", active, grad_branch, preferred_element_type=f32)
    g_bproj = jnp.sum(grad_branch.astype(f32), axis=0)
    d_active = jnp.einsum("td,fd->tf", grad_branch, w_proj, preferred_element_type=f32)
    unused, pull_smooth = jax.vjp(smooth, inner)
    d_inner = pull_smooth(d_active)[0].astype(jnp.bfloat16)
    g_wfc = jnp.einsum("td,tf->df", h_two, d_inner, preferred_element_type=f32)
    g_bfc = jnp.sum(d_inner.astype(f32), axis=0)
    d_htwo = jnp.einsum("tf,df->td", d_inner, w_fc, preferred_element_type=f32)
    unused, pull_two = jax.vjp(normalize, middle, gain_two.astype(f32), shift_two.astype(f32))
    d_mid, g_gain2, g_shift2 = pull_two(d_htwo)
    d_middle = grad + d_mid
    d_attn = d_middle.astype(jnp.bfloat16)
    g_wout = jnp.einsum("td,te->de", mixed, d_attn, preferred_element_type=f32)
    g_bout = jnp.sum(d_attn.astype(f32), axis=0)
    d_mixed = jnp.einsum("te,de->td", d_attn, w_out, preferred_element_type=f32).astype(
        jnp.bfloat16
    )
    d_mixed = d_mixed.reshape(count, HEADS, HEAD_DIM)
    d_probs = jnp.einsum("thd,shd->hts", d_mixed, value, preferred_element_type=f32)
    d_value = jnp.einsum("hts,thd->shd", probs_low, d_mixed, preferred_element_type=f32)
    d_scores = probs * (d_probs - jnp.sum(d_probs * probs, axis=-1, keepdims=True))
    d_scores = d_scores.astype(jnp.bfloat16)
    d_query = jnp.einsum("hts,shd->thd", d_scores, key, preferred_element_type=f32) * scale
    d_key = jnp.einsum("hts,thd->shd", d_scores, query, preferred_element_type=f32) * scale
    d_packed = jnp.concatenate(
        [d_query.reshape(count, width), d_key.reshape(count, width), d_value.reshape(count, width)],
        axis=1,
    ).astype(jnp.bfloat16)
    g_wqkv = jnp.einsum("td,te->de", h_one, d_packed, preferred_element_type=f32)
    column_sums = jnp.sum(d_packed.astype(f32), axis=0)
    g_bquery = column_sums[:width]
    g_bvalue = column_sums[2 * width :]
    d_hone = jnp.einsum("te,de->td", d_packed, w_qkv, preferred_element_type=f32)
    unused, pull_one = jax.vjp(normalize, x, gain_one.astype(f32), shift_one.astype(f32))
    d_input, g_gain1, g_shift1 = pull_one(d_hone)
    terms = (
        g_gain1,
        g_shift1,
        g_wqkv,
        g_bquery,
        g_bvalue,
        g_wout,
        g_bout,
        g_gain2,
        g_shift2,
        g_wfc,
        g_bfc,
        g_wproj,
        g_bproj,
    )
    return (d_middle + d_input, terms)


def plain_body(
    tokens,
    doc_ids,
    cotangent,
    norm1_gain,
    norm1_shift,
    qkv_weight,
    query_bias,
    value_bias,
    out_weight,
    out_bias,
    norm2_gain,
    norm2_shift,
    fc_weight,
    fc_bias,
    proj_weight,
    proj_bias,
):
    shards = (
        norm1_gain,
        norm1_shift,
        qkv_weight,
        query_bias,
        value_bias,
        out_weight,
        out_bias,
        norm2_gain,
        norm2_shift,
        fc_weight,
        fc_bias,
        proj_weight,
        proj_bias,
    )
    mask = visible(doc_ids)

    def fetch():
        return (
            lax.all_gather(shards[0], "own", axis=0, tiled=True),
            lax.all_gather(shards[1], "own", axis=0, tiled=True),
            lax.all_gather(shards[2], "own", axis=0, tiled=True),
            lax.all_gather(shards[3], "own", axis=0, tiled=True),
            lax.all_gather(shards[4], "own", axis=0, tiled=True),
            lax.all_gather(shards[5], "own", axis=0, tiled=True),
            lax.all_gather(shards[6], "own", axis=0, tiled=True),
            lax.all_gather(shards[7], "own", axis=0, tiled=True),
            lax.all_gather(shards[8], "own", axis=0, tiled=True),
            lax.all_gather(shards[9], "own", axis=0, tiled=True),
            lax.all_gather(shards[10], "own", axis=0, tiled=True),
            lax.all_gather(shards[11], "own", axis=0, tiled=True),
            lax.all_gather(shards[12], "own", axis=0, tiled=True),
        )

    current = tokens.astype(jnp.float32)
    saved = []
    for use in range(USES):
        saved.append(current)
        current, kept = plain_forward(current, fetch(), mask)
    grad = cotangent.astype(jnp.float32)
    summed = None
    for use in reversed(range(USES)):
        grad, terms = plain_backward(saved[use], fetch(), mask, grad)
        if summed is None:
            summed = terms
        else:
            summed = tuple((first + second for first, second in zip(summed, terms)))
    owned = (
        lax.psum_scatter(summed[0], "own", scatter_dimension=0, tiled=True),
        lax.psum_scatter(summed[1], "own", scatter_dimension=0, tiled=True),
        lax.psum_scatter(summed[2], "own", scatter_dimension=0, tiled=True),
        lax.psum_scatter(summed[3], "own", scatter_dimension=0, tiled=True),
        lax.psum_scatter(summed[4], "own", scatter_dimension=0, tiled=True),
        lax.psum_scatter(summed[5], "own", scatter_dimension=0, tiled=True),
        lax.psum_scatter(summed[6], "own", scatter_dimension=0, tiled=True),
        lax.psum_scatter(summed[7], "own", scatter_dimension=0, tiled=True),
        lax.psum_scatter(summed[8], "own", scatter_dimension=0, tiled=True),
        lax.psum_scatter(summed[9], "own", scatter_dimension=0, tiled=True),
        lax.psum_scatter(summed[10], "own", scatter_dimension=0, tiled=True),
        lax.psum_scatter(summed[11], "own", scatter_dimension=0, tiled=True),
        lax.psum_scatter(summed[12], "own", scatter_dimension=0, tiled=True),
    )
    final = jax.tree.map(lambda part: part.astype(jnp.float32), lax.psum(as_sent(owned), "grp"))
    return (current.astype(jnp.bfloat16), grad) + tuple(final)


def solution(mesh):
    return jax.shard_map(
        kernels_body if tuple(mesh.axis_sizes) == (4, 8) else plain_body,
        mesh=mesh,
        in_specs=(
            P(("grp", "own"), None),
            P(("grp", "own")),
            P(("grp", "own"), None),
            P("own"),
            P("own"),
            P("own", None),
            P("own"),
            P("own"),
            P("own", None),
            P("own"),
            P("own"),
            P("own"),
            P("own", None),
            P("own"),
            P("own", None),
            P("own"),
        ),
        out_specs=(
            P(("grp", "own"), None),
            P(("grp", "own"), None),
            P("own"),
            P("own"),
            P("own", None),
            P("own"),
            P("own"),
            P("own", None),
            P("own"),
            P("own"),
            P("own"),
            P("own", None),
            P("own"),
            P("own", None),
            P("own"),
        ),
        check_vma=False,
    )
```
